32 devices in a mesh: seq: 4 (over y, x), dp: 8 (over z, core).
Axes of the slice: x: 2, y: 2, z: 4, core: 2. Of those that a mesh axis runs over, the one named last changes fastest.
Arguments:
- tokens: bfloat16 [8, 1024, 2048], P('dp', 'seq'), may hold values from -6 to 6
- cotangent: bfloat16 [8, 1024, 2048], P('dp', 'seq'), may hold values from -6 to 6
- first_gain: bfloat16 [2048], P(('seq', 'dp')), may hold values from 0.5 to 1.5
- first_shift: bfloat16 [2048], P(('seq', 'dp')), may hold values from -1.25 to 1.25
- second_gain: bfloat16 [2048], P(('seq', 'dp')), may hold values from 0.5 to 1.5
- second_shift: bfloat16 [2048], P(('seq', 'dp')), may hold values from -1.25 to 1.25
- joint_weight: bfloat16 [2048, 6144], P(('seq', 'dp')), may hold values from -0.125 to 0.125
- joint_bias: bfloat16 [6144], P(('seq', 'dp')), may hold values from -1.25 to 1.25
- dense_weight: bfloat16 [2048, 2048], P(('seq', 'dp')), may hold values from -1 to 1
- dense_bias: bfloat16 [2048], P(('seq', 'dp')), may hold values from -1.25 to 1.25
- expand_weight: bfloat16 [2048, 8192], P(('seq', 'dp')), may hold values from -0.125 to 0.125
- expand_bias: bfloat16 [8192], P(('seq', 'dp')), may hold values from -1.25 to 1.25
- shrink_weight: bfloat16 [8192, 2048], P(('seq', 'dp')), may hold values from -0.0625 to 0.0625
- shrink_bias: bfloat16 [2048], P(('seq', 'dp')), may hold values from -1.25 to 1.25
Outputs:
- output: bfloat16 [8, 1024, 2048], P('dp', 'seq')
- grad_tokens: float32 [8, 1024, 2048], P('dp', 'seq')
- grad_first_gain: float32 [2048], P(('seq', 'dp'))
- grad_first_shift: float32 [2048], P(('seq', 'dp'))
- grad_second_gain: float32 [2048], P(('seq', 'dp'))
- grad_second_shift: float32 [2048], P(('seq', 'dp'))
- grad_joint_weight: float32 [2048, 6144], P(('seq', 'dp'))
- grad_joint_bias: float32 [6144], P(('seq', 'dp'))
- grad_dense_weight: float32 [2048, 2048], P(('seq', 'dp'))
- grad_dense_bias: float32 [2048], P(('seq', 'dp'))
- grad_expand_weight: float32 [2048, 8192], P(('seq', 'dp'))
- grad_expand_bias: float32 [8192], P(('seq', 'dp'))
- grad_shrink_weight: float32 [8192, 2048], P(('seq', 'dp'))
- grad_shrink_bias: float32 [2048], P(('seq', 'dp'))
The draws below stay inside these ranges and needn't reach their ends.
All inputs are finite; a program needn't handle non-finite values.
Results may differ from the reference program's by a relative error of at most 0.0089.
Values may be sent and summed in bfloat16 or wider, within the bound.
A program may use at most 384 MiB of HBM per device.

```python
import jax
import jax.numpy as jnp
from jax import lax

D = 2048
HEADS = 8
ROT = 64
FF = 8192
LENGTH = 1024
SEQS = 8


def shard_levels(own_key, shape, pieces, smallest, top_value):
    loudness = 1.0
    for dim, blocks in pieces:
        steps = jax.random.uniform(jax.random.fold_in(jax.random.fold_in(own_key, 6), dim), (blocks,), jnp.float32, smallest / len(pieces), top_value / len(pieces))
        loudness = loudness * jnp.repeat(jnp.exp(steps), shape[dim] // blocks).reshape((-1,) + (1,) * (len(shape) - 1 - dim))
    return loudness


def centred(key, dims, scale, reach, split=(), kind=jnp.bfloat16):
    level = shard_levels(key, dims, split, -0.22, 0.18) if split else 1.0
    entries = jax.random.normal(key, dims, jnp.float32) * scale * level
    return jnp.minimum(jnp.maximum(entries, -reach), reach).astype(kind)


def setup_inputs(seed: int = 0) -> dict:
    key_of = jax.random.split(jax.random.key(seed), 15)
    return {
        "tokens": centred(key_of[0], (SEQS, LENGTH, D), 1.0, 6.0, ((0, 8), (1, 4))),
        "cotangent": centred(key_of[1], (SEQS, LENGTH, D), 1.0, 6.0, ((0, 8), (1, 4))),
        "first_gain": jnp.clip(1.0 + 0.1 * jax.random.normal(key_of[2], (D,), jnp.float32), 0.5, 1.5).astype(jnp.bfloat16),
        "first_shift": centred(key_of[3], (D,), 0.2, 1.25, ((0, 32),)),
        "second_gain": jnp.clip(1.0 + 0.1 * jax.random.normal(key_of[4], (D,), jnp.float32), 0.5, 1.5).astype(jnp.bfloat16),
        "second_shift": centred(key_of[5], (D,), 0.2, 1.25, ((0, 32),)),
        "joint_weight": centred(key_of[6], (D, 3 * D), D ** -0.5, 0.125, ((0, 32),)),
        "joint_bias": centred(key_of[7], (3 * D,), 0.2, 1.25, ((0, 32),)),
        "dense_weight": centred(key_of[8], (D, D), (D // 64) ** -0.5, 1.0, ((0, 32),)),
        "dense_bias": centred(key_of[9], (D,), 0.2, 1.25, ((0, 32),)),
        "expand_weight": centred(key_of[10], (D, FF), D ** -0.5, 0.125, ((0, 32),)),
        "expand_bias": centred(key_of[11], (FF,), 0.2, 1.25, ((0, 32),)),
        "shrink_weight": centred(key_of[12], (FF, D), FF ** -0.5, 0.0625, ((0, 32),)),
        "shrink_bias": centred(key_of[13], (D,), 0.2, 1.25, ((0, 32),)),
    }


@jax.custom_vjp
def low(v):
    return lax.optimization_barrier(v.astype(jnp.bfloat16)).astype(jnp.float32)

@jax.custom_vjp
def low_back(v):
    return v

def low_keep(v):
    return (low(v), None)

def low_pass(kept, grad):
    return (grad,)

def back_keep(v):
    return (v, None)

def back_low(kept, grad):
    return (low(grad),)
low.defvjp(low_keep, low_pass)
low_back.defvjp(back_keep, back_low)

def layer_norm(values, gain, shift):
    center = values - lax.optimization_barrier(jnp.mean(values, axis=-1, keepdims=True))
    spread = lax.optimization_barrier(jnp.mean(center * center, axis=-1, keepdims=True))
    return center * lax.rsqrt(spread + 1e-05) * gain + shift

def matmul(left, right):
    return jnp.dot(left, right, precision=lax.Precision.HIGHEST, preferred_element_type=jnp.float32)

def rotate(field, cosine, sine):
    half = ROT // 2
    part = field[..., :ROT]
    turned = jnp.concatenate([-part[..., half:], part[..., :half]], axis=-1)
    return jnp.concatenate([part * cosine + turned * sine, field[..., ROT:]], axis=-1)

def layer(hidden, params):
    gain_one, shift_one, gain_two, shift_two, joint_full, joint_offset, dense_full, dense_offset, expand_full, expand_offset, shrink_full, shrink_offset = params
    length = hidden.shape[0]
    width = hidden.shape[1]
    head_size = width // HEADS
    normed_one = low(layer_norm(hidden, gain_one, shift_one))
    normed_two = low(layer_norm(hidden, gain_two, shift_two))
    joint = low_back(matmul(normed_one, joint_full) + joint_offset)
    query = joint[:, :width].reshape(length, HEADS, head_size)
    keyed = joint[:, width:2 * width].reshape(length, HEADS, head_size)
    valued = joint[:, 2 * width:].reshape(length, HEADS, head_size)
    places = jnp.arange(length, dtype=jnp.float32)
    inverse = 10000.0 ** (-jnp.arange(0, ROT, 2, dtype=jnp.float32) / ROT)
    angle = places[:, None] * inverse[None, :]
    angle = jnp.concatenate([angle, angle], axis=-1)[:, None, :]
    cosine = jnp.cos(angle)
    sine = jnp.sin(angle)
    query = low(rotate(query, cosine, sine))
    keyed = low(rotate(keyed, cosine, sine))
    valued = low(valued)
    scale = head_size ** (-0.5)
    scores = low_back(jnp.einsum('qhd,khd->hqk', query, keyed, precision=lax.Precision.HIGHEST) * scale)
    rows = jnp.arange(length, dtype=jnp.int32)
    visible = rows[None, :] <= rows[:, None]
    scores = jnp.where(visible[None], scores, -1e+30)
    peak = lax.optimization_barrier(jnp.max(scores, axis=-1, keepdims=True))
    expo = jnp.exp(scores - peak)
    probs = low(expo / lax.optimization_barrier(jnp.sum(expo, axis=-1, keepdims=True)))
    mixed = jnp.einsum('hqk,khd->qhd', probs, valued, precision=lax.Precision.HIGHEST).reshape(length, width)
    mixed = low(low_back(mixed))
    attend = matmul(mixed, dense_full) + dense_offset
    pre = low_back(matmul(normed_two, expand_full) + expand_offset)
    act = low(jax.nn.gelu(pre, approximate=False))
    feed = matmul(act, shrink_full) + shrink_offset
    return hidden + attend + feed

def reference(tokens, cotangent, first_gain, first_shift, second_gain, second_shift, joint_weight, joint_bias, dense_weight, dense_bias, expand_weight, expand_bias, shrink_weight, shrink_bias):
    params = tuple((p.astype(jnp.float32) for p in (first_gain, first_shift, second_gain, second_shift, joint_weight, joint_bias, dense_weight, dense_bias, expand_weight, expand_bias, shrink_weight, shrink_bias)))

    def one(totals, pair):
        seq_tokens, seq_grad = pair
        result, pull = jax.vjp(layer, seq_tokens.astype(jnp.float32), params)
        grad_hidden, grad_params = pull(seq_grad.astype(jnp.float32))
        totals = tuple((a + b for a, b in zip(totals, grad_params)))
        return (totals, (result.astype(jnp.bfloat16), grad_hidden))
    start = tuple((jnp.zeros(p.shape, jnp.float32) for p in params))
    totals, (outputs, grads_hidden) = lax.scan(one, start, (tokens, cotangent))
    return (outputs, grads_hidden, totals[0], totals[1], totals[2], totals[3], totals[4], totals[5], totals[6], totals[7], totals[8], totals[9], totals[10], totals[11])
```

```python
import jax
import jax.numpy as jnp
from jax import lax
from jax.sharding import PartitionSpec as P

HEADS = 8
ROT = 64
CORES = 2
BF = jnp.bfloat16
F32 = jnp.float32


def mm(left, right):
    return jnp.dot(left, right, preferred_element_type=F32)


def mm_first(left, right):
    return lax.dot_general(left, right, (((0,), (0,)), ((), ())), preferred_element_type=F32)


def mm_last(left, right):
    return lax.dot_general(left, right, (((1,), (1,)), ((), ())), preferred_element_type=F32)


def rotate(field, cosine, sine):
    half = ROT // 2
    part = field[..., :ROT]
    turned = jnp.concatenate([-part[..., half:], part[..., :half]], axis=-1)
    return jnp.concatenate([part * cosine + turned * sine, field[..., ROT:]], axis=-1)


def rotate_back(grad, cosine, sine):
    half = ROT // 2
    part = grad[..., :ROT]
    scaled = part * sine
    back = jnp.concatenate([scaled[..., half:], -scaled[..., :half]], axis=-1)
    return jnp.concatenate([part * cosine + back, grad[..., ROT:]], axis=-1)


def turn_tables(length):
    inverse = 10000.0 ** (-jnp.arange(0, ROT, 2, dtype=F32) / ROT)
    angle = jnp.arange(length, dtype=F32)[:, None] * inverse[None, :]
    angle = jnp.concatenate([angle, angle], axis=-1)[:, None, :]
    return jnp.cos(angle), jnp.sin(angle)


class Ring:
    def __init__(self, n, m):
        self.n, self.m, self.line = n, m, m // CORES
        self.s = lax.axis_index("seq")
        self.d = lax.axis_index("dp")
        self.z, self.c = self.d // CORES, self.d % CORES
        self.up = [(i, i + CORES) for i in range(m - CORES)]
        self.down = [(i + CORES, i) for i in range(m - CORES)]
        self.swap = [(i, i ^ 1) for i in range(m)]

    def pick(self, stack, index):
        return lax.dynamic_index_in_dim(stack, index, 0, keepdims=False)

    def partner(self, k):
        return [(i, i ^ k) for i in range(self.n)]

    def order(self, slots):
        stack = jnp.stack(slots)
        return jnp.stack([self.pick(stack, self.s ^ j) for j in range(self.n)])

    def gather_seq(self, block):
        slots = [block] + [lax.ppermute(block, "seq", self.partner(k)) for k in range(1, self.n)]
        return self.order(slots)

    def exchange_seq(self, blocks):
        slots = [self.pick(blocks, self.s)]
        for k in range(1, self.n):
            slots.append(lax.ppermute(self.pick(blocks, self.s ^ k), "seq", self.partner(k)))
        return slots

    def scatter_seq(self, blocks):
        slots = self.exchange_seq(blocks)
        total = slots[0].astype(F32)
        for other in slots[1:]:
            total = total + other.astype(F32)
        return total

    def gather_dp(self, block):
        ups, downs = [block], [block]
        for _ in range(self.line - 1):
            ups.append(lax.ppermute(ups[-1], "dp", self.up))
            downs.append(lax.ppermute(downs[-1], "dp", self.down))
        span = jnp.stack(ups[::-1] + downs[1:])
        mine = lax.dynamic_slice_in_dim(span, self.line - 1 - self.z, self.line, 0)
        other = lax.ppermute(mine, "dp", self.swap)
        first = self.c == 0
        both = jnp.stack(
            [jnp.where(first, mine, other), jnp.where(first, other, mine)], axis=1
        )
        return both.reshape((self.m,) + block.shape)

    def scatter_dp(self, blocks):
        parts = blocks.reshape((self.line, CORES) + blocks.shape[1:])
        parts = jnp.swapaxes(parts, 0, 1)
        sent = lax.ppermute(self.pick(parts, 1 - self.c), "dp", self.swap)
        held = (self.pick(parts, self.c).astype(F32) + sent.astype(F32)).astype(BF)
        reach = self.line - 1
        rising, falling = None, None
        for i in range(1, self.line):
            first = self.pick(held, jnp.minimum(self.z + self.line - i, reach))
            second = self.pick(held, jnp.maximum(self.z - self.line + i, 0))
            if rising is not None:
                first = (first.astype(F32) + rising.astype(F32)).astype(BF)
                second = (second.astype(F32) + falling.astype(F32)).astype(BF)
            rising = lax.ppermute(first, "dp", self.up)
            falling = lax.ppermute(second, "dp", self.down)
        return self.pick(held, self.z).astype(F32) + rising.astype(F32) + falling.astype(F32)


def block_plan(n, m, tokens, cotangent, shards):
    (
        first_gain,
        first_shift,
        second_gain,
        second_shift,
        joint_weight,
        joint_bias,
        dense_weight,
        dense_bias,
        expand_weight,
        expand_bias,
        shrink_weight,
        shrink_bias,
    ) = shards
    ring = Ring(n, m)
    devices = n * m
    own, upstream = tokens[0], cotangent[0]
    rows, width = own.shape
    length = rows * n
    piece = width // devices
    head_size = width // HEADS
    heads = HEADS // n
    part = width // n
    hidden_part = expand_weight.shape[1] // n

    def shuffle(values):
        shape = values.shape[:-1]
        values = values.reshape(shape + (n, m, piece))
        return jnp.swapaxes(values, -3, -2).reshape(shape + (width,))

    def unshuffle(values):
        shape = values.shape[:-1]
        values = values.reshape(shape + (m, n, piece))
        return jnp.swapaxes(values, -3, -2).reshape(shape + (width,))

    vectors = (
        first_gain,
        first_shift,
        second_gain,
        second_shift,
        joint_bias,
        dense_bias,
        expand_bias,
        shrink_bias,
    )
    packed = lax.all_gather(jnp.concatenate(vectors)[None], ("seq", "dp"), axis=0, tiled=True)
    full, start = [], 0
    for vector in vectors:
        full.append(packed[:, start : start + vector.shape[0]].reshape(-1).astype(F32))
        start += vector.shape[0]
    gain_one, shift_one, gain_two, shift_two = [shuffle(v) for v in full[:4]]
    joint_offset, dense_offset, expand_offset, shrink_offset = full[4:]
    joint_offset = ring.pick(jnp.swapaxes(joint_offset.reshape(3, n, part), 0, 1), ring.s)
    joint_offset = joint_offset.reshape(3 * part)
    expand_offset = ring.pick(expand_offset.reshape(n, hidden_part), ring.s)

    all_tokens = ring.gather_seq(shuffle(own)).reshape(length, width)
    joint_blocks = jnp.transpose(joint_weight.reshape(piece, 3, n, part), (2, 0, 1, 3))
    joint_mine = ring.order(ring.exchange_seq(joint_blocks.reshape(n, piece, 3 * part)))
    expand_blocks = jnp.swapaxes(expand_weight.reshape(piece, n, hidden_part), 0, 1)
    expand_mine = ring.order(ring.exchange_seq(expand_blocks))
    all_upstream = ring.gather_seq(upstream).reshape(length, width)
    dense_full = ring.gather_dp(dense_weight).reshape(part, width)
    joint_full = ring.gather_dp(joint_mine).reshape(width, 3 * part)
    expand_full = ring.gather_dp(expand_mine).reshape(width, hidden_part)
    shrink_full = ring.gather_dp(shrink_weight).reshape(hidden_part, width)

    values = all_tokens.astype(F32)
    center = values - jnp.mean(values, axis=-1, keepdims=True)
    spread = lax.rsqrt(jnp.mean(center * center, axis=-1, keepdims=True) + 1e-05)
    normal = center * spread
    normed_one = (normal * gain_one + shift_one).astype(BF)
    normed_two = (normal * gain_two + shift_two).astype(BF)

    joint = mm(normed_one, joint_full) + joint_offset
    query, keyed, valued = [
        joint[:, i * part : (i + 1) * part].reshape(length, heads, head_size) for i in range(3)
    ]
    cosine, sine = turn_tables(length)
    query = rotate(query, cosine, sine).astype(BF)
    keyed = rotate(keyed, cosine, sine).astype(BF)
    valued = valued.astype(BF)
    scale = head_size ** (-0.5)
    places = jnp.arange(length, dtype=jnp.int32)
    visible = places[None, :] <= places[:, None]
    scores = jnp.einsum("qhd,khd->hqk", query, keyed, preferred_element_type=F32) * scale
    scores = jnp.where(visible[None], scores, -1e30)
    peak = jnp.max(scores, axis=-1, keepdims=True)
    expo = jnp.exp(scores - peak)
    probs = expo / jnp.sum(expo, axis=-1, keepdims=True)
    probs_low = probs.astype(BF)
    mixed = jnp.einsum("hqk,khd->qhd", probs_low, valued, preferred_element_type=F32)
    mixed = mixed.reshape(length, part).astype(BF)

    grad_dense = mm_first(mixed, all_upstream).astype(BF)
    grad_mixed = mm_last(all_upstream, dense_full).astype(BF).reshape(length, heads, head_size)
    grad_valued = jnp.einsum("hqk,qhd->khd", probs_low, grad_mixed, preferred_element_type=F32)
    grad_probs = jnp.einsum("qhd,khd->hqk", grad_mixed, valued, preferred_element_type=F32)
    inner = jnp.sum(probs * grad_probs, axis=-1, keepdims=True)
    grad_scores = (probs * (grad_probs - inner)).astype(BF)
    grad_query = jnp.einsum("hqk,khd->qhd", grad_scores, keyed, preferred_element_type=F32) * scale
    grad_keyed = jnp.einsum("hqk,qhd->khd", grad_scores, query, preferred_element_type=F32) * scale
    grad_joint = jnp.concatenate(
        [
            rotate_back(grad_query, cosine, sine).reshape(length, part),
            rotate_back(grad_keyed, cosine, sine).reshape(length, part),
            grad_valued.reshape(length, part),
        ],
        axis=1,
    ).astype(BF)
    grad_joint_weight = mm_first(normed_one, grad_joint).astype(BF)
    grad_joint_offset = jnp.sum(grad_joint.astype(F32), axis=0)
    grad_normed_one = mm_last(grad_joint, joint_full)

    pre = mm(normed_two, expand_full) + expand_offset
    act, pull_gelu = jax.vjp(lambda v: jax.nn.gelu(v, approximate=False), pre)
    act = act.astype(BF)
    grad_shrink = mm_first(act, all_upstream).astype(BF)
    grad_pre = pull_gelu(mm_last(all_upstream, shrink_full))[0].astype(BF)
    grad_expand = mm_first(normed_two, grad_pre).astype(BF)
    grad_expand_offset = jnp.sum(grad_pre.astype(F32), axis=0)
    grad_normed_two = mm_last(grad_pre, expand_full)

    partial = (mm(mixed, dense_full) + mm(act, shrink_full)).astype(BF)
    summed = ring.scatter_seq(partial.reshape(n, rows, width))
    own_wide = own.astype(F32)
    output = (own_wide + (summed + (dense_offset + shrink_offset))).astype(BF)[None]

    grad_normal = (grad_normed_one * gain_one + grad_normed_two * gain_two).astype(BF)
    grad_normal = unshuffle(ring.scatter_seq(grad_normal.reshape(n, rows, width)))
    own_center = own_wide - jnp.mean(own_wide, axis=-1, keepdims=True)
    own_spread = lax.rsqrt(jnp.mean(own_center * own_center, axis=-1, keepdims=True) + 1e-05)
    own_normal = own_center * own_spread
    through = grad_normal - jnp.mean(grad_normal, axis=-1, keepdims=True)
    through = through - own_normal * jnp.mean(grad_normal * own_normal, axis=-1, keepdims=True)
    upstream_wide = upstream.astype(F32)
    grad_tokens = (upstream_wide + own_spread * through)[None]

    def placed(vector, groups):
        blocks = vector.reshape(groups, 1, -1)
        mine = (jnp.arange(n) == ring.s).reshape(1, n, 1)
        return jnp.where(mine, blocks, 0.0).reshape(-1)

    sums = (
        unshuffle(jnp.sum(grad_normed_one * normal, axis=0)),
        unshuffle(jnp.sum(grad_normed_one, axis=0)),
        unshuffle(jnp.sum(grad_normed_two * normal, axis=0)),
        unshuffle(jnp.sum(grad_normed_two, axis=0)),
        placed(grad_joint_offset, 3),
        placed(grad_expand_offset, 1),
        jnp.sum(upstream_wide, axis=0),
    )
    sums = jnp.concatenate([v.reshape(devices, -1) for v in sums], axis=1)
    sums = lax.psum_scatter(sums, ("seq", "dp"), scatter_dimension=0, tiled=True)[0]
    small, start = [], 0
    for length_of in (piece, piece, piece, piece, joint_bias.shape[0], expand_bias.shape[0], piece):
        small.append(sums[start : start + length_of])
        start += length_of

    def by_rows(grad):
        return ring.scatter_dp(grad.reshape((m, -1) + grad.shape[1:]))

    dense_grad = by_rows(grad_dense)
    joint_grad = by_rows(grad_joint_weight).astype(BF).reshape(n, piece, 3, part)
    shrink_grad = by_rows(grad_shrink)
    expand_grad = by_rows(grad_expand).astype(BF).reshape(n, piece, hidden_part)
    joint_grad = ring.order(ring.exchange_seq(joint_grad))
    joint_grad = jnp.transpose(joint_grad, (1, 2, 0, 3)).reshape(piece, 3 * width).astype(F32)
    expand_grad = ring.order(ring.exchange_seq(expand_grad))
    expand_grad = jnp.swapaxes(expand_grad, 0, 1).reshape(piece, n * hidden_part).astype(F32)
    return (
        output,
        grad_tokens,
        small[0],
        small[1],
        small[2],
        small[3],
        joint_grad,
        small[4],
        dense_grad,
        small[6],
        expand_grad,
        small[5],
        shrink_grad,
        small[6],
    )


def solution(mesh):
    n, m = mesh.shape["seq"], mesh.shape["dp"]

    def body(tokens, cotangent, *shards):
        return block_plan(n, m, tokens, cotangent, shards)

    both = ("seq", "dp")
    tokens = P("dp", "seq", None)
    vector, matrix = P(both), P(both, None)
    return jax.shard_map(
        body,
        mesh=mesh,
        in_specs=(tokens, tokens) + (vector,) * 4 + (matrix, vector) * 4,
        out_specs=(tokens, tokens) + (vector,) * 4 + (matrix, vector) * 4,
        check_vma=False,
    )
```

```python
import functools

import jax
import jax.numpy as jnp
from jax import lax
from jax.experimental import pallas as pl
from jax.experimental.pallas import tpu as pltpu
from jax.sharding import PartitionSpec as P

HEADS = 8
ROT = 64
CORES = 2
LANES = 128
BF = jnp.bfloat16
F32 = jnp.float32
MESH = pl.DeviceIdType.MESH


def nn(left, right):
    return jnp.dot(left, right, preferred_element_type=F32)


def nt(left, right):
    return lax.dot_general(left, right, (((1,), (1,)), ((), ())), preferred_element_type=F32)


def tn(left, right):
    return lax.dot_general(left, right, (((0,), (0,)), ((), ())), preferred_element_type=F32)


def turn_tables(length):
    inverse = 10000.0 ** (-jnp.arange(0, ROT, 2, dtype=F32) / ROT)
    angle = jnp.arange(length, dtype=F32)[:, None] * inverse[None, :]
    cosine, sine = jnp.cos(angle), jnp.sin(angle)
    rest = jnp.zeros((length, LANES - ROT), F32)
    return jnp.stack(
        [
            jnp.concatenate([cosine, cosine, rest + 1.0], axis=1),
            jnp.concatenate([sine, sine, rest], axis=1),
        ]
    )


def kernel(n, m, dims, names, *refs):
    ref = dict(zip(names, refs))
    rows, width, piece, part, hidden, heads, head_size = dims
    line = m // CORES
    hops = line - 1
    length = rows * n
    scale = head_size ** (-0.5)
    s, d = lax.axis_index("seq"), lax.axis_index("dp")
    z, c = d // CORES, d % CORES
    other = z * CORES + 1 - c
    drains = []

    def remote(src, dst, send, recv, device):
        return pltpu.make_async_remote_copy(
            src_ref=src, dst_ref=dst, send_sem=send, recv_sem=recv, device_id=device, device_id_type=MESH
        )

    def push(src, dst, send, recv, device, when=None):
        copy = remote(src, dst, send, recv, device)
        if when is None:
            copy.start()
        else:
            pl.when(when)(copy.start)
        drains.append((copy, when))

    def arrived(dst, recv):
        remote(dst, dst, recv, recv, {"dp": other}).wait_recv()

    def local(src, dst, sem):
        copy = pltpu.make_async_copy(src, dst, sem)
        copy.start()
        return copy

    def block(buffer, index, size, offset=0, count=None):
        count = size if count is None else count
        return buffer.at[pl.ds(pl.multiple_of(index * size + offset, count), count)]

    barrier = pltpu.get_barrier_semaphore()

    def greet(device):
        pl.semaphore_signal(barrier, inc=1, device_id=device, device_id_type=MESH)

    for k in range(1, n):
        greet({"seq": (s + k) % n})
    greet({"dp": other})
    pl.when(z > 0)(lambda: greet({"dp": d - CORES}))
    pl.when(z < line - 1)(lambda: greet({"dp": d + CORES}))
    pl.semaphore_wait(barrier, n + (z + line - 1) // line + 1 - (z + 1) // line)

    seq_send, seq_recv = ref["seq_send"], ref["seq_recv"]

    def seq_push(item, src, dst):
        for k in range(1, n):
            j = (s + k) % n
            push(src(j), dst, seq_send.at[item, k], seq_recv.at[item, k], {"seq": j})

    def seq_wait(item, dst):
        for k in range(1, n):
            arrived(dst((s - k + n) % n), seq_recv.at[item, k])

    square = n == 4
    beside, across = s + 1 - 2 * (s % 2), (s + 2) % n
    corner = n - 1 - s

    def halves(item, buffer, owner, half):
        return block(buffer, owner, rows, half * (rows // 2), rows // 2)

    def spread_first(item, buffer):
        mine = block(buffer, s, rows)
        if not square:
            seq_push(item, lambda j: mine, mine)
            return
        push(mine, mine, seq_send.at[item, 0], seq_recv.at[item, 0], {"seq": beside})
        push(mine, mine, seq_send.at[item, 1], seq_recv.at[item, 1], {"seq": across})

    def spread_second(item, buffer):
        if not square:
            return
        arrived(block(buffer, beside, rows), seq_recv.at[item, 0])
        part_one = halves(item, buffer, beside, 0)
        push(part_one, part_one, seq_send.at[item, 2], seq_recv.at[item, 2], {"seq": across})
        arrived(block(buffer, across, rows), seq_recv.at[item, 1])
        part_two = halves(item, buffer, across, 1)
        push(part_two, part_two, seq_send.at[item, 3], seq_recv.at[item, 3], {"seq": beside})

    def spread_wait(item, buffer):
        if not square:
            seq_wait(item, lambda j: block(buffer, j, rows))
            return
        arrived(halves(item, buffer, corner, 0), seq_recv.at[item, 2])
        arrived(halves(item, buffer, corner, 1), seq_recv.at[item, 3])

    dense_rows, mid_rows, shrink_rows = part // m, width // m, hidden // m
    chains = {
        "dense": (0, ref["dense_all"], dense_rows, 0, dense_rows),
        "joint_a": (1, ref["joint_all"], mid_rows, 0, mid_rows // 2),
        "joint_b": (2, ref["joint_all"], mid_rows, mid_rows // 2, mid_rows // 2),
        "expand_a": (3, ref["expand_all"], mid_rows, 0, mid_rows // 2),
        "expand_b": (4, ref["expand_all"], mid_rows, mid_rows // 2, mid_rows // 2),
        "shrink_a": (5, ref["shrink_all"], shrink_rows, 0, shrink_rows // 2),
        "shrink_b": (6, ref["shrink_all"], shrink_rows, shrink_rows // 2, shrink_rows // 2),
    }
    ag_send, ag_recv = ref["ag_send"], ref["ag_recv"]
    swap_send, swap_recv = ref["swap_send"], ref["swap_recv"]

    def shard(name, owner):
        _, buffer, size, offset, count = chains[name]
        return block(buffer, owner, size, offset, count)

    def gather_step(name, hop):
        number = chains[name][0]

        def swap(owner, when=None):
            view = shard(name, owner * CORES + c)
            push(
                view,
                view,
                swap_send.at[number, owner],
                swap_recv.at[number, owner],
                {"dp": other},
                when,
            )

        def forward(side, owner, when):
            view = shard(name, owner * CORES + c)
            push(
                view,
                view,
                ag_send.at[number, side, hop],
                ag_recv.at[number, side, hop],
                {"dp": d + CORES if side == 0 else d - CORES},
                when,
            )

        if hop == 0:
            forward(0, z, z < line - 1)
            forward(1, z, z > 0)
            swap(z)
            return
        for side, owner, valid, more in (
            (0, z - hop, z >= hop, z < line - 1),
            (1, z + hop, z + hop < line, z > 0),
        ):
            owner = (owner + line) % line
            view = shard(name, owner * CORES + c)
            pl.when(valid)(functools.partial(arrived, view, ag_recv.at[number, side, hop - 1]))
            if hop < hops:
                forward(side, owner, valid & more)
            swap(owner, valid)

    def gather_wait(name):
        for owner in range(line):
            arrived(shard(name, owner * CORES + 1 - c), swap_recv.at[chains[name][0], owner])

    groups = (("dense", "joint_a", "joint_b"), ("expand_a", "expand_b"), ("shrink_a", "shrink_b"))
    gather_queue = []
    for index, group in enumerate(groups):
        following = groups[index + 1] if index + 1 < len(groups) else ()
        for hop in range(1, hops + 1):
            for place, name in enumerate(group):
                gather_queue.append((name, hop))
                if hop == hops and place < len(following):
                    gather_queue.append((following[place], 0))

    def gather(upto):
        while gather_queue:
            entry = gather_queue.pop(0)
            gather_step(*entry)
            if entry == upto:
                return

    sums = {
        "dense": (0, "dense", 0, dense_rows, width),
        "joint_a": (1, "joint", 0, mid_rows // 2, 3 * part),
        "joint_b": (2, "joint", mid_rows // 2, mid_rows // 2, 3 * part),
        "expand_a": (3, "expand", 0, mid_rows // 2, hidden),
        "expand_b": (4, "expand", mid_rows // 2, mid_rows // 2, hidden),
        "shrink_a": (5, "shrink", 0, shrink_rows // 2, width),
        "shrink_b": (6, "shrink", shrink_rows // 2, shrink_rows // 2, width),
    }
    core_send, core_recv = ref["core_send"], ref["core_recv"]
    rs_send, rs_recv = ref["rs_send"], ref["rs_recv"]
    adds, add_sem = ref["adds"], ref["add_sem"]

    def reduce_start(name):
        number, kind, offset, count, _ = sums[name]
        push(
            ref[kind + "_sum"].at[:, 1 - c, pl.ds(offset, count)],
            ref[kind + "_core"].at[:, pl.ds(offset, count)],
            core_send.at[number],
            core_recv.at[number],
            {"dp": other},
        )

    def added(sources, count, columns, into):
        copies = []
        for slot, source in enumerate(sources):
            copies.append(local(source, adds.at[slot, pl.ds(0, count), pl.ds(0, columns)], add_sem.at[slot]))
        for copy in copies:
            copy.wait()

        @pl.loop(0, count // 16)
        def _(i):
            at = pl.ds(pl.multiple_of(i * 16, 16), 16)
            total = adds[0, at, 0:columns].astype(F32)
            for slot in range(1, len(sources)):
                total = total + adds[slot, at, 0:columns].astype(F32)
            into(at, total)

    def reduce_hop(name, hop):
        number, kind, offset, count, columns = sums[name]
        at = pl.ds(offset, count)
        held, core, chain = ref[kind + "_sum"], ref[kind + "_core"], ref[kind + "_chain"]
        if hop == 1:
            arrived(core.at[:, at], core_recv.at[number])

        def keep(where, total):
            adds[0, where, 0:columns] = total.astype(BF)

        for side, target, valid, joined in (
            (0, z + line - hop, z < hop, z > 0),
            (1, z - line + hop, z + hop >= line, z < line - 1),
        ):
            target = (target + line) % line
            mine, theirs = held.at[target, c, at], core.at[target, at]
            behind = chain.at[side, target, at]

            @pl.when(valid)
            def _():
                if hop > 1:

                    @pl.when(joined)
                    def _():
                        arrived(behind, rs_recv.at[number, side, hop - 2])
                        added((mine, theirs, behind), count, columns, keep)

                    @pl.when(jnp.logical_not(joined))
                    def _():
                        added((mine, theirs), count, columns, keep)
                else:
                    added((mine, theirs), count, columns, keep)
                local(adds.at[0, pl.ds(0, count), pl.ds(0, columns)], mine, add_sem.at[0]).wait()

            push(
                mine,
                behind,
                rs_send.at[number, side, hop - 1],
                rs_recv.at[number, side, hop - 1],
                {"dp": d + CORES if side == 0 else d - CORES},
                valid,
            )

    def reduce_last(name, into):
        number, kind, offset, count, columns = sums[name]
        at = pl.ds(offset, count)
        held, core, chain = ref[kind + "_sum"], ref[kind + "_core"], ref[kind + "_chain"]
        mine, theirs = held.at[z, c, at], core.at[z, at]
        below, above = chain.at[0, z, at], chain.at[1, z, at]

        @pl.when(z > 0)
        def _():
            arrived(below, rs_recv.at[number, 0, hops - 1])

        @pl.when(z < line - 1)
        def _():
            arrived(above, rs_recv.at[number, 1, hops - 1])

        @pl.when(z == 0)
        def _():
            added((mine, theirs, above), count, columns, into)

        @pl.when(z == line - 1)
        def _():
            added((mine, theirs, below), count, columns, into)

        @pl.when((z > 0) & (z < line - 1))
        def _():
            added((mine, theirs, below, above), count, columns, into)

    def finish_direct(name, out):
        _, _, offset, count, columns = sums[name]

        def keep(where, total):
            ref["wide_one"][where, 0:columns] = total

        reduce_last(name, keep)
        local(ref["wide_one"].at[pl.ds(0, count), pl.ds(0, columns)], out.at[pl.ds(offset, count)], add_sem.at[0]).wait()

    def finish_exchange(name, item, out):
        _, kind, offset, count, columns = sums[name]
        done = ref[kind + "_done"]

        def keep(where, total):
            adds[0, where, 0:columns] = total.astype(BF)

        reduce_last(name, keep)
        local(adds.at[0, pl.ds(0, count), pl.ds(0, columns)], done.at[pl.ds(offset, count)], add_sem.at[0]).wait()
        for j in range(offset // piece, (offset + count) // piece):
            view = done.at[pl.ds(j * piece, piece)]
            k = (j - s + n) % n
            mine = block(out, s, piece)
            push(view, mine, seq_send.at[item, k], seq_recv.at[item, k], {"seq": j}, k != 0)

            @pl.when(k == 0)
            def _():
                local(view, mine, add_sem.at[0]).wait()

    upstream, normed = ref["upstream"], ref["normed"]
    qkv, gate, mixed, grad_qkv = ref["qkv"], ref["gate"], ref["mixed"], ref["grad_qkv"]
    act, slope = ref["act"], ref["slope"]
    left, right, dense = ref["left"], ref["right"], ref["dense"]
    wide_one, wide_two = ref["wide_one"], ref["wide_two"]
    stage, stage_sem, load_sem = ref["stage"], ref["stage_sem"], ref["load_sem"]
    x_sem = ref["x_sem"]
    gains, tables = ref["gains"], ref["tables"]
    small = 32

    def tile(i, size=rows):
        return pl.ds(pl.multiple_of(i * size, size), size)

    def each_tile(body):
        load = lambda i: local(ref["tokens_all"].at[pl.ds(i * rows, rows)], stage.at[i % 2, pl.ds(0, rows), pl.ds(0, width)], x_sem.at[i % 2])
        copy = load(0)
        for i in range(n):
            copy.wait()
            if i + 1 < n:
                copy = load(i + 1)
            body(i, i % 2)

    def normal_of(slot, at):
        value = stage[slot, at, 0:width].astype(F32)
        center = value - jnp.mean(value, axis=-1, keepdims=True)
        return center * lax.rsqrt(jnp.mean(center * center, axis=-1, keepdims=True) + 1e-05)

    def norm_stage(which):
        def body(i, slot):
            @pl.loop(0, rows // small)
            def _(j):
                value = normal_of(slot, tile(j, small))
                value = value * gains[2 * which : 2 * which + 1, :] + gains[2 * which + 1 : 2 * which + 2, :]
                at = pl.ds(pl.multiple_of(i * rows + j * small, small), small)
                normed[at, :] = value.astype(BF)

        each_tile(body)

    def turn(value, at, sign):
        head = value[:, :LANES]
        lane = lax.broadcasted_iota(jnp.int32, head.shape, 1)
        lower = -sign * pltpu.roll(head, LANES - ROT // 2, 1)
        upper = sign * pltpu.roll(head, ROT // 2, 1)
        head = head * tables[0, at, :] + jnp.where(lane < ROT // 2, lower, upper) * tables[1, at, :]
        if value.shape[1] == LANES:
            return head
        return jnp.concatenate([head, value[:, LANES:]], axis=1)

    def joint_stage():
        @pl.loop(0, n)
        def _(i):
            at = tile(i)
            joint = nn(normed[at, :], right[0:width, 0 : 3 * part]) + ref["joint_bias"][...]
            for kind in range(3):
                for head in range(heads):
                    first = kind * part + head * head_size
                    value = joint[:, first : first + head_size]
                    if kind < 2:
                        value = turn(value, at, 1.0)
                    qkv[at, first : first + head_size] = value.astype(BF)

    def gate_stage():
        @pl.loop(0, n)
        def _(i):
            gate[tile(i), :] = nt(upstream[tile(i), :], dense[...]).astype(BF)

    query_tile = rows
    grad_key, grad_value = wide_one, wide_two

    def attend_tile(head, i):
        keys = (i + 1) * query_tile
        at = pl.ds(i * query_tile, query_tile)
        seen = pl.ds(0, keys)
        q_at = pl.ds(head * head_size, head_size)
        k_at = pl.ds(part + head * head_size, head_size)
        v_at = pl.ds(2 * part + head * head_size, head_size)
        query = qkv[at, q_at]
        scores = nt(query, qkv[seen, k_at]) * scale
        row = lax.broadcasted_iota(jnp.int32, (query_tile, keys), 0) + i * query_tile
        column = lax.broadcasted_iota(jnp.int32, (query_tile, keys), 1)
        scores = jnp.where(column <= row, scores, -1e30)
        expo = jnp.exp(scores - jnp.max(scores, axis=-1, keepdims=True))
        probs = expo / jnp.sum(expo, axis=-1, keepdims=True)
        low = probs.astype(BF)
        mixed[at, q_at] = nn(low, qkv[seen, v_at]).astype(BF)
        back = gate[at, q_at]
        grad_probs = nt(back, qkv[seen, v_at])
        inner = jnp.sum(probs * grad_probs, axis=-1, keepdims=True)
        grad_scores = (probs * (grad_probs - inner)).astype(BF)
        grad_query = nn(grad_scores, qkv[seen, k_at]) * scale
        grad_qkv[at, q_at] = turn(grad_query, at, -1.0).astype(BF)
        key_part, value_part = tn(grad_scores, query), tn(low, back)
        for b in range(i + 1):
            here = (slice(0, rows), slice(b * head_size, (b + 1) * head_size))
            for total, added_part in ((grad_key, key_part), (grad_value, value_part)):
                added_part = added_part[b * rows : (b + 1) * rows]
                total[here] = added_part if i == n - 1 else total[here] + added_part

    def attend_stage(head):
        for i in range(n - 1, -1, -1):
            attend_tile(head, i)

        for b in range(n):
            at = pl.ds(b * rows, rows)
            here = (slice(0, rows), slice(b * head_size, (b + 1) * head_size))
            k_at = pl.ds(part + head * head_size, head_size)
            v_at = pl.ds(2 * part + head * head_size, head_size)
            grad_qkv[at, k_at] = turn(grad_key[here] * scale, at, -1.0).astype(BF)
            grad_qkv[at, v_at] = grad_value[here].astype(BF)

    def weight_grad(kind, left_of, right_of, count, columns):
        out = ref[kind + "_sum"]

        def stored(b, slot):
            return pltpu.make_async_copy(
                stage.at[slot, pl.ds(0, count), pl.ds(0, columns)],
                out.at[b // CORES, b % CORES],
                stage_sem.at[slot],
            )

        @pl.loop(0, m)
        def _(b):
            slot = b % 2

            @pl.when(b >= 2)
            def _():
                stored(b - 2, slot).wait()

            stage[slot, 0:count, 0:columns] = tn(left_of(b), right_of()).astype(BF)
            stored(b, slot).start()

        for b in range(max(m - 2, 0), m):
            stored(b, b % 2).wait()

    def dense_grad_stage():
        out = ref["dense_sum"]
        wide = min(part, stage.shape[1])
        for first in range(0, part, wide):
            stage[0, 0:wide, 0:width] = tn(mixed[:, first : first + wide], upstream[...]).astype(BF)
            copies = []
            for b in range(wide // dense_rows):
                owner = first // dense_rows + b
                copies.append(
                    local(
                        stage.at[0, pl.ds(b * dense_rows, dense_rows), pl.ds(0, width)],
                        out.at[owner // CORES, owner % CORES],
                        ref["dense_sem"].at[b],
                    )
                )
            for copy in copies:
                copy.wait()

    def columns_of(buffer, count):
        return lambda b: buffer[:, pl.ds(pl.multiple_of(b * count, LANES), count)]

    def expand_stage(start, stop):
        @pl.loop(start, stop)
        def _(i):
            wide_one[:, 0:hidden] = nn(normed[tile(i), :], left[...]) + ref["expand_bias"][...]

            @pl.loop(0, rows // small)
            def _(j):
                value = wide_one[tile(j, small), 0:hidden]
                share = 0.5 * (1.0 + lax.erf(value * 0.7071067811865476))
                density = jnp.exp(-0.5 * value * value) * 0.3989422804014327
                at = pl.ds(pl.multiple_of(i * rows + j * small, small), small)
                act[at, :] = (value * share).astype(BF)
                slope[at, :] = (share + value * density).astype(BF)

    def shrink_stage(start, stop):
        @pl.loop(start, stop)
        def _(i):
            wide_one[:, 0:hidden] = nt(upstream[tile(i), :], right[0:hidden, 0:width])

            @pl.loop(0, rows // small)
            def _(j):
                at = pl.ds(pl.multiple_of(i * rows + j * small, small), small)
                grad = (wide_one[tile(j, small), 0:hidden] * slope[at, :].astype(F32)).astype(BF)
                slope[at, :] = grad
                ref["expand_total"][...] += jnp.sum(grad.astype(F32), axis=0, keepdims=True)

    def owner_push(item, source, out, i):
        k = (i - s + n) % n
        mine = block(out, s, rows)
        push(source, mine, seq_send.at[item, k], seq_recv.at[item, k], {"seq": i}, k != 0)

        @pl.when(k == 0)
        def _():
            local(source, mine, add_sem.at[0]).wait()

    def output_stage(i):
        at = pl.ds(i * rows, rows)
        total = nn(mixed[at, :], dense[...]) + nn(act[at, :], right[0:hidden, 0:width])
        stage[i % 2, 0:rows, 0:width] = total.astype(BF)
        local(stage.at[i % 2, pl.ds(0, rows), pl.ds(0, width)], ref["output_part"].at[at], stage_sem.at[0]).wait()
        owner_push(4, ref["output_part"].at[at], ref["output_all"], i)

    def input_stage(i, slot):
        at = pl.ds(i * rows, rows)
        wide_one[:, 0:width] = nt(grad_qkv[at, :], right[0:width, 0 : 3 * part])
        wide_two[...] = nt(slope[at, :], left[...])

        @pl.loop(0, rows // small)
        def _(j):
            here = tile(j, small)
            normal = normal_of(slot, here)
            grad_one, grad_two = wide_one[here, 0:width], wide_two[here, :]
            total = grad_one * gains[0:1, :] + grad_two * gains[2:3, :]
            normed[pl.ds(pl.multiple_of(i * rows + j * small, small), small), :] = total.astype(BF)
            gain_total = ref["gain_total"]
            gain_total[0:1, :] += jnp.sum(grad_one * normal, axis=0, keepdims=True)
            gain_total[1:2, :] += jnp.sum(grad_one, axis=0, keepdims=True)
            gain_total[2:3, :] += jnp.sum(grad_two * normal, axis=0, keepdims=True)
            gain_total[3:4, :] += jnp.sum(grad_two, axis=0, keepdims=True)

        owner_push(5, normed.at[at], ref["input_all"], i)

    ref["gain_total"][...] = jnp.zeros_like(ref["gain_total"])
    ref["joint_total"][...] = jnp.zeros_like(ref["joint_total"])
    ref["expand_total"][...] = jnp.zeros_like(ref["expand_total"])
    own = [
        local(ref["dense_own"], block(ref["dense_all"], d, dense_rows), load_sem.at[0]),
        local(ref["joint_own"].at[s], joint_block := block(ref["joint_all"], d * n + s, piece), load_sem.at[1]),
        local(ref["expand_own"].at[s], expand_block := block(ref["expand_all"], d * n + s, piece), load_sem.at[2]),
        local(ref["shrink_own"], block(ref["shrink_all"], d, shrink_rows), load_sem.at[3]),
        local(ref["tokens"], block(ref["tokens_all"], s, rows), load_sem.at[4]),
        local(ref["cotangent"], block(upstream, s, rows), load_sem.at[5]),
    ]
    seq_push(0, lambda j: ref["joint_own"].at[j], joint_block)
    for copy in own:
        copy.wait()
    gather_step("dense", 0)
    seq_wait(0, lambda j: block(ref["joint_all"], d * n + j, piece))
    gather_step("joint_a", 0)
    gather_step("joint_b", 0)
    spread_first(2, ref["tokens_all"])
    seq_push(1, lambda j: ref["expand_own"].at[j], expand_block)
    gather(("dense", 1))
    spread_second(2, ref["tokens_all"])
    spread_first(3, upstream)
    gather(("joint_b", 1))
    seq_wait(1, lambda j: block(ref["expand_all"], d * n + j, piece))
    spread_wait(2, ref["tokens_all"])
    gather(("joint_b", 2) if hops > 2 else ("joint_b", hops))
    norm_stage(0)
    spread_second(3, upstream)
    gather(("joint_b", hops))
    for name in groups[0]:
        gather_wait(name)
    load_joint = local(ref["joint_all"], right.at[pl.ds(0, width), pl.ds(0, 3 * part)], load_sem.at[0])
    load_dense = local(ref["dense_all"], dense, load_sem.at[1])
    load_joint.wait()
    joint_stage()
    spread_wait(3, upstream)
    load_dense.wait()
    gather(("expand_b", 1))
    gate_stage()
    for head in range(heads):
        attend_stage(head)
        if head == 0:
            gather(("expand_b", 2) if hops > 2 else ("expand_b", hops))
    dense_grad_stage()
    reduce_start("dense")
    gather(("shrink_b", 0))
    weight_grad("joint", columns_of(normed, mid_rows), lambda: grad_qkv[...], mid_rows, 3 * part)
    reduce_start("joint_a")
    reduce_start("joint_b")

    @pl.loop(0, n)
    def _(i):
        ref["joint_total"][...] += jnp.sum(grad_qkv[tile(i), :].astype(F32), axis=0, keepdims=True)

    for name in ("expand_a", "expand_b"):
        gather_wait(name)
    load_expand = local(ref["expand_all"], left, load_sem.at[0])
    norm_stage(1)
    load_expand.wait()
    for name in ("dense", "joint_a", "joint_b"):
        reduce_hop(name, 1)
    expand_stage(0, n // 2)
    gather(("shrink_b", 1))
    expand_stage(n // 2, n)
    for name in ("dense", "joint_a", "joint_b"):
        reduce_hop(name, 2)
    weight_grad("shrink", columns_of(act, shrink_rows), lambda: upstream[...], shrink_rows, width)
    reduce_start("shrink_a")
    reduce_start("shrink_b")
    for hop in range(3, hops + 1):
        for name in ("dense", "joint_a", "joint_b"):
            reduce_hop(name, hop)
    gather(("shrink_b", 2) if hops > 2 else ("shrink_b", hops))
    reduce_hop("shrink_a", 1)
    reduce_hop("shrink_b", 1)
    gather(("shrink_b", hops))
    for name in ("shrink_a", "shrink_b"):
        gather_wait(name)
    local(ref["shrink_all"], right.at[pl.ds(0, hidden), pl.ds(0, width)], load_sem.at[0]).wait()
    shrink_stage(0, n)
    reduce_hop("shrink_a", 2)
    reduce_hop("shrink_b", 2)
    weight_grad("expand", columns_of(normed, mid_rows), lambda: slope[...], mid_rows, hidden)
    reduce_start("expand_a")
    reduce_start("expand_b")
    for hop in range(3, hops + 1):
        for name in ("shrink_a", "shrink_b"):
            reduce_hop(name, hop)
    finish_direct("dense", ref["dense_grad"])
    finish_exchange("joint_a", 6, ref["joint_grad"])
    finish_exchange("joint_b", 6, ref["joint_grad"])
    for i in range(n // 2):
        output_stage(i)
    reduce_hop("expand_a", 1)
    reduce_hop("expand_b", 1)
    for i in range(n // 2, n):
        output_stage(i)
    load_joint = local(ref["joint_all"], right.at[pl.ds(0, width), pl.ds(0, 3 * part)], load_sem.at[0])
    reduce_hop("expand_a", 2)
    reduce_hop("expand_b", 2)
    load_joint.wait()
    each_tile(input_stage)
    for hop in range(3, hops + 1):
        for name in ("expand_a", "expand_b"):
            reduce_hop(name, hop)
    finish_direct("shrink_a", ref["shrink_grad"])
    finish_direct("shrink_b", ref["shrink_grad"])
    finish_exchange("expand_a", 7, ref["expand_grad"])
    finish_exchange("expand_b", 7, ref["expand_grad"])
    seq_wait(4, lambda j: block(ref["output_all"], j, rows))
    seq_wait(5, lambda j: block(ref["input_all"], j, rows))
    seq_wait(6, lambda j: block(ref["joint_grad"], j, piece))
    seq_wait(7, lambda j: block(ref["expand_grad"], j, piece))
    for copy, when in drains:
        if when is None:
            copy.wait_send()
        else:
            pl.when(when)(copy.wait_send)


def run_kernel(n, m, dims, inputs):
    rows, width, piece, part, hidden, heads, head_size = dims
    line, length = m // CORES, rows * n
    hops = line - 1
    dense_rows, mid_rows, shrink_rows = part // m, width // m, hidden // m
    high = max(rows, mid_rows, shrink_rows)
    broad = max(width, hidden, 3 * part)
    anywhere, vmem = pl.BlockSpec(memory_space=pl.ANY), pl.BlockSpec(memory_space=pltpu.VMEM)
    outputs = {
        "output_all": ((length, width), BF),
        "input_all": ((length, width), BF),
        "dense_grad": ((dense_rows, width), F32),
        "shrink_grad": ((shrink_rows, width), F32),
        "joint_grad": ((n * piece, 3 * part), BF),
        "expand_grad": ((n * piece, hidden), BF),
        "gain_total": ((4, width), F32),
        "joint_total": ((1, 3 * part), F32),
        "expand_total": ((1, hidden), F32),
        "dense_all": ((part, width), BF),
        "joint_all": ((width, 3 * part), BF),
        "expand_all": ((width, hidden), BF),
        "shrink_all": ((hidden, width), BF),
        "tokens_all": ((length, width), BF),
        "output_part": ((length, width), BF),
        "joint_done": ((mid_rows, 3 * part), BF),
        "expand_done": ((mid_rows, hidden), BF),
    }
    shapes = {
        "dense": (dense_rows, width),
        "joint": (mid_rows, 3 * part),
        "expand": (mid_rows, hidden),
        "shrink": (shrink_rows, width),
    }
    for kind, shape in shapes.items():
        outputs[kind + "_sum"] = ((line, CORES) + shape, BF)
        outputs[kind + "_core"] = ((line,) + shape, BF)
        outputs[kind + "_chain"] = ((2, line) + shape, BF)
    in_vmem = ("gain_total", "joint_total", "expand_total")
    dma = pltpu.SemaphoreType.DMA
    scratch = {
        "upstream": pltpu.VMEM((length, width), BF),
        "normed": pltpu.VMEM((length, width), BF),
        "qkv": pltpu.VMEM((length, 3 * part), BF),
        "gate": pltpu.VMEM((length, part), BF),
        "mixed": pltpu.VMEM((length, part), BF),
        "grad_qkv": pltpu.VMEM((length, 3 * part), BF),
        "act": pltpu.VMEM((length, hidden), BF),
        "slope": pltpu.VMEM((length, hidden), BF),
        "left": pltpu.VMEM((width, hidden), BF),
        "right": pltpu.VMEM((max(width, hidden), max(width, 3 * part)), BF),
        "dense": pltpu.VMEM((part, width), BF),
        "wide_one": pltpu.VMEM((max(rows, shrink_rows // 2), max(width, hidden)), F32),
        "wide_two": pltpu.VMEM((rows, width), F32),
        "stage": pltpu.VMEM((2, high, broad), BF),
        "adds": pltpu.VMEM((4, max(mid_rows, shrink_rows) // 2, broad), BF),
        "seq_send": dma((8, max(n, 4))),
        "seq_recv": dma((8, max(n, 4))),
        "ag_send": dma((7, 2, hops)),
        "ag_recv": dma((7, 2, hops)),
        "swap_send": dma((7, line)),
        "swap_recv": dma((7, line)),
        "core_send": dma((7,)),
        "core_recv": dma((7,)),
        "rs_send": dma((7, 2, hops)),
        "rs_recv": dma((7, 2, hops)),
        "add_sem": dma((4,)),
        "stage_sem": dma((2,)),
        "load_sem": dma((6,)),
        "x_sem": dma((2,)),
        "dense_sem": dma((max(m, 8),)),
    }
    resident = ("gains", "joint_bias", "expand_bias", "tables")
    names = list(inputs) + list(outputs) + list(scratch)
    results = pl.pallas_call(
        functools.partial(kernel, n, m, dims, names),
        out_shape=[jax.ShapeDtypeStruct(shape, kind) for shape, kind in outputs.values()],
        in_specs=[vmem if name in resident else anywhere for name in inputs],
        out_specs=[vmem if name in in_vmem else anywhere for name in outputs],
        scratch_shapes=list(scratch.values()),
        compiler_params=pltpu.CompilerParams(
            collective_id=0, has_side_effects=True, vmem_limit_bytes=63 * 2**20
        ),
        cost_estimate=pl.CostEstimate(flops=10**11, bytes_accessed=10**9, transcendentals=0),
        name="block",
    )(*inputs.values())
    return dict(zip(outputs, results))


def block_plan(n, m, tokens, cotangent, shards):
    (
        first_gain,
        first_shift,
        second_gain,
        second_shift,
        joint_weight,
        joint_bias,
        dense_weight,
        dense_bias,
        expand_weight,
        expand_bias,
        shrink_weight,
        shrink_bias,
    ) = shards
    devices = n * m
    own, upstream = tokens[0], cotangent[0]
    rows, width = own.shape
    piece = width // devices
    head_size = width // HEADS
    heads = HEADS // n
    part = width // n
    hidden = expand_weight.shape[1] // n
    s = lax.axis_index("seq")

    def shuffle(values):
        shape = values.shape[:-1]
        values = values.reshape(shape + (n, m, piece))
        return jnp.swapaxes(values, -3, -2).reshape(shape + (width,))

    def unshuffle(values):
        shape = values.shape[:-1]
        values = values.reshape(shape + (m, n, piece))
        return jnp.swapaxes(values, -3, -2).reshape(shape + (width,))

    def pick(stack):
        return lax.dynamic_index_in_dim(stack, s, 0, keepdims=False)

    vectors = (
        first_gain,
        first_shift,
        second_gain,
        second_shift,
        joint_bias,
        dense_bias,
        expand_bias,
        shrink_bias,
    )
    packed = lax.all_gather(jnp.concatenate(vectors)[None], ("seq", "dp"), axis=0, tiled=True)
    full, start = [], 0
    for vector in vectors:
        full.append(packed[:, start : start + vector.shape[0]].reshape(-1).astype(F32))
        start += vector.shape[0]
    gains = shuffle(jnp.stack(full[:4]))
    joint_offset, dense_offset, expand_offset, shrink_offset = full[4:]
    inputs = {
        "tokens": shuffle(own),
        "cotangent": upstream,
        "joint_own": jnp.transpose(joint_weight.reshape(piece, 3, n, part), (2, 0, 1, 3)).reshape(
            n, piece, 3 * part
        ),
        "expand_own": jnp.swapaxes(expand_weight.reshape(piece, n, hidden), 0, 1),
        "dense_own": dense_weight,
        "shrink_own": shrink_weight,
        "gains": gains,
        "joint_bias": pick(jnp.swapaxes(joint_offset.reshape(3, n, part), 0, 1)).reshape(1, 3 * part),
        "expand_bias": pick(expand_offset.reshape(n, 1, hidden)),
        "tables": turn_tables(rows * n),
    }
    dims = (rows, width, piece, part, hidden, heads, head_size)
    got = run_kernel(n, m, dims, inputs)

    summed = jnp.sum(got["output_all"].reshape(n, rows, width).astype(F32), axis=0)
    own_wide = own.astype(F32)
    output = (own_wide + (summed + (dense_offset + shrink_offset))).astype(BF)[None]

    grad_normal = jnp.sum(got["input_all"].reshape(n, rows, width).astype(F32), axis=0)
    grad_normal = unshuffle(grad_normal)
    center = own_wide - jnp.mean(own_wide, axis=-1, keepdims=True)
    spread = lax.rsqrt(jnp.mean(center * center, axis=-1, keepdims=True) + 1e-05)
    normal = center * spread
    through = grad_normal - jnp.mean(grad_normal, axis=-1, keepdims=True)
    through = through - normal * jnp.mean(grad_normal * normal, axis=-1, keepdims=True)
    upstream_wide = upstream.astype(F32)
    grad_tokens = (upstream_wide + spread * through)[None]

    def placed(vector, groups):
        blocks = vector.reshape(groups, 1, -1)
        mine = (jnp.arange(n) == s).reshape(1, n, 1)
        return jnp.where(mine, blocks, 0.0).reshape(-1)

    gain_total = unshuffle(got["gain_total"])
    sums = (
        gain_total[0],
        gain_total[1],
        gain_total[2],
        gain_total[3],
        placed(got["joint_total"], 3),
        placed(got["expand_total"], 1),
        jnp.sum(upstream_wide, axis=0),
    )
    sums = jnp.concatenate([v.reshape(devices, -1) for v in sums], axis=1)
    sums = lax.psum_scatter(sums, ("seq", "dp"), scatter_dimension=0, tiled=True)[0]
    small, start = [], 0
    for length_of in (piece, piece, piece, piece, joint_bias.shape[0], expand_bias.shape[0], piece):
        small.append(sums[start : start + length_of])
        start += length_of

    joint_grad = got["joint_grad"].reshape(n, piece, 3, part)
    joint_grad = jnp.transpose(joint_grad, (1, 2, 0, 3)).reshape(piece, 3 * width).astype(F32)
    expand_grad = got["expand_grad"].reshape(n, piece, hidden)
    expand_grad = jnp.swapaxes(expand_grad, 0, 1).reshape(piece, n * hidden).astype(F32)
    return (
        output,
        grad_tokens,
        small[0],
        small[1],
        small[2],
        small[3],
        joint_grad,
        small[4],
        got["dense_grad"],
        small[6],
        expand_grad,
        small[5],
        got["shrink_grad"],
        small[6],
    )


def solution(mesh):
    n, m = mesh.shape["seq"], mesh.shape["dp"]

    def body(tokens, cotangent, *shards):
        return block_plan(n, m, tokens, cotangent, shards)

    both = ("seq", "dp")
    tokens = P("dp", "seq", None)
    vector, matrix = P(both), P(both, None)
    return jax.shard_map(
        body,
        mesh=mesh,
        in_specs=(tokens, tokens) + (vector,) * 4 + (matrix, vector) * 4,
        out_specs=(tokens, tokens) + (vector,) * 4 + (matrix, vector) * 4,
        check_vma=False,
    )
```

```python
import functools
import types

import jax
import jax.numpy as jnp
from jax import lax
from jax.experimental import pallas as pl
from jax.experimental.pallas import tpu as pltpu
from jax.sharding import PartitionSpec as P

HEADS = 8
ROT = 64
CORES = 2
LANES = 128
VECTOR_ROWS = 16
SEQ, DP = "seq", "dp"
BF = jnp.bfloat16
F32 = jnp.float32
MESH = pl.DeviceIdType.MESH


def nn(left, right):
    return jnp.dot(left, right, preferred_element_type=F32)


def nt(left, right):
    return lax.dot_general(left, right, (((1,), (1,)), ((), ())), preferred_element_type=F32)


def tn(left, right):
    return lax.dot_general(left, right, (((0,), (0,)), ((), ())), preferred_element_type=F32)


def turn_tables(length):
    inverse = 10000.0 ** (-jnp.arange(0, ROT, 2, dtype=F32) / ROT)
    angle = jnp.arange(length, dtype=F32)[:, None] * inverse[None, :]
    cosine, sine = jnp.cos(angle), jnp.sin(angle)
    rest = jnp.zeros((length, LANES - ROT), F32)
    return jnp.stack(
        [
            jnp.concatenate([cosine, cosine, rest + 1.0], axis=1),
            jnp.concatenate([sine, sine, rest], axis=1),
        ]
    )


def sizes_of(n, m, rows, width, feed):
    devices = n * m
    z = types.SimpleNamespace(n=n, m=m, rows=rows, width=width)
    z.line, z.hops = m // CORES, m // CORES - 1
    z.length = rows * n
    z.piece = width // devices
    z.part = width // n
    z.hidden = feed // n
    z.heads, z.head_size = HEADS // n, width // HEADS
    z.dense_rows, z.mid_rows, z.shrink_rows = z.part // m, width // m, z.hidden // m
    z.feed_pieces = feed // width
    z.high = max(rows, z.mid_rows, z.shrink_rows)
    z.broad = max(width, z.hidden, 3 * z.part)
    z.chunk = max(z.mid_rows, z.shrink_rows) // 2
    z.gain_rows = width // LANES
    z.joint_small = 5 * z.gain_rows
    z.expand_small = z.joint_small + 3 * z.part // LANES
    z.small = -(-(z.expand_small + z.hidden // LANES) // 8) * 8
    return z


def kernel(size, names, *refs):
    ref = types.SimpleNamespace(**dict(zip(names, refs)))
    n, m, line, hops = size.n, size.m, size.line, size.hops
    rows, width, piece, part, hidden = size.rows, size.width, size.piece, size.part, size.hidden
    heads, head_size, length = size.heads, size.head_size, size.length
    dense_rows, mid_rows, shrink_rows = size.dense_rows, size.mid_rows, size.shrink_rows
    scale = head_size ** (-0.5)
    s, d = lax.axis_index(SEQ), lax.axis_index(DP)
    z, c = d // CORES, d % CORES
    twin = {DP: z * CORES + 1 - c}
    above, below = {DP: d + CORES}, {DP: d - CORES}
    drains = []

    def remote(src, dst, send, recv, device):
        return pltpu.make_async_remote_copy(
            src_ref=src, dst_ref=dst, send_sem=send, recv_sem=recv, device_id=device, device_id_type=MESH
        )

    def push_all(make, when=None, keep=True):
        def start():
            pairs, _, send, recv, device = make()
            for src, dst in pairs:
                remote(src, dst, send, recv, device).start()

        def settle():
            _, whole, send, recv, device = make()
            remote(whole, whole, send, recv, device).wait_send()

        def guarded(step):
            return step if when is None else lambda: pl.when(when())(step)

        guarded(start)()
        if keep:
            drains.append(guarded(settle))
        return guarded(settle)

    def arrived(whole, recv):
        remote(whole, whole, recv, recv, twin).wait_recv()

    def local(src, dst, sem):
        copy = pltpu.make_async_copy(src, dst, sem)
        copy.start()
        return copy

    def span(index, size, count=None, offset=0):
        count = size if count is None else count
        return pl.ds(pl.multiple_of(index * size + offset, count), count)

    def lanes(index, size, offset=0):
        return pl.ds(pl.multiple_of(index * size + offset, LANES), size)

    barrier = pltpu.get_barrier_semaphore()
    greeted = [{SEQ: (s + k) % n} for k in range(1, n)]
    greeted += [{DP: (z + k) % line * CORES + c} for k in range(1, line)] + [twin]
    for device in greeted:
        pl.semaphore_signal(barrier, inc=1, device_id=device, device_id_type=MESH)
    pl.semaphore_wait(barrier, len(greeted))

    def seq_push(item, pairs_of, whole):
        for k in range(1, n):
            j = (s + k) % n
            push_all(
                lambda j=j, k=k: (
                    pairs_of(j), whole, ref.seq_send.at[item, k], ref.seq_recv.at[item, k], {SEQ: j}
                )
            )

    def seq_wait(item, whole):
        for k in range(1, n):
            arrived(whole, ref.seq_recv.at[item, k])

    square = n == 4
    beside, across = s + 1 - 2 * (s % 2), (s + 2) % n

    def spread_first(item, buffer):
        mine = buffer.at[span(s, rows)]
        if not square:
            seq_push(item, lambda j: [(mine, mine)], mine)
            return
        for way, target in ((0, beside), (1, across)):
            push_all(
                lambda way=way, target=target: (
                    [(mine, mine)], mine, ref.seq_send.at[item, way], ref.seq_recv.at[item, way], {SEQ: target}
                )
            )

    def spread_second(item, buffer):
        if not square:
            return
        for way, source, target in ((0, beside, across), (1, across, beside)):
            arrived(buffer.at[span(source, rows)], ref.seq_recv.at[item, way])
            half = buffer.at[span(source, rows, rows // 2, way * (rows // 2))]
            push_all(
                lambda way=2 + way, target=target, half=half: (
                    [(half, half)], half, ref.seq_send.at[item, way], ref.seq_recv.at[item, way], {SEQ: target}
                )
            )

    def spread_wait(item, buffer):
        if not square:
            seq_wait(item, buffer.at[pl.ds(0, rows)])
            return
        for way in range(2):
            arrived(buffer.at[pl.ds(0, rows // 2)], ref.seq_recv.at[item, 2 + way])

    def chain_of(number, buffer, runs, count):
        def views(owner):
            return [buffer.at[span(run(owner), count)] for run in runs]

        whole = buffer.at[pl.ds(0, count * len(runs))]
        return types.SimpleNamespace(number=number, views=views, whole=whole)

    def piece_runs(first, last):
        return [lambda owner, j=j: j * m + owner for j in range(first, last)]

    def half_runs(half):
        return [lambda owner: owner * 2 + half]

    dense_in = chain_of(0, ref.dense_all, [lambda owner: owner], dense_rows)
    joint_a = chain_of(1, ref.joint_all, piece_runs(0, n // 2), piece)
    joint_b = chain_of(2, ref.joint_all, piece_runs(n // 2, n), piece)
    expand_a = chain_of(3, ref.expand_all, piece_runs(0, n // 2), piece)
    expand_b = chain_of(4, ref.expand_all, piece_runs(n // 2, n), piece)
    shrink_a = chain_of(5, ref.shrink_all, half_runs(0), shrink_rows // 2)
    shrink_b = chain_of(6, ref.shrink_all, half_runs(1), shrink_rows // 2)
    vector_in = chain_of(7, ref.vectors, [lambda owner: owner], n * VECTOR_ROWS)

    def gather_step(chain, hop):
        number = chain.number

        def views(owner):
            return [(view, view) for view in chain.views(owner() * CORES + c)]

        def swap(owner, when=None):
            push_all(
                lambda: (
                    views(owner),
                    chain.whole,
                    ref.swap_send.at[number, owner()],
                    ref.swap_recv.at[number, owner()],
                    twin,
                ),
                when,
            )

        def forward(side, owner, when):
            push_all(
                lambda: (
                    views(owner),
                    chain.whole,
                    ref.ag_send.at[number, side, hop],
                    ref.ag_recv.at[number, side, hop],
                    below if side else above,
                ),
                when,
            )

        if hop == 0:
            forward(0, lambda: z, lambda: z < line - 1)
            forward(1, lambda: z, lambda: z > 0)
            swap(lambda: z)
            return
        for side, owner, valid, more in (
            (0, lambda: (z - hop + line) % line, lambda: z >= hop, lambda: z < line - 1),
            (1, lambda: (z + hop) % line, lambda: z + hop < line, lambda: z > 0),
        ):
            pl.when(valid())(functools.partial(arrived, chain.whole, ref.ag_recv.at[number, side, hop - 1]))
            if hop < hops:
                forward(side, owner, lambda valid=valid, more=more: valid() & more())
            swap(owner, valid)

    def gather_wait(*chains):
        for chain in chains:
            for owner in range(line):
                arrived(chain.whole, ref.swap_recv.at[chain.number, owner])

    groups = (
        (vector_in, dense_in, joint_a, joint_b),
        (expand_a, expand_b),
        (shrink_a, shrink_b),
    )
    gather_queue = []
    for index, group in enumerate(groups):
        following = groups[index + 1] if index + 1 < len(groups) else ()
        for hop in range(1, hops + 1):
            for place, chain in enumerate(group):
                gather_queue.append((chain, hop))
                place -= len(group) - len(following)
                if hop == hops and 0 <= place:
                    gather_queue.append((following[place], 0))

    def gather(chain, hop):
        while gather_queue:
            entry = gather_queue.pop(0)
            gather_step(*entry)
            if entry[0] is chain and entry[1] == min(hop, hops):
                return

    def kind_of(first, total, core, chain, halves, count, columns):
        return types.SimpleNamespace(
            first=first, total=total, core=core, chain=chain, halves=halves, count=count, columns=columns
        )

    mid, low = mid_rows // 2, shrink_rows // 2
    dense_kind = kind_of(0, ref.dense_sum, ref.dense_core, ref.dense_chain, 1, dense_rows, width)
    joint_kind = kind_of(1, ref.joint_sum, ref.joint_core, ref.joint_chain, 2, mid, 3 * part)
    expand_kind = kind_of(3, ref.expand_sum, ref.expand_core, ref.expand_chain, 2, mid, hidden)
    shrink_kind = kind_of(5, ref.shrink_sum, ref.shrink_core, ref.shrink_chain, 2, low, width)
    adds, add_sem, sent = ref.adds, ref.add_sem, ref.sent
    rounds = types.SimpleNamespace(ring=0, pending=[None, None])

    def reduce_start(kind):
        for half in range(kind.halves):
            at = pl.ds(half * kind.count, kind.count)
            push_all(
                lambda at=at, half=half: (
                    [(kind.total.at[:, 1 - c, at], kind.core.at[:, at])],
                    kind.core.at[:, at],
                    ref.core_send.at[kind.first + half],
                    ref.core_recv.at[kind.first + half],
                    twin,
                )
            )

    def summed(slots, count, columns, into):
        @pl.loop(0, count // 16)
        def _(i):
            at = span(i, 16)
            total = adds[slots[0], at, 0:columns].astype(F32)
            for slot in slots[1:]:
                total = total + adds[slot, at, 0:columns].astype(F32)
            into(at, total)

    def added(sources, count, columns, into):
        copies = []
        for slot, source in enumerate(sources):
            copies.append(local(source, adds.at[slot, pl.ds(0, count), pl.ds(0, columns)], add_sem.at[slot]))
        for copy in copies:
            copy.wait()
        summed(range(len(sources)), count, columns, into)

    def add_slot(kind, slot):
        return adds.at[slot, pl.ds(0, kind.count), pl.ds(0, kind.columns)]

    def add_load(kind, source, slot):
        return pltpu.make_async_copy(source, add_slot(kind, slot), add_sem.at[slot])

    def blank(kind, slot):
        adds[slot, 0 : kind.count, 0 : kind.columns] = jnp.zeros((kind.count, kind.columns), BF)

    def reduce_round(kind, hop, side, valid):
        count, columns = kind.count, kind.columns
        ring = rounds.ring
        rounds.ring = 1 - ring
        if rounds.pending[ring] is not None:
            rounds.pending[ring]()
        target = lambda: (z + (line - hop) * (1 - 2 * side()) + line) % line
        joined = lambda: z + side() * (line - 1 - 2 * z) > 0
        device = lambda: {DP: d + CORES * (1 - 2 * side())}

        def at(half):
            return span(half, count)

        @pl.when(valid())
        def _():
            @pl.loop(0, kind.halves)
            def _(half):
                add_load(kind, kind.total.at[target(), c, at(half)], half * 3).start()
                add_load(kind, kind.core.at[target(), at(half)], half * 3 + 1).start()

            @pl.loop(0, kind.halves)
            def _(half):
                behind = kind.chain.at[side(), target(), at(half)]
                slots = [half * 3, half * 3 + 1]
                if hop > 1:
                    slots.append(half * 3 + 2)

                    @pl.when(joined())
                    def _():
                        arrived(behind, ref.rs_recv.at[kind.first + half, side(), hop - 2])
                        add_load(kind, behind, half * 3 + 2).start()

                    @pl.when(jnp.logical_not(joined()))
                    def _():
                        blank(kind, half * 3 + 2)

                add_load(kind, kind.total.at[target(), c, at(half)], half * 3).wait()
                add_load(kind, kind.core.at[target(), at(half)], half * 3 + 1).wait()
                if hop > 1:

                    @pl.when(joined())
                    def _():
                        add_load(kind, behind, half * 3 + 2).wait()

                def keep(where, total):
                    sent[ring * 2 + half, where, 0:columns] = total.astype(BF)

                summed(slots, count, columns, keep)
                remote(
                    sent.at[ring * 2 + half, pl.ds(0, count), pl.ds(0, columns)],
                    behind,
                    ref.rs_send.at[kind.first + half, side(), hop - 1],
                    ref.rs_recv.at[kind.first + half, side(), hop - 1],
                    device(),
                ).start()

        def settle():
            @pl.when(valid())
            def _():
                view = sent.at[0, pl.ds(0, count), pl.ds(0, columns)]
                for half in range(kind.halves):
                    remote(
                        view,
                        view,
                        ref.rs_send.at[kind.first + half, side(), hop - 1],
                        ref.rs_recv.at[kind.first + half, side(), hop - 1],
                        device(),
                    ).wait_send()

        rounds.pending[ring] = settle

    def reduce_hop(hop, *kinds):
        if hop > hops:
            return
        for kind in kinds:
            if hop == 1:
                for half in range(kind.halves):
                    arrived(
                        kind.core.at[:, pl.ds(half * kind.count, kind.count)], ref.core_recv.at[kind.first + half]
                    )
            if 2 * hop <= line:
                reduce_round(kind, hop, lambda: z * 2 // line, lambda: (z < hop) | (z >= line - hop))
            else:
                reduce_round(kind, hop, lambda: 0, lambda: z < hop)
                reduce_round(kind, hop, lambda: 1, lambda: z >= line - hop)

    def reduce_last(kind, half, into):
        at = span(half, kind.count)
        sources = [kind.total.at[z, c, at], kind.core.at[z, at], kind.chain.at[0, z, at], kind.chain.at[1, z, at]]
        for slot in range(2):
            add_load(kind, sources[slot], slot).start()
        for side, there in ((0, lambda: z > 0), (1, lambda: z < line - 1)):

            @pl.when(there())
            def _():
                arrived(sources[2 + side], ref.rs_recv.at[kind.first + half, side, hops - 1])
                add_load(kind, sources[2 + side], 2 + side).start()

            @pl.when(jnp.logical_not(there()))
            def _():
                blank(kind, 2 + side)

        for slot in range(2):
            add_load(kind, sources[slot], slot).wait()
        for side, there in ((0, lambda: z > 0), (1, lambda: z < line - 1)):
            pl.when(there())(lambda: add_load(kind, sources[2 + side], 2 + side).wait())

        def keep(where, total):
            into[where, 0 : kind.columns] = total

        summed(range(4), kind.count, kind.columns, keep)

    def finish_rows(kind, out):
        @pl.loop(0, kind.halves)
        def _(half):
            reduce_last(kind, half, ref.wide_one)
            view = ref.wide_one.at[pl.ds(0, kind.count), pl.ds(0, kind.columns)]
            local(view, out.at[span(half, kind.count)], add_sem.at[0]).wait()

    def finish_columns(kind, item, done, out, kinds):
        wide = kind.columns // kinds
        whole = done.at[pl.ds(0, piece)]
        each = kind.count // piece

        def pairs(j):
            return [
                (
                    done.at[span(j, piece), pl.ds(part_of * wide, wide)],
                    out.at[:, lanes(s, wide, part_of * wide * n)],
                )
                for part_of in range(kinds)
            ]

        def sems(j):
            k = (j - s + n) % n
            return ref.seq_send.at[item, k], ref.seq_recv.at[item, k], {SEQ: j}

        @pl.loop(0, kind.halves)
        def _(half):
            reduce_last(kind, half, ref.wide_one)
            view = ref.wide_one.at[pl.ds(0, kind.count), pl.ds(0, kind.columns)]
            local(view, done.at[span(half, kind.count)], add_sem.at[0]).wait()

            @pl.loop(0, each)
            def _(q):
                j = half * each + q

                @pl.when(j != s)
                def _():
                    for src, dst in pairs(j):
                        remote(src, dst, *sems(j)).start()

                @pl.when(j == s)
                def _():
                    copies = [
                        local(
                            ref.wide_one.at[span(q, piece), pl.ds(part_of * wide, wide)],
                            pairs(j)[part_of][1],
                            add_sem.at[part_of],
                        )
                        for part_of in range(kinds)
                    ]
                    for copy in copies:
                        copy.wait()

        for k in range(1, n):
            drains.append(lambda k=k: remote(whole, whole, *sems((s + k) % n)).wait_send())

    upstream, normed, qkv = ref.upstream, ref.normed, ref.qkv
    gate, mixed, grad_qkv = ref.gate, ref.mixed, ref.grad_qkv
    act, slope = ref.act, ref.slope
    left, right, dense = ref.left, ref.right, ref.dense
    wide_one, wide_two = ref.wide_one, ref.wide_two
    stage, gains, tables = ref.stage, ref.gains, ref.tables
    few = 32

    def joined_row(rows_of):
        lane = lax.broadcasted_iota(jnp.int32, (1, LANES), 1)
        value = ref.vectors[pl.ds(rows_of(0), 1), :]
        for q in range(1, LANES // piece):
            value = jnp.where(lane >= q * piece, ref.vectors[pl.ds(rows_of(q), 1), :], value)
        return value

    def vector_row(owner, row):
        return (owner % m * n + owner // m) * VECTOR_ROWS + row

    def unpack_vectors():
        group = LANES // piece
        for j in range(width // LANES):
            at = slice(j * LANES, (j + 1) * LANES)
            natural = lambda row: joined_row(lambda q: vector_row(j * group + q, row))
            for k in range(4):
                gains[k : k + 1, at] = natural(k)
            ref.offsets[0:1, at] = natural(7) + natural(8 + size.feed_pieces)
        for target, per, row, kinds, wide in (
            (ref.joint_bias, 3, 4, 3, part),
            (ref.expand_bias, size.feed_pieces, 8, 1, hidden),
        ):
            for j in range(kinds * wide // LANES):
                kind, inner = j // (wide // LANES), j % (wide // LANES)
                first = (kind * wide * n + inner * LANES) // piece + s * (wide // piece)
                target[0:1, j * LANES : (j + 1) * LANES] = joined_row(
                    lambda q: vector_row((first + q) // per, row + (first + q) % per)
                )

    def each_tile(body):
        def load(i, slot):
            return pltpu.make_async_copy(
                ref.tokens_all.at[span(i, rows)],
                stage.at[slot, pl.ds(0, rows), pl.ds(0, width)],
                ref.x_sem.at[slot],
            )

        load(0, 0).start()

        @pl.loop(0, n)
        def _(i):
            slot = i % 2
            load(i, slot).wait()

            @pl.when(i + 1 < n)
            def _():
                load(i + 1, 1 - slot).start()

            body(i, slot)

    def normal_of(slot, at):
        value = stage[slot, at, 0:width].astype(F32)
        center = value - jnp.mean(value, axis=-1, keepdims=True)
        spread = lax.rsqrt(jnp.mean(center * center, axis=-1, keepdims=True) + 1e-05)
        return center * spread, spread

    def norm_stage(which):
        def body(i, slot):
            @pl.loop(0, rows // few)
            def _(j):
                value, _ = normal_of(slot, span(j, few))
                value = value * gains[2 * which : 2 * which + 1, :] + gains[2 * which + 1 : 2 * which + 2, :]
                normed[pl.ds(pl.multiple_of(i * rows + j * few, few), few), :] = value.astype(BF)

        each_tile(body)

    def turn(value, at, sign):
        head = value[:, :LANES]
        lane = lax.broadcasted_iota(jnp.int32, head.shape, 1)
        lower = -sign * pltpu.roll(head, LANES - ROT // 2, 1)
        upper = sign * pltpu.roll(head, ROT // 2, 1)
        head = head * tables[0, at, :] + jnp.where(lane < ROT // 2, lower, upper) * tables[1, at, :]
        if value.shape[1] == LANES:
            return head
        return jnp.concatenate([head, value[:, LANES:]], axis=1)

    def joint_stage():
        @pl.loop(0, n)
        def _(i):
            at = span(i, rows)
            joint = nn(normed[at, :], right[0:width, 0 : 3 * part]) + ref.joint_bias[...]
            for kind in range(3):
                for head in range(heads):
                    first = kind * part + head * head_size
                    value = joint[:, first : first + head_size]
                    if kind < 2:
                        value = turn(value, at, 1.0)
                    qkv[at, first : first + head_size] = value.astype(BF)

    def gate_stage():
        @pl.loop(0, n)
        def _(i):
            gate[span(i, rows), :] = nt(upstream[span(i, rows), :], dense[...]).astype(BF)

    def attend_tile(head, i):
        keys = (i + 1) * rows
        at = pl.ds(i * rows, rows)
        seen = pl.ds(0, keys)
        q_at = pl.ds(head * head_size, head_size)
        k_at = pl.ds(part + head * head_size, head_size)
        v_at = pl.ds(2 * part + head * head_size, head_size)
        query = qkv[at, q_at]
        scores = nt(query, qkv[seen, k_at]) * scale
        row = lax.broadcasted_iota(jnp.int32, (rows, keys), 0) + i * rows
        column = lax.broadcasted_iota(jnp.int32, (rows, keys), 1)
        scores = jnp.where(column <= row, scores, -1e30)
        expo = jnp.exp(scores - jnp.max(scores, axis=-1, keepdims=True))
        probs = expo / jnp.sum(expo, axis=-1, keepdims=True)
        low_probs = probs.astype(BF)
        mixed[at, q_at] = nn(low_probs, qkv[seen, v_at]).astype(BF)
        back = gate[at, q_at]
        grad_probs = nt(back, qkv[seen, v_at])
        inner = jnp.sum(probs * grad_probs, axis=-1, keepdims=True)
        grad_scores = (probs * (grad_probs - inner)).astype(BF)
        grad_query = nn(grad_scores, qkv[seen, k_at]) * scale
        grad_qkv[at, q_at] = turn(grad_query, at, -1.0).astype(BF)
        for total, extra in ((wide_one, tn(grad_scores, query)), (wide_two, tn(low_probs, back))):
            for b in range(i + 1):
                here = (slice(0, rows), slice(b * head_size, (b + 1) * head_size))
                block = extra[b * rows : (b + 1) * rows]
                total[here] = block if i == n - 1 else total[here] + block

    def attend_stage(head):
        for i in range(n - 1, -1, -1):
            attend_tile(head, i)
        for b in range(n):
            at = pl.ds(b * rows, rows)
            here = (slice(0, rows), slice(b * head_size, (b + 1) * head_size))
            k_at = pl.ds(part + head * head_size, head_size)
            v_at = pl.ds(2 * part + head * head_size, head_size)
            grad_qkv[at, k_at] = turn(wide_one[here] * scale, at, -1.0).astype(BF)
            grad_qkv[at, v_at] = wide_two[here].astype(BF)

    def weight_grad(left_of, right_of, tiles, tall, columns, places):
        def stored(b, slot):
            return [
                pltpu.make_async_copy(
                    stage.at[slot, pl.ds(first, count), pl.ds(0, columns)], target, ref.stage_sem.at[slot]
                )
                for first, count, target in places(b)
            ]

        def settled(slot):
            view = stage.at[slot, pl.ds(0, tall), pl.ds(0, columns)]
            pltpu.make_async_copy(view, view, ref.stage_sem.at[slot]).wait()

        @pl.loop(0, tiles)
        def _(b):
            slot = b % 2

            @pl.when(b >= 2)
            def _():
                settled(slot)

            stage[slot, 0:tall, 0:columns] = tn(left_of(b), right_of()).astype(BF)
            for copy in stored(b, slot):
                copy.start()

        for b in range(max(tiles - 2, 0), tiles):
            settled(b % 2)

    def columns_of(buffer, count):
        return lambda b: buffer[:, lanes(b, count)]

    def block_places(out, count):
        return lambda b: [(0, count, out.at[b // CORES, b % CORES])]

    def piece_places(out, tall):
        def places(b):
            found = []
            for q in range(tall // piece):
                g = b * (tall // piece) + q
                owner = g % m
                found.append((q * piece, piece, out.at[owner // CORES, owner % CORES, span(g // m, piece)]))
            return found

        return places

    def dense_places(tall):
        def places(b):
            found = []
            for q in range(tall // dense_rows):
                owner = b * (tall // dense_rows) + q
                found.append((q * dense_rows, dense_rows, ref.dense_sum.at[owner // CORES, owner % CORES]))
            return found

        return places

    def expand_stage(start, stop):
        @pl.loop(start, stop)
        def _(i):
            wide_one[:, 0:hidden] = nn(normed[span(i, rows), :], left[...]) + ref.expand_bias[...]

            @pl.loop(0, rows // few)
            def _(j):
                value = wide_one[span(j, few), 0:hidden]
                share = 0.5 * (1.0 + lax.erf(value * 0.7071067811865476))
                density = jnp.exp(-0.5 * value * value) * 0.3989422804014327
                at = pl.ds(pl.multiple_of(i * rows + j * few, few), few)
                act[at, :] = (value * share).astype(BF)
                slope[at, :] = (share + value * density).astype(BF)

    def shrink_stage(start, stop):
        @pl.loop(start, stop)
        def _(i):
            wide_one[:, 0:hidden] = nt(upstream[span(i, rows), :], right[0:hidden, 0:width])

            @pl.loop(0, rows // few)
            def _(j):
                at = pl.ds(pl.multiple_of(i * rows + j * few, few), few)
                grad = (wide_one[span(j, few), 0:hidden] * slope[at, :].astype(F32)).astype(BF)
                slope[at, :] = grad
                ref.expand_total[...] += eights(grad.astype(F32))

    def owner_push(item, source, near, out, i):
        k = (i - s + n) % n
        mine = out.at[span(s, rows)]

        @pl.when(k != 0)
        def _():
            remote(source, mine, ref.seq_send.at[item, k], ref.seq_recv.at[item, k], {SEQ: i}).start()

        @pl.when(k == 0)
        def _():
            local(near, mine, add_sem.at[0]).wait()

    def owner_drain(item, buffer):
        whole = buffer.at[pl.ds(0, rows)]
        for k in range(1, n):
            drains.append(
                lambda k=k: remote(
                    whole, whole, ref.seq_send.at[item, k], ref.seq_recv.at[item, k], {SEQ: (s + k) % n}
                ).wait_send()
            )

    def output_stage():
        def tile_of(slot):
            return stage.at[slot, pl.ds(0, rows), pl.ds(0, width)]

        def moved(i, slot):
            return pltpu.make_async_copy(tile_of(slot), ref.output_part.at[span(i, rows)], ref.stage_sem.at[slot])

        @pl.loop(0, n)
        def _(i):
            at, slot = span(i, rows), i % 2
            wide_one[:, 0:width] = nn(mixed[at, :], dense[...])

            @pl.when(i >= 2)
            def _():
                moved(i - 2, slot).wait()
                owner_push(4, ref.output_part.at[span(i - 2, rows)], tile_of(slot), ref.output_all, i - 2)

            total = nn(act[at, :], right[0:hidden, 0:width]) + wide_one[:, 0:width]
            stage[slot, 0:rows, 0:width] = total.astype(BF)
            moved(i, slot).start()

        for i in range(max(n - 2, 0), n):
            moved(i, i % 2).wait()
            owner_push(4, ref.output_part.at[pl.ds(i * rows, rows)], tile_of(i % 2), ref.output_all, i)
        owner_drain(4, ref.output_part)

    def eights(value):
        return jnp.sum(value.reshape(value.shape[0] // 8, 8, value.shape[1]), axis=0)

    def input_stage(i, slot):
        at = span(i, rows)
        wide_one[:, 0:width] = nt(grad_qkv[at, :], right[0:width, 0 : 3 * part])
        wide_two[...] = nt(slope[at, :], left[...])

        @pl.loop(0, rows // few)
        def _(j):
            here = span(j, few)
            normal, _ = normal_of(slot, here)
            grad_one, grad_two = wide_one[here, 0:width], wide_two[here, :]
            total = grad_one * gains[0:1, :] + grad_two * gains[2:3, :]
            normed[pl.ds(pl.multiple_of(i * rows + j * few, few), few), :] = total.astype(BF)
            ref.gain_total[0] += eights(grad_one * normal)
            ref.gain_total[1] += eights(grad_one)
            ref.gain_total[2] += eights(grad_two * normal)
            ref.gain_total[3] += eights(grad_two)

        owner_push(5, normed.at[at], normed.at[at], ref.input_all, i)

    def joint_total_stage():
        ref.joint_total[...] = jnp.zeros_like(ref.joint_total)

        @pl.loop(0, length // few)
        def _(j):
            ref.joint_total[...] += eights(grad_qkv[span(j, few), :].astype(F32))

    small = ref.small
    wide_rows = size.gain_rows

    def small_pack():
        ref.own_total[...] = jnp.zeros_like(ref.own_total)

        @pl.loop(0, rows // few)
        def _(j):
            at = pl.ds(pl.multiple_of(s * rows + j * few, few), few)
            ref.own_total[...] += eights(upstream[at, :].astype(F32))

        small[0] = jnp.zeros_like(small[0])
        for first, source, count in (
            (0, ref.gain_total.at[0], wide_rows),
            (wide_rows, ref.gain_total.at[1], wide_rows),
            (2 * wide_rows, ref.gain_total.at[2], wide_rows),
            (3 * wide_rows, ref.gain_total.at[3], wide_rows),
            (4 * wide_rows, ref.own_total, wide_rows),
            (size.joint_small, ref.joint_total, 3 * part // LANES),
            (size.expand_small, ref.expand_total, hidden // LANES),
        ):
            for j in range(count):
                value = source[:, j * LANES : (j + 1) * LANES]
                small[0, first + j : first + j + 1, :] = jnp.sum(value, axis=0, keepdims=True)

    def small_core():
        push_all(
            lambda: (
                [(small.at[0], ref.small_in.at[0])], small.at[0], ref.small_send.at[0], ref.small_recv.at[0], twin
            )
        )

    def small_line():
        arrived(small.at[0], ref.small_recv.at[0])
        small[1] = small[0] + ref.small_in[0]
        for k in range(1, line):
            push_all(
                lambda k=k: (
                    [(small.at[1], ref.small_in.at[k])],
                    small.at[1],
                    ref.small_send.at[k],
                    ref.small_recv.at[k],
                    {DP: (z + k) % line * CORES + c},
                )
            )

    def small_seq():
        total = small[1]
        for k in range(1, line):
            arrived(small.at[0], ref.small_recv.at[k])
            total = total + ref.small_in[k]
        ref.small_all[s] = total
        mine = ref.small_all.at[s]
        seq_push(9, lambda j: [(mine, mine)], mine)

    def small_last():
        seq_wait(9, small.at[0])
        total = ref.small_all[0, 0 : 5 * wide_rows, :]
        for j in range(1, n):
            total = total + ref.small_all[j, 0 : 5 * wide_rows, :]
        ref.gain_grads[...] = total
        for j in range(n):
            ref.joint_grads[j] = ref.small_all[j, size.joint_small : size.expand_small, :]
            ref.expand_grads[j] = ref.small_all[j, size.expand_small : size.expand_small + hidden // LANES, :]

    def owner_sum(buffer):
        chunk = min(size.chunk, rows)
        for q in range(rows // chunk):
            for first in range(0, n, 4):
                sources = [buffer.at[pl.ds(j * rows + q * chunk, chunk)] for j in range(first, min(first + 4, n))]

                def into(where, total):
                    at = pl.ds(pl.multiple_of(where.start + q * chunk, 16), 16)
                    wide_one[at, 0:width] = total if first == 0 else wide_one[at, 0:width] + total

                added(sources, chunk, width, into)

    def own_tokens():
        return local(
            ref.tokens_all.at[span(s, rows)], stage.at[0, pl.ds(0, rows), pl.ds(0, width)], ref.x_sem.at[0]
        )

    def finish_output():
        copy = own_tokens()
        seq_wait(4, ref.output_all.at[pl.ds(0, rows)])
        owner_sum(ref.output_all)
        copy.wait()

        @pl.loop(0, rows // few)
        def _(j):
            at = span(j, few)
            total = stage[0, at, 0:width].astype(F32) + (wide_one[at, 0:width] + ref.offsets[...])
            stage[1, at, 0:width] = total.astype(BF)

        local(stage.at[1, pl.ds(0, rows), pl.ds(0, width)], ref.output, ref.stage_sem.at[0]).wait()

    def finish_input():
        copy = own_tokens()
        seq_wait(5, ref.input_all.at[pl.ds(0, rows)])
        owner_sum(ref.input_all)
        copy.wait()

        @pl.loop(0, rows // few)
        def _(j):
            at = span(j, few)
            normal, spread = normal_of(0, at)
            grad = wide_one[at, 0:width]
            through = grad - jnp.mean(grad, axis=-1, keepdims=True)
            through = through - normal * jnp.mean(grad * normal, axis=-1, keepdims=True)
            own = upstream[pl.ds(pl.multiple_of(s * rows + j * few, few), few), :].astype(F32)
            wide_two[at, :] = own + spread * through

        local(wide_two, ref.grad_tokens, ref.stage_sem.at[0]).wait()

    def load_joint():
        return local(ref.joint_all, right.at[pl.ds(0, width), pl.ds(0, 3 * part)], ref.load_sem.at[0])

    def joint_pairs(j):
        return [
            (
                ref.joint_own.at[:, lanes(j, part, kind * width)],
                ref.joint_all.at[span(s * m + d, piece), pl.ds(kind * part, part)],
            )
            for kind in range(3)
        ]

    def expand_pairs(j):
        return [(ref.expand_own.at[:, lanes(j, hidden)], ref.expand_all.at[span(s * m + d, piece)])]

    def vector_pairs(j):
        return [(ref.vector_own, ref.vectors.at[span(d * n + s, VECTOR_ROWS)])]

    seq_push(0, joint_pairs, ref.joint_all.at[pl.ds(0, piece)])
    seq_push(8, vector_pairs, ref.vector_own)

    def room(buffer, slot, source):
        return buffer.at[slot, pl.ds(0, source.shape[0]), pl.ds(0, source.shape[1])]

    joint_held = ref.adds.at[0, pl.ds(0, piece), pl.ds(0, 3 * part)]
    moves = [
        ([(ref.dense_own, room(ref.sent, 0, ref.dense_own))], ref.dense_all.at[span(d, dense_rows)]),
        (
            [
                (src, ref.adds.at[0, pl.ds(0, piece), pl.ds(kind * part, part)])
                for kind, (src, _) in enumerate(joint_pairs(s))
            ],
            ref.joint_all.at[span(s * m + d, piece)],
        ),
        ([(ref.tokens, room(stage, 0, ref.tokens))], ref.tokens_all.at[span(s, rows)]),
        ([(expand_pairs(s)[0][0], ref.adds.at[1, pl.ds(0, piece), pl.ds(0, hidden)])], expand_pairs(s)[0][1]),
        ([(ref.shrink_own, room(stage, 1, ref.shrink_own))], ref.shrink_all.at[span(d, shrink_rows)]),
    ]
    held = [moves[0][0][0][1], joint_held, moves[2][0][0][1], moves[3][0][0][1], moves[4][0][0][1]]
    fetched = [
        [local(src, dst, ref.own_sem.at[k, q]) for q, (src, dst) in enumerate(pairs)]
        for k, (pairs, _) in enumerate(moves)
    ]
    own_vectors = [local(src, dst, ref.own_sem.at[5, 0]) for src, dst in vector_pairs(s)]
    own_upstream = local(ref.cotangent, upstream.at[span(s, rows)], ref.own_sem.at[5, 1])
    stored = []
    for k, copies in enumerate(fetched):
        for copy in copies:
            copy.wait()
        stored.append(local(held[k], moves[k][1], ref.own_sem.at[k, 0]))
    stored[0].wait()
    gather_step(dense_in, 0)
    stored[2].wait()
    spread_first(2, ref.tokens_all)
    own_vectors[0].wait()
    seq_wait(8, ref.vector_own)
    gather_step(vector_in, 0)
    stored[1].wait()
    seq_wait(0, ref.joint_all.at[pl.ds(0, piece)])
    gather_step(joint_a, 0)
    gather_step(joint_b, 0)
    seq_push(1, expand_pairs, ref.expand_all.at[pl.ds(0, piece)])
    ref.gain_total[...] = jnp.zeros_like(ref.gain_total)
    ref.expand_total[...] = jnp.zeros_like(ref.expand_total)
    stored[3].wait()
    stored[4].wait()
    own_upstream.wait()
    gather(joint_b, 1)
    gather(dense_in, 2)
    spread_second(2, ref.tokens_all)
    spread_first(3, upstream)
    gather(joint_b, 2)
    gather(vector_in, hops)
    gather_wait(vector_in)
    unpack_vectors()
    seq_wait(1, ref.expand_all.at[pl.ds(0, piece)])
    spread_wait(2, ref.tokens_all)
    gather(dense_in, hops)
    norm_stage(0)
    gather(expand_a, 0)
    spread_second(3, upstream)
    gather(expand_b, 0)
    gather_wait(dense_in, joint_a, joint_b)
    copy_one = load_joint()
    copy_two = local(ref.dense_all, dense, ref.load_sem.at[1])
    copy_one.wait()
    joint_stage()
    gather(expand_a, 1)
    spread_wait(3, upstream)
    copy_two.wait()
    gate_stage()
    gather(expand_b, 1)
    for head in range(heads):
        attend_stage(head)
    tall = min(part, size.high)
    weight_grad(columns_of(mixed, tall), lambda: upstream[...], part // tall, tall, width, dense_places(tall))
    reduce_start(dense_kind)
    gather(expand_a, 2)
    weight_grad(
        columns_of(normed, mid_rows),
        lambda: grad_qkv[...],
        m,
        mid_rows,
        3 * part,
        piece_places(ref.joint_sum, mid_rows),
    )
    reduce_start(joint_kind)
    gather(expand_b, 2)
    joint_total_stage()
    norm_stage(1)
    reduce_hop(1, dense_kind, joint_kind)
    gather(shrink_a, 0)
    reduce_hop(2, dense_kind)
    gather(shrink_b, 0)
    gather_wait(expand_a, expand_b)
    copy_one = local(ref.expand_all, left, ref.load_sem.at[0])
    reduce_hop(2, joint_kind)
    copy_one.wait()
    expand_stage(0, n // 2)
    gather(shrink_a, 1)
    expand_stage(n // 2, n)
    gather(shrink_b, 1)
    reduce_hop(3, dense_kind, joint_kind)
    weight_grad(
        columns_of(act, shrink_rows),
        lambda: upstream[...],
        m,
        shrink_rows,
        width,
        block_places(ref.shrink_sum, shrink_rows),
    )
    reduce_start(shrink_kind)
    gather(shrink_a, 2)
    for hop in range(4, hops + 1):
        reduce_hop(hop, dense_kind, joint_kind)
    reduce_hop(1, shrink_kind)
    gather(shrink_b, 2)
    finish_rows(dense_kind, ref.dense_grad)
    finish_columns(joint_kind, 6, ref.joint_done, ref.joint_grad, 3)
    gather(shrink_b, hops)
    gather_wait(shrink_a, shrink_b)
    local(ref.shrink_all, right.at[pl.ds(0, hidden), pl.ds(0, width)], ref.load_sem.at[0]).wait()
    shrink_stage(0, n)
    reduce_hop(2, shrink_kind)
    weight_grad(
        columns_of(normed, mid_rows),
        lambda: slope[...],
        m,
        mid_rows,
        hidden,
        piece_places(ref.expand_sum, mid_rows),
    )
    reduce_start(expand_kind)
    for hop in range(3, hops + 1):
        reduce_hop(hop, shrink_kind)
    reduce_hop(1, expand_kind)
    output_stage()
    copy_one = load_joint()
    reduce_hop(2, expand_kind)
    copy_one.wait()
    each_tile(input_stage)
    owner_drain(5, ref.input_all)
    small_pack()
    small_core()
    for hop in range(3, hops + 1):
        reduce_hop(hop, expand_kind)
    small_line()
    finish_rows(shrink_kind, ref.shrink_grad)
    small_seq()
    finish_output()
    finish_columns(expand_kind, 7, ref.expand_done, ref.expand_grad, 1)
    small_last()
    finish_input()
    seq_wait(6, ref.joint_done.at[pl.ds(0, piece)])
    seq_wait(7, ref.expand_done.at[pl.ds(0, piece)])
    for pending in rounds.pending:
        if pending is not None:
            pending()
    for drain in drains:
        drain()


def run_kernel(size, inputs):
    n, m, line, hops = size.n, size.m, size.line, size.hops
    rows, width, piece, part, hidden = size.rows, size.width, size.piece, size.part, size.hidden
    dense_rows, mid_rows, shrink_rows, length = size.dense_rows, size.mid_rows, size.shrink_rows, size.length
    anywhere, vmem = pl.BlockSpec(memory_space=pl.ANY), pl.BlockSpec(memory_space=pltpu.VMEM)

    def reduced(count, columns):
        shape = (count, columns)
        return ((line, CORES) + shape, BF), ((line,) + shape, BF), ((2, line) + shape, BF)

    dense, joint = reduced(dense_rows, width), reduced(mid_rows, 3 * part)
    expand, shrink = reduced(mid_rows, hidden), reduced(shrink_rows, width)
    small_outputs = dict(
        gain_grads=((5 * size.gain_rows, LANES), F32),
        joint_grads=((n, 3 * part // LANES, LANES), F32),
        expand_grads=((n, hidden // LANES, LANES), F32),
    )
    outputs = dict(
        output=((rows, width), BF),
        grad_tokens=((rows, width), F32),
        dense_grad=((dense_rows, width), F32),
        shrink_grad=((shrink_rows, width), F32),
        joint_grad=((piece, 3 * width), F32),
        expand_grad=((piece, n * hidden), F32),
        dense_all=((part, width), BF),
        joint_all=((width, 3 * part), BF),
        expand_all=((width, hidden), BF),
        shrink_all=((hidden, width), BF),
        tokens_all=((length, width), BF),
        output_all=((length, width), BF),
        input_all=((length, width), BF),
        output_part=((length, width), BF),
        joint_done=((mid_rows, 3 * part), F32),
        expand_done=((mid_rows, hidden), F32),
        dense_sum=dense[0],
        dense_core=dense[1],
        dense_chain=dense[2],
        joint_sum=joint[0],
        joint_core=joint[1],
        joint_chain=joint[2],
        expand_sum=expand[0],
        expand_core=expand[1],
        expand_chain=expand[2],
        shrink_sum=shrink[0],
        shrink_core=shrink[1],
        shrink_chain=shrink[2],
    )
    dma = pltpu.SemaphoreType.DMA
    small = (size.small, LANES)
    scratch = dict(
        upstream=pltpu.VMEM((length, width), BF),
        normed=pltpu.VMEM((length, width), BF),
        qkv=pltpu.VMEM((length, 3 * part), BF),
        gate=pltpu.VMEM((length, part), BF),
        mixed=pltpu.VMEM((length, part), BF),
        grad_qkv=pltpu.VMEM((length, 3 * part), BF),
        act=pltpu.VMEM((length, hidden), BF),
        slope=pltpu.VMEM((length, hidden), BF),
        left=pltpu.VMEM((width, hidden), BF),
        right=pltpu.VMEM((max(width, hidden), max(width, 3 * part)), BF),
        dense=pltpu.VMEM((part, width), BF),
        wide_one=pltpu.VMEM((max(rows, size.chunk), max(width, hidden)), F32),
        wide_two=pltpu.VMEM((rows, width), F32),
        stage=pltpu.VMEM((2, size.high, size.broad), BF),
        adds=pltpu.VMEM((6, size.chunk, size.broad), BF),
        sent=pltpu.VMEM((4, size.chunk, size.broad), BF),
        vectors=pltpu.VMEM((n * m * VECTOR_ROWS, LANES), F32),
        gains=pltpu.VMEM((4, width), F32),
        offsets=pltpu.VMEM((1, width), F32),
        joint_bias=pltpu.VMEM((1, 3 * part), F32),
        expand_bias=pltpu.VMEM((1, hidden), F32),
        gain_total=pltpu.VMEM((4, 8, width), F32),
        own_total=pltpu.VMEM((8, width), F32),
        joint_total=pltpu.VMEM((8, 3 * part), F32),
        expand_total=pltpu.VMEM((8, hidden), F32),
        small=pltpu.VMEM((2,) + small, F32),
        small_in=pltpu.VMEM((line,) + small, F32),
        small_all=pltpu.VMEM((n,) + small, F32),
        seq_send=dma((10, max(n, 4))),
        seq_recv=dma((10, max(n, 4))),
        ag_send=dma((8, 2, hops)),
        ag_recv=dma((8, 2, hops)),
        swap_send=dma((8, line)),
        swap_recv=dma((8, line)),
        core_send=dma((7,)),
        core_recv=dma((7,)),
        rs_send=dma((7, 2, hops)),
        rs_recv=dma((7, 2, hops)),
        small_send=dma((line,)),
        small_recv=dma((line,)),
        add_sem=dma((6,)),
        stage_sem=dma((2,)),
        load_sem=dma((2,)),
        own_sem=dma((6, 3)),
        x_sem=dma((2,)),
    )
    names = list(inputs) + list(outputs) + list(small_outputs) + list(scratch)
    results = pl.pallas_call(
        functools.partial(kernel, size, names),
        out_shape=[
            jax.ShapeDtypeStruct(shape, kind)
            for shape, kind in list(outputs.values()) + list(small_outputs.values())
        ],
        in_specs=[vmem if name == next(reversed(inputs)) else anywhere for name in inputs],
        out_specs=[anywhere] * len(outputs) + [vmem] * len(small_outputs),
        scratch_shapes=list(scratch.values()),
        compiler_params=pltpu.CompilerParams(
            collective_id=0, has_side_effects=True, vmem_limit_bytes=64 * 2**20 - 2**17
        ),
        name="block",
    )(*inputs.values())
    return types.SimpleNamespace(**dict(zip(list(outputs) + list(small_outputs), results)))


def block_plan(n, m, tokens, cotangent, shards):
    (
        first_gain,
        first_shift,
        second_gain,
        second_shift,
        joint_weight,
        joint_bias,
        dense_weight,
        dense_bias,
        expand_weight,
        expand_bias,
        shrink_weight,
        shrink_bias,
    ) = shards
    rows, width = tokens.shape[1:]
    size = sizes_of(n, m, rows, width, expand_weight.shape[1])
    piece, devices = size.piece, n * m
    vectors = jnp.concatenate(
        [
            first_gain,
            first_shift,
            second_gain,
            second_shift,
            joint_bias,
            dense_bias,
            expand_bias,
            shrink_bias,
        ]
    )
    vectors = vectors.astype(F32).reshape(-1, 1, piece)
    vectors = jnp.broadcast_to(vectors, (vectors.shape[0], LANES // piece, piece)).reshape(-1, LANES)
    vectors = jnp.pad(vectors, ((0, VECTOR_ROWS - vectors.shape[0]), (0, 0)))
    got = run_kernel(
        size,
        dict(
            tokens=tokens[0],
            cotangent=cotangent[0],
            joint_own=joint_weight,
            expand_own=expand_weight,
            dense_own=dense_weight,
            shrink_own=shrink_weight,
            vector_own=vectors,
            tables=turn_tables(size.length),
        ),
    )
    index = lax.axis_index(SEQ) * m + lax.axis_index(DP)

    def own(values):
        return lax.dynamic_index_in_dim(values.reshape(devices, -1), index, 0, keepdims=False)

    gains = lax.dynamic_slice_in_dim(got.gain_grads.reshape(5, width), index * piece, piece, 1)
    joint_grads = jnp.swapaxes(got.joint_grads.reshape(n, 3, size.part), 0, 1)
    return (
        got.output[None],
        got.grad_tokens[None],
        gains[0],
        gains[1],
        gains[2],
        gains[3],
        got.joint_grad,
        own(joint_grads),
        got.dense_grad,
        gains[4],
        got.expand_grad,
        own(got.expand_grads),
        got.shrink_grad,
        gains[4],
    )


def solution(mesh):
    n, m = mesh.shape[SEQ], mesh.shape[DP]

    def body(tokens, cotangent, *shards):
        return block_plan(n, m, tokens, cotangent, shards)

    both = (SEQ, DP)
    tokens = P(DP, SEQ, None)
    vector, matrix = P(both), P(both, None)
    return jax.shard_map(
        body,
        mesh=mesh,
        in_specs=(tokens, tokens) + (vector,) * 4 + (matrix, vector) * 4,
        out_specs=(tokens, tokens) + (vector,) * 4 + (matrix, vector) * 4,
        check_vma=False,
    )
```

```python
import functools
import types

import jax
import jax.numpy as jnp
from jax import lax
from jax.experimental import pallas as pl
from jax.experimental.pallas import tpu as pltpu
from jax.sharding import PartitionSpec as P

HEADS = 8
ROT = 64
CORES = 2
LANES = 128
VECTOR_ROWS = 16
STEP = 64
SEQ, DP = "seq", "dp"
BF = jnp.bfloat16
F32 = jnp.float32
MESH = pl.DeviceIdType.MESH


def nn(left, right):
    return jnp.dot(left, right, preferred_element_type=F32)


def nt(left, right):
    return lax.dot_general(left, right, (((1,), (1,)), ((), ())), preferred_element_type=F32)


def tn(left, right):
    return lax.dot_general(left, right, (((0,), (0,)), ((), ())), preferred_element_type=F32)


def turn_tables(length):
    inverse = 10000.0 ** (-jnp.arange(0, ROT, 2, dtype=F32) / ROT)
    angle = jnp.arange(length, dtype=F32)[:, None] * inverse[None, :]
    cosine, sine = jnp.cos(angle), jnp.sin(angle)
    rest = jnp.zeros((length, LANES - ROT), F32)
    return jnp.stack(
        [
            jnp.concatenate([cosine, cosine, rest + 1.0], axis=1),
            jnp.concatenate([sine, sine, rest], axis=1),
        ]
    )


def sizes_of(n, m, rows, width, feed):
    devices = n * m
    z = types.SimpleNamespace(n=n, m=m, rows=rows, width=width)
    z.line, z.hops = m // CORES, m // CORES - 1
    z.length = rows * n
    z.piece = width // devices
    z.part = width // n
    z.hidden = feed // n
    z.heads, z.head_size = HEADS // n, width // HEADS
    z.dense_rows, z.mid_rows, z.shrink_rows = z.part // m, width // m, z.hidden // m
    z.feed_pieces = feed // width
    z.split = 2 if z.shrink_rows % (2 * LANES) == 0 else 1
    z.share = z.shrink_rows // z.split
    z.units = z.hidden // z.split
    z.units_tall = min(z.units, max(z.share, 2 * LANES))
    z.high = max(rows, z.mid_rows, z.shrink_rows)
    z.broad = max(width, z.hidden, 3 * z.part)
    z.chunk = max(z.mid_rows // 2, z.shrink_rows // 4)
    z.gain_rows = width // LANES
    z.joint_small = 5 * z.gain_rows
    z.expand_small = z.joint_small + 3 * z.part // LANES
    z.small = -(-(z.expand_small + z.hidden // LANES) // 8) * 8
    return z


def kernel(size, names, *refs):
    ref = types.SimpleNamespace(**dict(zip(names, refs)))
    n, m, line, hops = size.n, size.m, size.line, size.hops
    rows, width, piece, part, hidden = size.rows, size.width, size.piece, size.part, size.hidden
    heads, head_size, length = size.heads, size.head_size, size.length
    dense_rows, mid_rows, shrink_rows = size.dense_rows, size.mid_rows, size.shrink_rows
    split, share, units = size.split, size.share, size.units
    scale = head_size ** (-0.5)
    s, d = lax.axis_index(SEQ), lax.axis_index(DP)
    z, c = d // CORES, d % CORES
    twin = {DP: z * CORES + 1 - c}
    above, below = {DP: d + CORES}, {DP: d - CORES}
    drains = []

    def remote(src, dst, send, recv, device):
        return pltpu.make_async_remote_copy(
            src_ref=src, dst_ref=dst, send_sem=send, recv_sem=recv, device_id=device, device_id_type=MESH
        )

    def push_all(make, when=None, keep=True):
        def start():
            pairs, _, send, recv, device = make()
            for src, dst in pairs:
                remote(src, dst, send, recv, device).start()

        def settle():
            _, whole, send, recv, device = make()
            remote(whole, whole, send, recv, device).wait_send()

        def guarded(step):
            return step if when is None else lambda: pl.when(when())(step)

        guarded(start)()
        if keep:
            drains.append(guarded(settle))
        return guarded(settle)

    def arrived(whole, recv):
        remote(whole, whole, recv, recv, twin).wait_recv()

    def local(src, dst, sem):
        copy = pltpu.make_async_copy(src, dst, sem)
        copy.start()
        return copy

    def span(index, size, count=None, offset=0):
        count = size if count is None else count
        return pl.ds(pl.multiple_of(index * size + offset, count), count)

    def lanes(index, size, offset=0):
        return pl.ds(pl.multiple_of(index * size + offset, LANES), size)

    barrier = pltpu.get_barrier_semaphore()
    greeted = [{SEQ: (s + k) % n} for k in range(1, n)]
    greeted += [{DP: (z + k) % line * CORES + c} for k in range(1, line)] + [twin]
    for device in greeted:
        pl.semaphore_signal(barrier, inc=1, device_id=device, device_id_type=MESH)
    pl.semaphore_wait(barrier, len(greeted))

    def seq_push(item, pairs_of, whole):
        for k in range(1, n):
            j = (s + k) % n
            push_all(
                lambda j=j, k=k: (
                    pairs_of(j), whole, ref.seq_send.at[item, k], ref.seq_recv.at[item, k], {SEQ: j}
                )
            )

    def seq_wait(item, whole):
        for k in range(1, n):
            arrived(whole, ref.seq_recv.at[item, k])

    square = n == 4
    beside, across = s + 1 - 2 * (s % 2), (s + 2) % n

    def spread_first(item, buffer, tall=rows):
        mine = buffer.at[span(s, tall)]
        if not square:
            seq_push(item, lambda j: [(mine, mine)], mine)
            return
        for way, target in ((0, beside), (1, across)):
            push_all(
                lambda way=way, target=target: (
                    [(mine, mine)], mine, ref.seq_send.at[item, way], ref.seq_recv.at[item, way], {SEQ: target}
                )
            )

    def spread_second(item, buffer, tall=rows):
        if not square:
            return
        for way, source, target in ((0, beside, across), (1, across, beside)):
            arrived(buffer.at[span(source, tall)], ref.seq_recv.at[item, way])
            half = buffer.at[span(source, tall, tall // 2, way * (tall // 2))]
            push_all(
                lambda way=2 + way, target=target, half=half: (
                    [(half, half)], half, ref.seq_send.at[item, way], ref.seq_recv.at[item, way], {SEQ: target}
                )
            )

    def spread_wait(item, buffer, tall=rows):
        if not square:
            seq_wait(item, buffer.at[pl.ds(0, tall)])
            return
        for way in range(2):
            arrived(buffer.at[pl.ds(0, tall // 2)], ref.seq_recv.at[item, 2 + way])

    def chain_of(number, buffer, runs, count):
        def views(owner):
            return [buffer.at[span(run(owner), count)] for run in runs]

        whole = buffer.at[pl.ds(0, count * len(runs))]
        return types.SimpleNamespace(number=number, views=views, whole=whole)

    def piece_runs(first, last):
        return [lambda owner, j=j: j * m + owner for j in range(first, last)]

    shrink_in = [chain_of(u, ref.shrink_all.at[u], [lambda owner: owner], share) for u in range(split)]
    expand_in = [chain_of(2 + u, ref.expand_all.at[u], piece_runs(0, n), piece) for u in range(split)]
    dense_in = chain_of(4, ref.dense_all, [lambda owner: s * m + owner], dense_rows)
    joint_a = chain_of(5, ref.joint_all, piece_runs(0, n // 2), piece)
    joint_b = chain_of(6, ref.joint_all, piece_runs(n // 2, n), piece)
    vector_in = chain_of(7, ref.vectors, [lambda owner: owner], n * VECTOR_ROWS)

    def vector_send():
        for k in range(1, line):
            view = ref.vectors.at[span(d, n * VECTOR_ROWS)]
            push_all(
                lambda k=k, view=view: (
                    [(view, view)],
                    view,
                    ref.vector_out.at[k],
                    ref.vector_back.at[k],
                    {DP: (z + k) % line * CORES + c},
                )
            )

    def vector_swap():
        for k in range(1, line):
            arrived(vector_in.whole, ref.vector_back.at[k])
        for k in range(line):
            view = ref.vectors.at[span(k * CORES + c, n * VECTOR_ROWS)]
            push_all(
                lambda k=k, view=view: (
                    [(view, view)], view, ref.swap_send.at[7, k], ref.swap_recv.at[7, k], twin
                )
            )


    def gather_step(chain, hop):
        number = chain.number

        def views(owner):
            return [(view, view) for view in chain.views(owner() * CORES + c)]

        def swap(owner, when=None):
            push_all(
                lambda: (
                    views(owner),
                    chain.whole,
                    ref.swap_send.at[number, owner()],
                    ref.swap_recv.at[number, owner()],
                    twin,
                ),
                when,
            )

        def forward(side, owner, when):
            push_all(
                lambda: (
                    views(owner),
                    chain.whole,
                    ref.ag_send.at[number, side, hop],
                    ref.ag_recv.at[number, side, hop],
                    below if side else above,
                ),
                when,
            )

        if hop > hops:
            return
        if hop == 0:
            forward(0, lambda: z, lambda: z < line - 1)
            forward(1, lambda: z, lambda: z > 0)
            swap(lambda: z)
            return
        for side, owner, valid, more in (
            (0, lambda: (z - hop + line) % line, lambda: z >= hop, lambda: z < line - 1),
            (1, lambda: (z + hop) % line, lambda: z + hop < line, lambda: z > 0),
        ):
            pl.when(valid())(functools.partial(arrived, chain.whole, ref.ag_recv.at[number, side, hop - 1]))
            if hop < hops:
                forward(side, owner, lambda valid=valid, more=more: valid() & more())
            swap(owner, valid)

    def gather_wait(*chains):
        for chain in chains:
            for owner in range(line):
                arrived(chain.whole, ref.swap_recv.at[chain.number, owner])

    def gather_rest(*chains):
        for hop in range(4, hops + 1):
            for chain in chains:
                gather_step(chain, hop)

    def kind_of(first, total, core, chain, halves, count, columns, together=True):
        return types.SimpleNamespace(
            first=first,
            total=total,
            core=core,
            chain=chain,
            halves=halves,
            count=count,
            columns=columns,
            together=together,
        )

    mid, low = mid_rows // 2, share // 2
    dense_kind = kind_of(0, ref.dense_sum, ref.dense_core, ref.dense_chain, 1, dense_rows, width)
    joint_kind = kind_of(1, ref.joint_sum, ref.joint_core, ref.joint_chain, 2, mid, 3 * part, False)
    expand_kind = [
        kind_of(3 + 2 * u, ref.expand_sum.at[u], ref.expand_core.at[u], ref.expand_chain.at[u], 2, mid, units)
        for u in range(split)
    ]
    shrink_kind = [
        kind_of(7 + 2 * u, ref.shrink_sum.at[u], ref.shrink_core.at[u], ref.shrink_chain.at[u], 2, low, width)
        for u in range(split)
    ]
    adds, add_sem, sent = ref.adds, ref.add_sem, ref.sent
    rounds = types.SimpleNamespace(ring=0, pending=[None, None])

    def reduce_start(kind):
        for half in range(kind.halves):
            at = pl.ds(half * kind.count, kind.count)
            push_all(
                lambda at=at, half=half: (
                    [(kind.total.at[:, 1 - c, at], kind.core.at[:, at])],
                    kind.core.at[:, at],
                    ref.core_send.at[kind.first + half],
                    ref.core_recv.at[kind.first + half],
                    twin,
                )
            )

    def summed(slots, count, columns, into):
        step = min(count, STEP)

        @pl.loop(0, count // step)
        def _(i):
            at = span(i, step)
            total = adds[slots[0], at, 0:columns].astype(F32)
            for slot in slots[1:]:
                total = total + adds[slot, at, 0:columns].astype(F32)
            into(at, total)

    def added(sources, count, columns, into):
        copies = []
        for slot, source in enumerate(sources):
            copies.append(local(source, adds.at[slot, pl.ds(0, count), pl.ds(0, columns)], add_sem.at[slot]))
        for copy in copies:
            copy.wait()
        summed(range(len(sources)), count, columns, into)

    def add_slot(kind, slot):
        return adds.at[slot, pl.ds(0, kind.count), pl.ds(0, kind.columns)]

    def add_load(kind, source, slot):
        return pltpu.make_async_copy(source, add_slot(kind, slot), add_sem.at[slot])

    def blank(kind, slot):
        adds[slot, 0 : kind.count, 0 : kind.columns] = jnp.zeros((kind.count, kind.columns), BF)

    def reduce_round(kind, hop, side, valid):
        count, columns = kind.count, kind.columns
        ring = rounds.ring
        rounds.ring = 1 - ring
        if rounds.pending[ring] is not None:
            rounds.pending[ring]()
        target = lambda: (z + (line - hop) * (1 - 2 * side()) + line) % line
        joined = lambda: z + side() * (line - 1 - 2 * z) > 0
        device = lambda: {DP: d + CORES * (1 - 2 * side())}

        def at(half):
            return span(half, count)

        @pl.when(valid())
        def _():
            @pl.loop(0, kind.halves)
            def _(half):
                add_load(kind, kind.total.at[target(), c, at(half)], half * 3).start()
                add_load(kind, kind.core.at[target(), at(half)], half * 3 + 1).start()

            def behind_of(half):
                return kind.chain.at[side(), target(), at(half)]

            def await_behind(half):
                if hop > 1:

                    @pl.when(joined())
                    def _():
                        arrived(behind_of(half), ref.rs_recv.at[kind.first + half, side(), hop - 2])
                        add_load(kind, behind_of(half), half * 3 + 2).start()

                    @pl.when(jnp.logical_not(joined()))
                    def _():
                        blank(kind, half * 3 + 2)

            def send(half):
                add_load(kind, kind.total.at[target(), c, at(half)], half * 3).wait()
                add_load(kind, kind.core.at[target(), at(half)], half * 3 + 1).wait()
                slots = [half * 3, half * 3 + 1]
                if hop > 1:
                    pl.when(joined())(lambda: add_load(kind, behind_of(half), half * 3 + 2).wait())
                    slots.append(half * 3 + 2)

                def keep(where, total):
                    sent[ring * 2 + half, where, 0:columns] = total.astype(BF)

                summed(slots, count, columns, keep)
                remote(
                    sent.at[ring * 2 + half, pl.ds(0, count), pl.ds(0, columns)],
                    behind_of(half),
                    ref.rs_send.at[kind.first + half, side(), hop - 1],
                    ref.rs_recv.at[kind.first + half, side(), hop - 1],
                    device(),
                ).start()

            if kind.together:
                pl.loop(0, kind.halves)(await_behind)
                pl.loop(0, kind.halves)(send)
            else:

                @pl.loop(0, kind.halves)
                def _(half):
                    await_behind(half)
                    send(half)

        def settle():
            @pl.when(valid())
            def _():
                view = sent.at[0, pl.ds(0, count), pl.ds(0, columns)]
                for half in range(kind.halves):
                    remote(
                        view,
                        view,
                        ref.rs_send.at[kind.first + half, side(), hop - 1],
                        ref.rs_recv.at[kind.first + half, side(), hop - 1],
                        device(),
                    ).wait_send()

        rounds.pending[ring] = settle

    def reduce_hop(hop, *kinds):
        if hop > hops:
            return
        for kind in kinds:
            if hop == 1:
                for half in range(kind.halves):
                    arrived(
                        kind.core.at[:, pl.ds(half * kind.count, kind.count)], ref.core_recv.at[kind.first + half]
                    )
            if 2 * hop <= line:
                reduce_round(kind, hop, lambda: z * 2 // line, lambda: (z < hop) | (z >= line - hop))
            else:
                reduce_round(kind, hop, lambda: 0, lambda: z < hop)
                reduce_round(kind, hop, lambda: 1, lambda: z >= line - hop)

    def reduce_last(kind):
        def sources(half):
            at = span(half, kind.count)
            return kind.total.at[z, c, at], kind.core.at[z, at], kind.chain.at[0, z, at], kind.chain.at[1, z, at]

        ends = ((0, lambda: z > 0), (1, lambda: z < line - 1))

        @pl.loop(0, kind.halves)
        def _(half):
            for slot in range(2):
                add_load(kind, sources(half)[slot], half * 4 + slot).start()
            for side, there in ends:

                @pl.when(there())
                def _():
                    arrived(sources(half)[2 + side], ref.rs_recv.at[kind.first + half, side, hops - 1])
                    add_load(kind, sources(half)[2 + side], half * 4 + 2 + side).start()

                @pl.when(jnp.logical_not(there()))
                def _():
                    blank(kind, half * 4 + 2 + side)

        @pl.loop(0, kind.halves)
        def _(half):
            for slot in range(2):
                add_load(kind, sources(half)[slot], half * 4 + slot).wait()
            for side, there in ends:
                pl.when(there())(lambda: add_load(kind, sources(half)[2 + side], half * 4 + 2 + side).wait())

            def keep(where, total):
                at = pl.ds(pl.multiple_of(half * kind.count + where.start, 16), where.size)
                ref.wide_one[at, 0 : kind.columns] = total

            summed([half * 4 + slot for slot in range(4)], kind.count, kind.columns, keep)

    def finish_rows(kind, out, first=0):
        reduce_last(kind)
        tall = kind.halves * kind.count
        local(ref.wide_one.at[pl.ds(0, tall), pl.ds(0, kind.columns)], out.at[pl.ds(first, tall)], add_sem.at[0]).wait()

    def finish_columns(kind, item, done, out, columns):
        whole = done.at[pl.ds(0, piece)]

        def pairs(j):
            return [
                (done.at[span(j, piece), pl.ds(first, count)], out.at[:, pl.ds(pl.multiple_of(to, LANES), count)])
                for first, to, count in columns
            ]

        def sems(j):
            k = (j - s + n) % n
            return ref.seq_send.at[item, k], ref.seq_recv.at[item, k], {SEQ: j}

        reduce_last(kind)
        tall = kind.halves * kind.count
        local(ref.wide_one.at[pl.ds(0, tall), pl.ds(0, kind.columns)], done.at[pl.ds(0, tall)], add_sem.at[0]).wait()

        @pl.loop(0, n)
        def _(j):
            @pl.when(j != s)
            def _():
                for src, dst in pairs(j):
                    remote(src, dst, *sems(j)).start()

            @pl.when(j == s)
            def _():
                for (first, _, count), (_, dst) in zip(columns, pairs(j)):
                    local(ref.wide_one.at[span(j, piece), pl.ds(first, count)], dst, add_sem.at[0])
                pltpu.make_async_copy(whole, whole, add_sem.at[0]).wait()

        for k in range(1, n):
            drains.append(lambda k=k: remote(whole, whole, *sems((s + k) % n)).wait_send())

    upstream, normed, qkv = ref.upstream, ref.normed, ref.qkv
    gate, mixed, grad_qkv = ref.gate, ref.gate, ref.qkv
    act, slope = ref.act, ref.slope
    left, right = ref.left, ref.right
    wide_one, wide_two = ref.wide_one, ref.wide_two
    stage, gains, tables = ref.stage, ref.gains, ref.tables
    few = 128

    def joined_row(rows_of):
        lane = lax.broadcasted_iota(jnp.int32, (1, LANES), 1)
        value = ref.vectors[pl.ds(rows_of(0), 1), :]
        for q in range(1, LANES // piece):
            value = jnp.where(lane >= q * piece, ref.vectors[pl.ds(rows_of(q), 1), :], value)
        return value

    def vector_row(owner, row):
        return (owner % m * n + owner // m) * VECTOR_ROWS + row

    def unpack_vectors():
        group = LANES // piece
        for j in range(width // LANES):
            at = slice(j * LANES, (j + 1) * LANES)
            natural = lambda row: joined_row(lambda q: vector_row(j * group + q, row))
            for k in range(4):
                gains[k : k + 1, at] = natural(k)
            ref.offsets[0:1, at] = natural(7) + natural(8 + size.feed_pieces)
        for target, per, row, kinds, wide in (
            (ref.joint_bias, 3, 4, 3, part),
            (ref.expand_bias, size.feed_pieces, 8, 1, hidden),
        ):
            for j in range(kinds * wide // LANES):
                kind, inner = j // (wide // LANES), j % (wide // LANES)
                if kinds == 1 and split > 1:
                    owner, within = inner // (share // LANES) % m, inner % (share // LANES)
                    inner = (owner * split + inner // (units // LANES)) * (share // LANES) + within
                first = (kind * wide * n + inner * LANES) // piece + s * (wide // piece)
                target[0:1, j * LANES : (j + 1) * LANES] = joined_row(
                    lambda q: vector_row((first + q) // per, row + (first + q) % per)
                )

    def each_tile(body):
        def load(i, slot):
            return pltpu.make_async_copy(
                ref.tokens_all.at[span(i, rows)],
                stage.at[slot, pl.ds(0, rows), pl.ds(0, width)],
                ref.x_sem.at[slot],
            )

        load(0, 0).start()

        @pl.loop(0, n)
        def _(i):
            slot = i % 2
            load(i, slot).wait()

            @pl.when(i + 1 < n)
            def _():
                load(i + 1, 1 - slot).start()

            body(i, slot)

    def normal_of(slot, at):
        value = stage[slot, at, 0:width].astype(F32)
        center = value - jnp.mean(value, axis=-1, keepdims=True)
        spread = lax.rsqrt(jnp.mean(center * center, axis=-1, keepdims=True) + 1e-05)
        return center * spread, spread

    def norm_stage(which):
        def body(i, slot):
            @pl.loop(0, rows // few)
            def _(j):
                value, _ = normal_of(slot, span(j, few))
                value = value * gains[2 * which : 2 * which + 1, :] + gains[2 * which + 1 : 2 * which + 2, :]
                normed[pl.ds(pl.multiple_of(i * rows + j * few, few), few), :] = value.astype(BF)

        each_tile(body)

    def turn(value, at, sign):
        head = value[:, :LANES]
        lane = lax.broadcasted_iota(jnp.int32, head.shape, 1)
        lower = -sign * pltpu.roll(head, LANES - ROT // 2, 1)
        upper = sign * pltpu.roll(head, ROT // 2, 1)
        head = head * tables[0, at, :] + jnp.where(lane < ROT // 2, lower, upper) * tables[1, at, :]
        if value.shape[1] == LANES:
            return head
        return jnp.concatenate([head, value[:, LANES:]], axis=1)

    def joint_stage():
        @pl.loop(0, n)
        def _(i):
            at = span(i, rows)
            joint = nn(normed[at, :], left[:, 0 : 3 * part]) + ref.joint_bias[...]
            for kind in range(3):
                for head in range(heads):
                    first = kind * part + head * head_size
                    value = joint[:, first : first + head_size]
                    if kind < 2:
                        value = turn(value, at, 1.0)
                    qkv[at, first : first + head_size] = value.astype(BF)

    gate_tall = min(part, size.high)

    def load_dense():
        return [
            local(
                ref.dense_all.at[span(s, part, gate_tall, first)],
                stage.at[k, pl.ds(0, gate_tall), pl.ds(0, width)],
                ref.load_sem.at[1 + k],
            )
            for k, first in enumerate(range(0, part, gate_tall))
        ]

    def gate_stage(copies):
        for copy in copies:
            copy.wait()

        @pl.loop(0, n)
        def _(i):
            for k in range(part // gate_tall):
                weight = stage[k, 0:gate_tall, 0:width]
                gate[span(i, rows), k * gate_tall : (k + 1) * gate_tall] = nt(upstream[span(i, rows), :], weight).astype(BF)

    queries = max(rows * min(1024, length) // length, 16)

    def attend_tile(head, i, sub):
        keys = (i + 1) * rows
        first = i * rows + sub * queries
        at = pl.ds(first, queries)
        seen = pl.ds(0, keys)
        q_at = pl.ds(head * head_size, head_size)
        k_at = pl.ds(part + head * head_size, head_size)
        v_at = pl.ds(2 * part + head * head_size, head_size)
        query, back = qkv[at, q_at], gate[at, q_at]
        scores = nt(query, qkv[seen, k_at]) * scale
        row = lax.broadcasted_iota(jnp.int32, (queries, keys), 0) + first
        column = lax.broadcasted_iota(jnp.int32, (queries, keys), 1)
        scores = jnp.where(column <= row, scores, -1e30)
        expo = jnp.exp(scores - jnp.max(scores, axis=-1, keepdims=True))
        probs = expo / jnp.sum(expo, axis=-1, keepdims=True)
        low_probs = probs.astype(BF)
        mixed[at, q_at] = nn(low_probs, qkv[seen, v_at]).astype(BF)
        grad_probs = nt(back, qkv[seen, v_at])
        inner = jnp.sum(probs * grad_probs, axis=-1, keepdims=True)
        grad_scores = (probs * (grad_probs - inner)).astype(BF)
        grad_query = nn(grad_scores, qkv[seen, k_at]) * scale
        grad_qkv[at, q_at] = turn(grad_query, at, -1.0).astype(BF)
        for total, extra in ((wide_one, tn(grad_scores, query)), (wide_two, tn(low_probs, back))):
            for b in range(i + 1):
                here = (slice(0, rows), slice(b * head_size, (b + 1) * head_size))
                block = extra[b * rows : (b + 1) * rows]
                total[here] = block if i == n - 1 and sub == 0 else total[here] + block

    def attend_stage(head):
        for i in range(n - 1, -1, -1):
            for sub in range(rows // queries):
                attend_tile(head, i, sub)
        for b in range(n):
            at = pl.ds(b * rows, rows)
            here = (slice(0, rows), slice(b * head_size, (b + 1) * head_size))
            k_at = pl.ds(part + head * head_size, head_size)
            v_at = pl.ds(2 * part + head * head_size, head_size)
            grad_qkv[at, k_at] = turn(wide_one[here] * scale, at, -1.0).astype(BF)
            grad_qkv[at, v_at] = wide_two[here].astype(BF)

    def weight_grad(left_of, right_of, tiles, tall, columns, places):
        def stored(b, slot):
            return [
                pltpu.make_async_copy(
                    stage.at[slot, pl.ds(first, count), pl.ds(0, columns)], target, ref.stage_sem.at[slot]
                )
                for first, count, target in places(b)
            ]

        def settled(slot):
            view = stage.at[slot, pl.ds(0, tall), pl.ds(0, columns)]
            pltpu.make_async_copy(view, view, ref.stage_sem.at[slot]).wait()

        @pl.loop(0, tiles)
        def _(b):
            slot = b % 2

            @pl.when(b >= 2)
            def _():
                settled(slot)

            stage[slot, 0:tall, 0:columns] = tn(left_of(b), right_of()).astype(BF)
            for copy in stored(b, slot):
                copy.start()

        for b in range(max(tiles - 2, 0), tiles):
            settled(b % 2)

    def columns_of(buffer, count):
        return lambda b: buffer[:, lanes(b, count)]

    def owner_places(out, tall, each):
        def places(b):
            found = []
            for q in range(tall // each):
                owner = b * (tall // each) + q
                found.append((q * each, each, out.at[owner // CORES, owner % CORES]))
            return found

        return places

    def piece_places(out, tall):
        def places(b):
            found = []
            for q in range(tall // piece):
                g = b * (tall // piece) + q
                owner = g % m
                found.append((q * piece, piece, out.at[owner // CORES, owner % CORES, span(g // m, piece)]))
            return found

        return places

    def group(u):
        return slice(u * units, (u + 1) * units)

    def expand_stage(u):
        @pl.loop(0, n)
        def _(i):
            wide_one[:, 0:units] = nn(normed[span(i, rows), :], left[:, group(u)]) + ref.expand_bias[:, group(u)]

            @pl.loop(0, rows // few)
            def _(j):
                value = wide_one[span(j, few), 0:units]
                area = 0.5 * (1.0 + lax.erf(value * 0.7071067811865476))
                density = jnp.exp(-0.5 * value * value) * 0.3989422804014327
                at = pl.ds(pl.multiple_of(i * rows + j * few, few), few)
                act[at, group(u)] = (value * area).astype(BF)
                slope[at, group(u)] = (area + value * density).astype(BF)

    def shrink_stage(u):
        @pl.loop(0, n)
        def _(i):
            wide_one[:, 0:units] = nt(upstream[span(i, rows), :], right[group(u), :])

            @pl.loop(0, rows // few)
            def _(j):
                at = pl.ds(pl.multiple_of(i * rows + j * few, few), few)
                grad = (wide_one[span(j, few), 0:units] * slope[at, group(u)].astype(F32)).astype(BF)
                slope[at, group(u)] = grad
                ref.expand_total[:, group(u)] += eights(grad.astype(F32))

    def eights(value):
        return jnp.sum(value.reshape(value.shape[0] // 8, 8, value.shape[1]), axis=0)

    outs, out_sem = ref.outs, ref.out_sem

    def tiles_to_owners(item, made, received):
        mine = received.at[span(s, rows)]

        def moved(i, slot):
            return pltpu.make_async_copy(outs.at[slot], made.at[span(i, rows)], out_sem.at[slot])

        def direct(i, k):
            return remote(
                made.at[span(i, rows)], mine, ref.seq_send.at[item, k], ref.seq_recv.at[item, k], {SEQ: i}
            )

        def give(i, slot):
            k = (i - s + n) % n

            @pl.when(k == 0)
            def _():
                local(outs.at[slot], mine, add_sem.at[0]).wait()

            @pl.when(k != 0)
            def _():
                direct(i, k).start()

        def ready(i, slot):
            @pl.when(i >= 2)
            def _():
                moved(i - 2, slot).wait()
                give(i - 2, slot)

        def filled(i, slot):
            moved(i, slot).start()

        def flush():
            for i in range(max(n - 2, 0), n):
                moved(i, i % 2).wait()
                give(i, i % 2)
            for k in range(1, n):
                drains.append(lambda k=k: direct((s + k) % n, k).wait_send())

        def wait():
            seq_wait(item, received.at[pl.ds(0, rows)])

        return types.SimpleNamespace(ready=ready, filled=filled, flush=flush, wait=wait)

    output_tiles = tiles_to_owners(4, ref.output_part, ref.output_all)
    input_tiles = tiles_to_owners(5, ref.input_part, ref.input_all)

    def kept(array):
        load = lambda i, slot: pltpu.make_async_copy(array.at[span(i, rows)], outs.at[slot], ref.keep_sem.at[slot])
        store = lambda i, slot: pltpu.make_async_copy(outs.at[slot], array.at[span(i, rows)], ref.keep_sem.at[slot])
        return load, store

    input_load, input_store = kept(ref.input_kept)

    def output_stage():
        @pl.loop(0, n)
        def _(i):
            slot = i % 2
            output_tiles.ready(i, slot)
            outs[slot] = nn(act[span(i, rows), :], right[0:hidden, :]).astype(BF)
            output_tiles.filled(i, slot)

        output_tiles.flush()

    def gain_sums(which, grad, normal):
        ref.gain_total[2 * which] += eights(grad * normal)
        ref.gain_total[2 * which + 1] += eights(grad)

    def input_feed_stage(i, slot):
        wide_two[...] = nt(slope[span(i, rows), :], left[:, 0:hidden])
        pl.when(i >= 2)(lambda: input_store(i - 2, slot).wait())

        @pl.loop(0, rows // few)
        def _(j):
            at = span(j, few)
            normal, _ = normal_of(slot, at)
            grad = wide_two[at, :]
            outs[slot, at, :] = (grad * gains[2:3, :]).astype(BF)
            gain_sums(1, grad, normal)

        input_store(i, slot).start()

    def input_feed_flush():
        for i in range(max(n - 2, 0), n):
            input_store(i, i % 2).wait()

    def input_stage(i, slot):
        input_tiles.ready(i, slot)
        input_load(i, slot).start()
        wide_one[:, 0:width] = nt(grad_qkv[span(i, rows), :], left[:, 0 : 3 * part])
        input_load(i, slot).wait()

        @pl.loop(0, rows // few)
        def _(j):
            at = span(j, few)
            normal, _ = normal_of(slot, at)
            grad = wide_one[at, 0:width]
            outs[slot, at, :] = (outs[slot, at, :].astype(F32) + grad * gains[0:1, :]).astype(BF)
            gain_sums(0, grad, normal)

        input_tiles.filled(i, slot)

    def joint_total_stage():
        ref.joint_total[...] = jnp.zeros_like(ref.joint_total)

        @pl.loop(0, length // few)
        def _(j):
            ref.joint_total[...] += eights(grad_qkv[span(j, few), :].astype(F32))

    small = ref.small
    wide_rows = size.gain_rows

    def small_pack():
        ref.own_total[...] = jnp.zeros_like(ref.own_total)

        @pl.loop(0, rows // few)
        def _(j):
            at = pl.ds(pl.multiple_of(s * rows + j * few, few), few)
            ref.own_total[...] += eights(upstream[at, :].astype(F32))

        small[0] = jnp.zeros_like(small[0])
        for first, source, count in (
            (0, ref.gain_total.at[0], wide_rows),
            (wide_rows, ref.gain_total.at[1], wide_rows),
            (2 * wide_rows, ref.gain_total.at[2], wide_rows),
            (3 * wide_rows, ref.gain_total.at[3], wide_rows),
            (4 * wide_rows, ref.own_total, wide_rows),
            (size.joint_small, ref.joint_total, 3 * part // LANES),
            (size.expand_small, ref.expand_total, hidden // LANES),
        ):
            for j in range(count):
                value = source[:, j * LANES : (j + 1) * LANES]
                small[0, first + j : first + j + 1, :] = jnp.sum(value, axis=0, keepdims=True)

    def small_core():
        push_all(
            lambda: (
                [(small.at[0], ref.small_in.at[0])], small.at[0], ref.small_send.at[0], ref.small_recv.at[0], twin
            )
        )

    def small_line():
        arrived(small.at[0], ref.small_recv.at[0])
        small[1] = small[0] + ref.small_in[0]
        for k in range(1, line):
            push_all(
                lambda k=k: (
                    [(small.at[1], ref.small_in.at[k])],
                    small.at[1],
                    ref.small_send.at[k],
                    ref.small_recv.at[k],
                    {DP: (z + k) % line * CORES + c},
                )
            )

    def small_seq():
        total = small[1]
        for k in range(1, line):
            arrived(small.at[0], ref.small_recv.at[k])
            total = total + ref.small_in[k]
        ref.small_all[s] = total
        mine = ref.small_all.at[s]
        seq_push(9, lambda j: [(mine, mine)], mine)

    def small_last():
        seq_wait(9, small.at[0])
        total = ref.small_all[0, 0 : 5 * wide_rows, :]
        for j in range(1, n):
            total = total + ref.small_all[j, 0 : 5 * wide_rows, :]
        ref.gain_grads[...] = total
        for j in range(n):
            ref.joint_grads[j] = ref.small_all[j, size.joint_small : size.expand_small, :]
            ref.expand_grads[j] = ref.small_all[j, size.expand_small : size.expand_small + hidden // LANES, :]

    def owner_sum(buffer):
        chunk = min(size.chunk, rows)
        for q in range(rows // chunk):
            for first in range(0, n, 4):
                sources = [buffer.at[pl.ds(j * rows + q * chunk, chunk)] for j in range(first, min(first + 4, n))]

                def into(where, total):
                    at = pl.ds(pl.multiple_of(where.start + q * chunk, 16), where.size)
                    wide_one[at, 0:width] = total if first == 0 else wide_one[at, 0:width] + total

                added(sources, chunk, width, into)

    def own_tokens():
        return local(
            ref.tokens_all.at[span(s, rows)], stage.at[0, pl.ds(0, rows), pl.ds(0, width)], ref.x_sem.at[0]
        )

    def mixed_pairs(j):
        return [(mixed.at[span(j, rows)], ref.mixed_own.at[:, lanes(s, part)])]

    def finish_output():
        copy = own_tokens()
        output_tiles.wait()
        owner_sum(ref.output_all)
        copy.wait()
        seq_wait(12, mixed.at[pl.ds(0, rows)])
        wide_two[...] = nn(ref.mixed_own[...], right[0:width, :])

        @pl.loop(0, rows // few)
        def _(j):
            at = span(j, few)
            total = stage[0, at, 0:width].astype(F32) + (wide_one[at, 0:width] + wide_two[at, :] + ref.offsets[...])
            stage[1, at, 0:width] = total.astype(BF)

        local(stage.at[1, pl.ds(0, rows), pl.ds(0, width)], ref.output, ref.stage_sem.at[0]).wait()

    def finish_input():
        copy = own_tokens()
        input_tiles.wait()
        owner_sum(ref.input_all)
        copy.wait()

        @pl.loop(0, rows // few)
        def _(j):
            at = span(j, few)
            normal, spread = normal_of(0, at)
            grad = wide_one[at, 0:width]
            through = grad - jnp.mean(grad, axis=-1, keepdims=True)
            through = through - normal * jnp.mean(grad * normal, axis=-1, keepdims=True)
            own = upstream[pl.ds(pl.multiple_of(s * rows + j * few, few), few), :].astype(F32)
            wide_two[at, :] = own + spread * through

        local(wide_two, ref.grad_tokens, ref.stage_sem.at[0]).wait()

    def load_joint():
        return local(ref.joint_all, left.at[:, pl.ds(0, 3 * part)], ref.load_sem.at[0])

    def joint_pairs(j):
        return [
            (
                ref.joint_own.at[:, lanes(j, part, kind * width)],
                ref.joint_all.at[span(s * m + d, piece), pl.ds(kind * part, part)],
            )
            for kind in range(3)
        ]

    def expand_columns(j, u):
        if split == 1:
            return [(pl.multiple_of(j * hidden, LANES), 0, hidden)]
        return [
            (pl.multiple_of(j * hidden + owner * shrink_rows + u * share, LANES), owner * share, share)
            for owner in range(m)
        ]

    def expand_pairs(u):
        return lambda j: [
            (
                ref.expand_own.at[:, pl.ds(first, count)],
                ref.expand_all.at[u, span(s * m + d, piece), pl.ds(to, count)],
            )
            for first, to, count in expand_columns(j, u)
        ]

    def vector_pairs(j):
        return [(ref.vector_own, ref.vectors.at[span(d * n + s, VECTOR_ROWS)])]

    expand_whole = ref.expand_all.at[0, pl.ds(0, piece)]
    joint_whole = ref.joint_all.at[pl.ds(0, piece)]
    expand_items = (1, 7)
    seq_push(expand_items[0], expand_pairs(0), expand_whole)
    seq_push(8, vector_pairs, ref.vector_own)

    def room(buffer, slot, source):
        return buffer.at[slot, pl.ds(0, source.shape[0]), pl.ds(0, source.shape[1])]

    moves = [
        ([(ref.shrink_own.at[pl.ds(u * share, share)], stage.at[1, pl.ds(u * share, share), pl.ds(0, width)])],
         ref.shrink_all.at[u, span(d, share)])
        for u in range(split)
    ]
    moves += [([(ref.tokens, room(stage, 0, ref.tokens))], ref.tokens_all.at[span(s, rows)])]
    moves += [
        (
            [
                (src, adds.at[u, pl.ds(0, piece), pl.ds(to, count)])
                for (src, _), (_, to, count) in zip(expand_pairs(u)(s), expand_columns(s, u))
            ],
            ref.expand_all.at[u, span(s * m + d, piece)],
        )
        for u in range(split)
    ]
    moves += [
        ([(ref.dense_own, room(sent, 0, ref.dense_own))], ref.dense_all.at[span(s * m + d, dense_rows)]),
        (
            [
                (src, adds.at[2, pl.ds(0, piece), pl.ds(kind * part, part)])
                for kind, (src, _) in enumerate(joint_pairs(s))
            ],
            ref.joint_all.at[span(s * m + d, piece)],
        ),
    ]
    held = [pairs[0][1] for pairs, _ in moves[: split + 1]]
    held += [adds.at[u, pl.ds(0, piece), pl.ds(0, units)] for u in range(split)]
    held += [room(sent, 0, ref.dense_own), adds.at[2, pl.ds(0, piece), pl.ds(0, 3 * part)]]
    for k, (pairs, _) in enumerate(moves):
        for src, dst in pairs:
            local(src, dst, ref.own_sem.at[k])
    own_vectors = [local(src, dst, ref.vector_sem.at[0]) for src, dst in vector_pairs(s)]
    own_upstream = local(ref.cotangent, upstream.at[span(s, rows)], ref.vector_sem.at[1])
    stored = []
    for k, (_, target) in enumerate(moves):
        pltpu.make_async_copy(held[k], held[k], ref.own_sem.at[k]).wait()
        stored.append(local(held[k], target, ref.own_sem.at[k]))
    own_tokens_at, own_expand_at, own_dense_at = split, split + 1, 2 * split + 1
    stored[0].wait()
    gather_step(shrink_in[0], 0)
    stored[own_tokens_at].wait()
    spread_first(2, ref.tokens_all)
    own_vectors[0].wait()
    seq_wait(8, ref.vector_own)
    vector_send()
    stored[own_expand_at].wait()
    seq_wait(expand_items[0], expand_whole)
    gather_step(expand_in[0], 0)
    for k, copy in enumerate(stored):
        if k not in (0, own_tokens_at, own_expand_at):
            copy.wait()
    own_upstream.wait()
    ref.gain_total[...] = jnp.zeros_like(ref.gain_total)
    ref.expand_total[...] = jnp.zeros_like(ref.expand_total)
    for u in range(1, split):
        seq_push(expand_items[u], expand_pairs(u), expand_whole)
    gather_step(shrink_in[0], 1)
    gather_step(expand_in[0], 1)
    spread_second(2, ref.tokens_all)
    spread_first(3, upstream)
    gather_step(shrink_in[0], 2)
    vector_swap()
    gather_step(dense_in, 0)
    spread_wait(2, ref.tokens_all)
    gather_step(expand_in[0], 2)
    for u in range(1, split):
        gather_step(shrink_in[u], 0)
    gather_wait(vector_in)
    unpack_vectors()
    norm_stage(1)
    gather_step(shrink_in[0], 3)
    for u in range(1, split):
        seq_wait(expand_items[u], expand_whole)
        gather_step(expand_in[u], 0)
    spread_second(3, upstream)
    seq_push(0, joint_pairs, joint_whole)
    gather_step(expand_in[0], 3)
    gather_rest(shrink_in[0], expand_in[0])

    def load_expand(u):
        return local(ref.expand_all.at[u], left.at[:, pl.ds(u * units, units)], ref.load_sem.at[0])

    def load_shrink(u):
        return local(ref.shrink_all.at[u], right.at[pl.ds(u * units, units)], ref.load_sem.at[1])

    def shrink_grad_stage(u):
        weight_grad(
            lambda b: act[:, lanes(b, size.units_tall, u * units)],
            lambda: upstream[...],
            units // size.units_tall,
            size.units_tall,
            width,
            owner_places(ref.shrink_sum.at[u], size.units_tall, share),
        )
        reduce_start(shrink_kind[u])

    def expand_grad_stage(u):
        weight_grad(
            columns_of(normed, mid_rows),
            lambda: slope[:, group(u)],
            m,
            mid_rows,
            units,
            piece_places(ref.expand_sum.at[u], mid_rows),
        )
        reduce_start(expand_kind[u])

    def finish_expand(u):
        columns = [(to, s * hidden + first, count) for first, to, count in expand_columns(0, u)]
        finish_columns(expand_kind[u], 10 + u, ref.expand_done.at[u], ref.expand_grad, columns)

    gather_wait(shrink_in[0], expand_in[0])
    copy_one, copy_two = load_expand(0), load_shrink(0)
    copy_one.wait()
    expand_stage(0)
    gather_step(dense_in, 1)
    if split > 1:
        gather_step(shrink_in[1], 1)
    spread_wait(3, upstream)
    shrink_grad_stage(0)
    copy_two.wait()
    shrink_stage(0)
    if split > 1:
        gather_step(expand_in[1], 1)
    expand_grad_stage(0)
    reduce_hop(1, shrink_kind[0])
    gather_step(dense_in, 2)
    if split > 1:
        gather_step(shrink_in[1], 2)
    reduce_hop(1, expand_kind[0])
    if split > 1:
        gather_step(expand_in[1], 2)
    gather_step(dense_in, 3)
    gather_rest(dense_in)
    gather_wait(dense_in)
    spread_first(13, ref.dense_all, part)
    gate_stage(load_dense())
    seq_wait(0, joint_whole)
    if split > 1:
        gather_step(shrink_in[1], 3)
    gather_step(joint_a, 0)
    reduce_hop(2, shrink_kind[0])
    if split > 1:
        gather_step(expand_in[1], 3)
        gather_rest(shrink_in[1], expand_in[1])
    gather_step(joint_b, 0)
    last = split - 1
    if split > 1:
        gather_wait(shrink_in[1], expand_in[1])
        copy_one, copy_two = load_expand(1), load_shrink(1)
        copy_one.wait()
        expand_stage(1)
    reduce_hop(2, expand_kind[0])
    gather_step(joint_a, 1)
    if split > 1:
        shrink_grad_stage(1)
    reduce_hop(3, shrink_kind[0])
    gather_step(joint_b, 1)
    if split > 1:
        copy_two.wait()
        shrink_stage(1)
    spread_second(13, ref.dense_all, part)
    if split > 1:
        expand_grad_stage(1)
    gather_step(joint_a, 2)
    reduce_hop(3, expand_kind[0])
    for hop in range(4, hops + 1):
        reduce_hop(hop, shrink_kind[0], expand_kind[0])
    if split > 1:
        reduce_hop(1, shrink_kind[1])
    gather_step(joint_b, 2)
    if split > 1:
        reduce_hop(1, expand_kind[1])
    output_stage()
    gather_step(joint_a, 3)
    if split > 1:
        finish_rows(shrink_kind[0], ref.shrink_grad, 0)
        reduce_hop(2, shrink_kind[1])
    gather_step(joint_b, 3)
    gather_rest(joint_a, joint_b)
    if split > 1:
        finish_expand(0)
        reduce_hop(2, expand_kind[1])
    each_tile(input_feed_stage)
    input_feed_flush()
    if split > 1:
        reduce_hop(3, shrink_kind[1])
    gather_wait(joint_a, joint_b)
    copy_one = load_joint()
    norm_stage(0)
    if split > 1:
        reduce_hop(3, expand_kind[1])
        for hop in range(4, hops + 1):
            reduce_hop(hop, shrink_kind[1], expand_kind[1])
    copy_one.wait()
    joint_stage()
    for head in range(heads):
        attend_stage(head)
    seq_push(12, mixed_pairs, mixed.at[pl.ds(0, rows)])
    tall = min(part, size.high)
    weight_grad(
        columns_of(mixed, tall),
        lambda: upstream[...],
        part // tall,
        tall,
        width,
        owner_places(ref.dense_sum, tall, dense_rows),
    )
    reduce_start(dense_kind)
    weight_grad(
        columns_of(normed, mid_rows),
        lambda: grad_qkv[...],
        m,
        mid_rows,
        3 * part,
        piece_places(ref.joint_sum, mid_rows),
    )
    reduce_start(joint_kind)
    spread_wait(13, ref.dense_all, part)
    load_wide = local(ref.dense_all, right.at[pl.ds(0, width)], ref.load_sem.at[1])
    ref.mixed_own[:, lanes(s, part)] = mixed[span(s, rows), :]
    reduce_hop(1, dense_kind, joint_kind)
    each_tile(input_stage)
    input_tiles.flush()
    reduce_hop(2, dense_kind, joint_kind)
    joint_total_stage()
    small_pack()
    small_core()
    finish_rows(shrink_kind[last], ref.shrink_grad, last * share)
    small_line()
    reduce_hop(3, dense_kind, joint_kind)
    small_seq()
    finish_expand(last)
    load_wide.wait()
    finish_output()
    for hop in range(4, hops + 1):
        reduce_hop(hop, dense_kind, joint_kind)
    finish_rows(dense_kind, ref.dense_grad)
    finish_columns(
        joint_kind,
        6,
        ref.joint_done,
        ref.joint_grad,
        [(kind * part, kind * width + s * part, part) for kind in range(3)],
    )
    small_last()
    finish_input()
    seq_wait(6, ref.joint_done.at[pl.ds(0, piece)])
    for u in range(split):
        seq_wait(10 + u, ref.expand_done.at[u, pl.ds(0, piece)])
    for pending in rounds.pending:
        if pending is not None:
            pending()
    for drain in drains:
        drain()


def run_kernel(size, inputs):
    n, m, line, hops = size.n, size.m, size.line, size.hops
    rows, width, piece, part, hidden = size.rows, size.width, size.piece, size.part, size.hidden
    dense_rows, mid_rows, shrink_rows, length = size.dense_rows, size.mid_rows, size.shrink_rows, size.length
    anywhere, vmem = pl.BlockSpec(memory_space=pl.ANY), pl.BlockSpec(memory_space=pltpu.VMEM)

    def reduced(count, columns):
        shape = (count, columns)
        return ((line, CORES) + shape, BF), ((line,) + shape, BF), ((2, line) + shape, BF)

    dense, joint = reduced(dense_rows, width), reduced(mid_rows, 3 * part)
    expand, shrink = reduced(mid_rows, size.units), reduced(size.share, width)
    expand, shrink = [[((size.split,) + shape, kind) for shape, kind in arrays] for arrays in (expand, shrink)]
    small_outputs = dict(
        gain_grads=((5 * size.gain_rows, LANES), F32),
        joint_grads=((n, 3 * part // LANES, LANES), F32),
        expand_grads=((n, hidden // LANES, LANES), F32),
    )
    outputs = dict(
        output=((rows, width), BF),
        grad_tokens=((rows, width), F32),
        dense_grad=((dense_rows, width), F32),
        shrink_grad=((shrink_rows, width), F32),
        joint_grad=((piece, 3 * width), F32),
        expand_grad=((piece, n * hidden), F32),
        dense_all=((width, width), BF),
        joint_all=((width, 3 * part), BF),
        expand_all=((size.split, width, size.units), BF),
        shrink_all=((size.split, size.units, width), BF),
        tokens_all=((length, width), BF),
        output_all=((length, width), BF),
        input_all=((length, width), BF),
        output_part=((length, width), BF),
        input_part=((length, width), BF),
        input_kept=((length, width), BF),
        joint_done=((mid_rows, 3 * part), F32),
        expand_done=((size.split, mid_rows, size.units), F32),
        dense_sum=dense[0],
        dense_core=dense[1],
        dense_chain=dense[2],
        joint_sum=joint[0],
        joint_core=joint[1],
        joint_chain=joint[2],
        expand_sum=expand[0],
        expand_core=expand[1],
        expand_chain=expand[2],
        shrink_sum=shrink[0],
        shrink_core=shrink[1],
        shrink_chain=shrink[2],
    )
    dma = pltpu.SemaphoreType.DMA
    small = (size.small, LANES)
    scratch = dict(
        upstream=pltpu.VMEM((length, width), BF),
        normed=pltpu.VMEM((length, width), BF),
        qkv=pltpu.VMEM((length, 3 * part), BF),
        gate=pltpu.VMEM((length, part), BF),
        act=pltpu.VMEM((length, hidden), BF),
        slope=pltpu.VMEM((length, hidden), BF),
        left=pltpu.VMEM((width, max(hidden, 3 * part)), BF),
        right=pltpu.VMEM((max(hidden, width), width), BF),
        mixed_own=pltpu.VMEM((rows, width), BF),
        outs=pltpu.VMEM((2, rows, width), BF),
        wide_one=pltpu.VMEM((max(rows, size.chunk), max(width, hidden)), F32),
        wide_two=pltpu.VMEM((rows, width), F32),
        stage=pltpu.VMEM((2, size.high, size.broad), BF),
        adds=pltpu.VMEM((8, size.chunk, size.broad), BF),
        sent=pltpu.VMEM((4, size.chunk, size.broad), BF),
        vectors=pltpu.VMEM((n * m * VECTOR_ROWS, LANES), F32),
        gains=pltpu.VMEM((4, width), F32),
        offsets=pltpu.VMEM((1, width), F32),
        joint_bias=pltpu.VMEM((1, 3 * part), F32),
        expand_bias=pltpu.VMEM((1, hidden), F32),
        gain_total=pltpu.VMEM((4, 8, width), F32),
        own_total=pltpu.VMEM((8, width), F32),
        joint_total=pltpu.VMEM((8, 3 * part), F32),
        expand_total=pltpu.VMEM((8, hidden), F32),
        small=pltpu.VMEM((2,) + small, F32),
        small_in=pltpu.VMEM((line,) + small, F32),
        small_all=pltpu.VMEM((n,) + small, F32),
        seq_send=dma((14, max(n, 4))),
        seq_recv=dma((14, max(n, 4))),

        ag_send=dma((8, 2, hops)),
        ag_recv=dma((8, 2, hops)),
        swap_send=dma((8, line)),
        swap_recv=dma((8, line)),
        core_send=dma((11,)),
        core_recv=dma((11,)),
        rs_send=dma((11, 2, hops)),
        rs_recv=dma((11, 2, hops)),
        small_send=dma((line,)),
        small_recv=dma((line,)),
        add_sem=dma((8,)),
        stage_sem=dma((2,)),
        load_sem=dma((3,)),
        own_sem=dma((7,)),
        vector_sem=dma((2,)),
        vector_out=dma((line,)),
        vector_back=dma((line,)),
        out_sem=dma((2,)),
        keep_sem=dma((2,)),
        x_sem=dma((2,)),
    )
    names = list(inputs) + list(outputs) + list(small_outputs) + list(scratch)
    results = pl.pallas_call(
        functools.partial(kernel, size, names),
        out_shape=[
            jax.ShapeDtypeStruct(shape, kind)
            for shape, kind in list(outputs.values()) + list(small_outputs.values())
        ],
        in_specs=[vmem if name == next(reversed(inputs)) else anywhere for name in inputs],
        out_specs=[anywhere] * len(outputs) + [vmem] * len(small_outputs),
        scratch_shapes=list(scratch.values()),
        compiler_params=pltpu.CompilerParams(
            collective_id=0, has_side_effects=True, vmem_limit_bytes=64 * 2**20 - 2**17
        ),
        name="block",
    )(*inputs.values())
    return types.SimpleNamespace(**dict(zip(list(outputs) + list(small_outputs), results)))


def block_plan(n, m, tokens, cotangent, shards):
    (
        first_gain,
        first_shift,
        second_gain,
        second_shift,
        joint_weight,
        joint_bias,
        dense_weight,
        dense_bias,
        expand_weight,
        expand_bias,
        shrink_weight,
        shrink_bias,
    ) = shards
    rows, width = tokens.shape[1:]
    size = sizes_of(n, m, rows, width, expand_weight.shape[1])
    piece, devices = size.piece, n * m
    vectors = jnp.concatenate(
        [
            first_gain,
            first_shift,
            second_gain,
            second_shift,
            joint_bias,
            dense_bias,
            expand_bias,
            shrink_bias,
        ]
    )
    vectors = vectors.astype(F32).reshape(-1, 1, piece)
    vectors = jnp.broadcast_to(vectors, (vectors.shape[0], LANES // piece, piece)).reshape(-1, LANES)
    vectors = jnp.pad(vectors, ((0, VECTOR_ROWS - vectors.shape[0]), (0, 0)))
    got = run_kernel(
        size,
        dict(
            tokens=tokens[0],
            cotangent=cotangent[0],
            joint_own=joint_weight,
            expand_own=expand_weight,
            dense_own=dense_weight,
            shrink_own=shrink_weight,
            vector_own=vectors,
            tables=turn_tables(size.length),
        ),
    )
    index = lax.axis_index(SEQ) * m + lax.axis_index(DP)

    def own(values):
        return lax.dynamic_index_in_dim(values.reshape(devices, -1), index, 0, keepdims=False)

    gains = lax.dynamic_slice_in_dim(got.gain_grads.reshape(5, width), index * piece, piece, 1)
    joint_grads = jnp.swapaxes(got.joint_grads.reshape(n, 3, size.part), 0, 1)
    expand_grads = jnp.swapaxes(got.expand_grads.reshape(n, size.split, m, size.share), 1, 2)
    return (
        got.output[None],
        got.grad_tokens[None],
        gains[0],
        gains[1],
        gains[2],
        gains[3],
        got.joint_grad,
        own(joint_grads),
        got.dense_grad,
        gains[4],
        got.expand_grad,
        own(expand_grads),
        got.shrink_grad,
        gains[4],
    )


def solution(mesh):
    n, m = mesh.shape[SEQ], mesh.shape[DP]

    def body(tokens, cotangent, *shards):
        return block_plan(n, m, tokens, cotangent, shards)

    both = (SEQ, DP)
    tokens = P(DP, SEQ, None)
    vector, matrix = P(both), P(both, None)
    return jax.shard_map(
        body,
        mesh=mesh,
        in_specs=(tokens, tokens) + (vector,) * 4 + (matrix, vector) * 4,
        out_specs=(tokens, tokens) + (vector,) * 4 + (matrix, vector) * 4,
        check_vma=False,
    )
```

```python
import functools
import types

import jax
import jax.numpy as jnp
import numpy as np
from jax import lax
from jax.experimental import pallas as pl
from jax.experimental.pallas import tpu as pltpu
from jax.sharding import PartitionSpec as P

HEADS = 8
ROT = 64
CORES = 2
LANES = 128
VECTOR_ROWS = 16
STEP = 64
SEQ, DP = "seq", "dp"
BF = jnp.bfloat16
F32 = jnp.float32
MESH = pl.DeviceIdType.MESH


def nn(left, right):
    return jnp.dot(left, right, preferred_element_type=F32)


def nt(left, right):
    return lax.dot_general(left, right, (((1,), (1,)), ((), ())), preferred_element_type=F32)


def tn(left, right):
    return lax.dot_general(left, right, (((0,), (0,)), ((), ())), preferred_element_type=F32)


def turn_tables(length):
    inverse = 10000.0 ** (-np.arange(0, ROT, 2, dtype=np.float64) / ROT)
    angle = np.arange(length, dtype=np.float32)[:, None] * inverse.astype(np.float32)[None, :]
    cosine, sine = np.cos(angle.astype(np.float64)), np.sin(angle.astype(np.float64))
    rest = np.zeros((length, LANES - ROT))
    table = np.stack(
        [
            np.concatenate([cosine, cosine, rest + 1.0], axis=1),
            np.concatenate([sine, sine, rest], axis=1),
        ]
    )
    return jnp.asarray(table, F32)


def sizes_of(n, m, rows, width, feed):
    devices = n * m
    z = types.SimpleNamespace(n=n, m=m, rows=rows, width=width)
    z.line, z.hops = m // CORES, m // CORES - 1
    z.length = rows * n
    z.piece = width // devices
    z.part = width // n
    z.hidden = feed // n
    z.heads, z.head_size = HEADS // n, width // HEADS
    z.dense_rows, z.mid_rows, z.shrink_rows = z.part // m, width // m, z.hidden // m
    z.feed_pieces = feed // width
    z.split = 2 if z.shrink_rows % (2 * LANES) == 0 else 1
    z.share = z.shrink_rows // z.split
    z.units = z.hidden // z.split
    z.units_tall = min(z.units, max(z.share, 2 * LANES))
    z.high = max(rows, z.mid_rows, z.shrink_rows)
    z.broad = max(width, z.hidden, 3 * z.part)
    z.chunk = max(z.mid_rows // 2, z.shrink_rows // 4)
    z.gain_rows = width // LANES
    z.joint_small = 5 * z.gain_rows
    z.expand_small = z.joint_small + 3 * z.part // LANES
    z.small = -(-(z.expand_small + z.hidden // LANES) // 8) * 8
    return z


def kernel(size, names, *refs):
    ref = types.SimpleNamespace(**dict(zip(names, refs)))
    n, m, line, hops = size.n, size.m, size.line, size.hops
    rows, width, piece, part, hidden = size.rows, size.width, size.piece, size.part, size.hidden
    heads, head_size, length = size.heads, size.head_size, size.length
    dense_rows, mid_rows, shrink_rows = size.dense_rows, size.mid_rows, size.shrink_rows
    split, share, units = size.split, size.share, size.units
    scale = head_size ** (-0.5)
    s, d = lax.axis_index(SEQ), lax.axis_index(DP)
    z, c = d // CORES, d % CORES
    twin = {DP: z * CORES + 1 - c}
    above, below = {DP: d + CORES}, {DP: d - CORES}
    drains = []

    def remote(src, dst, send, recv, device):
        return pltpu.make_async_remote_copy(
            src_ref=src, dst_ref=dst, send_sem=send, recv_sem=recv, device_id=device, device_id_type=MESH
        )

    def push_all(make, when=None, keep=True):
        def start():
            pairs, _, send, recv, device = make()
            for src, dst in pairs:
                remote(src, dst, send, recv, device).start()

        def settle():
            _, whole, send, recv, device = make()
            remote(whole, whole, send, recv, device).wait_send()

        def guarded(step):
            return step if when is None else lambda: pl.when(when())(step)

        guarded(start)()
        if keep:
            drains.append(guarded(settle))
        return guarded(settle)

    def arrived(whole, recv):
        remote(whole, whole, recv, recv, twin).wait_recv()

    def local(src, dst, sem):
        copy = pltpu.make_async_copy(src, dst, sem)
        copy.start()
        return copy

    def span(index, size, count=None, offset=0):
        count = size if count is None else count
        return pl.ds(pl.multiple_of(index * size + offset, count), count)

    def lanes(index, size, offset=0):
        return pl.ds(pl.multiple_of(index * size + offset, LANES), size)

    barrier = pltpu.get_barrier_semaphore()
    greeted = [{SEQ: (s + k) % n} for k in range(1, n)]
    greeted += [{DP: (z + k) % line * CORES + c} for k in range(1, line)] + [twin]
    for device in greeted:
        pl.semaphore_signal(barrier, inc=1, device_id=device, device_id_type=MESH)
    pl.semaphore_wait(barrier, len(greeted))

    def seq_push(item, pairs_of, whole):
        for k in range(1, n):
            j = (s + k) % n
            push_all(
                lambda j=j, k=k: (
                    pairs_of(j), whole, ref.seq_send.at[item, k], ref.seq_recv.at[item, k], {SEQ: j}
                )
            )

    def seq_wait(item, whole):
        for k in range(1, n):
            arrived(whole, ref.seq_recv.at[item, k])

    square = n == 4
    beside, across = s + 1 - 2 * (s % 2), (s + 2) % n

    def spread_first(item, buffer, tall=rows):
        mine = buffer.at[span(s, tall)]
        if not square:
            seq_push(item, lambda j: [(mine, mine)], mine)
            return
        for way, target in ((0, beside), (1, across)):
            push_all(
                lambda way=way, target=target: (
                    [(mine, mine)], mine, ref.seq_send.at[item, way], ref.seq_recv.at[item, way], {SEQ: target}
                )
            )

    def spread_second(item, buffer, tall=rows):
        if not square:
            return
        for way, source, target in ((0, beside, across), (1, across, beside)):
            arrived(buffer.at[span(source, tall)], ref.seq_recv.at[item, way])
            half = buffer.at[span(source, tall, tall // 2, way * (tall // 2))]
            push_all(
                lambda way=2 + way, target=target, half=half: (
                    [(half, half)], half, ref.seq_send.at[item, way], ref.seq_recv.at[item, way], {SEQ: target}
                )
            )

    def spread_wait(item, buffer, tall=rows):
        if not square:
            seq_wait(item, buffer.at[pl.ds(0, tall)])
            return
        for way in range(2):
            arrived(buffer.at[pl.ds(0, tall // 2)], ref.seq_recv.at[item, 2 + way])

    def chain_of(number, buffer, runs, count):
        def views(owner):
            return [buffer.at[span(run(owner), count)] for run in runs]

        whole = buffer.at[pl.ds(0, count * len(runs))]
        return types.SimpleNamespace(number=number, views=views, whole=whole)

    def piece_runs(first, last):
        return [lambda owner, j=j: j * m + owner for j in range(first, last)]

    shrink_in = [chain_of(u, ref.shrink_all.at[u], [lambda owner: owner], share) for u in range(split)]
    expand_in = [chain_of(2 + u, ref.expand_all.at[u], piece_runs(0, n), piece) for u in range(split)]
    dense_in = chain_of(4, ref.dense_all, [lambda owner: s * m + owner], dense_rows)
    joint_a = chain_of(5, ref.joint_all, piece_runs(0, n // 2), piece)
    joint_b = chain_of(6, ref.joint_all, piece_runs(n // 2, n), piece)
    vector_in = chain_of(7, ref.vectors, [lambda owner: owner], n * VECTOR_ROWS)

    def vector_send():
        for k in range(1, line):
            view = ref.vectors.at[span(d, n * VECTOR_ROWS)]
            push_all(
                lambda k=k, view=view: (
                    [(view, view)],
                    view,
                    ref.vector_out.at[k],
                    ref.vector_back.at[k],
                    {DP: (z + k) % line * CORES + c},
                )
            )

    def vector_swap():
        for k in range(1, line):
            arrived(vector_in.whole, ref.vector_back.at[k])
        for k in range(line):
            view = ref.vectors.at[span(k * CORES + c, n * VECTOR_ROWS)]
            push_all(
                lambda k=k, view=view: (
                    [(view, view)], view, ref.swap_send.at[7, k], ref.swap_recv.at[7, k], twin
                )
            )


    def gather_step(chain, hop):
        number = chain.number

        def views(owner):
            return [(view, view) for view in chain.views(owner() * CORES + c)]

        def swap(owner, when=None):
            push_all(
                lambda: (
                    views(owner),
                    chain.whole,
                    ref.swap_send.at[number, owner()],
                    ref.swap_recv.at[number, owner()],
                    twin,
                ),
                when,
            )

        def forward(side, owner, when):
            push_all(
                lambda: (
                    views(owner),
                    chain.whole,
                    ref.ag_send.at[number, side, hop],
                    ref.ag_recv.at[number, side, hop],
                    below if side else above,
                ),
                when,
            )

        if hop > hops:
            return
        if hop == 0:
            forward(0, lambda: z, lambda: z < line - 1)
            forward(1, lambda: z, lambda: z > 0)
            swap(lambda: z)
            return
        for side, owner, valid, more in (
            (0, lambda: (z - hop + line) % line, lambda: z >= hop, lambda: z < line - 1),
            (1, lambda: (z + hop) % line, lambda: z + hop < line, lambda: z > 0),
        ):
            pl.when(valid())(functools.partial(arrived, chain.whole, ref.ag_recv.at[number, side, hop - 1]))
            if hop < hops:
                forward(side, owner, lambda valid=valid, more=more: valid() & more())
            swap(owner, valid)

    def gather_wait(*chains):
        for chain in chains:
            for owner in range(line):
                arrived(chain.whole, ref.swap_recv.at[chain.number, owner])

    def gather_rest(*chains):
        for hop in range(4, hops + 1):
            for chain in chains:
                gather_step(chain, hop)

    def kind_of(first, total, core, chain, halves, count, columns, together=True):
        return types.SimpleNamespace(
            first=first,
            total=total,
            core=core,
            chain=chain,
            halves=halves,
            count=count,
            columns=columns,
            together=together,
        )

    mid, low = mid_rows // 2, share // 2
    dense_kind = kind_of(0, ref.dense_sum, ref.dense_core, ref.dense_chain, 1, dense_rows, width)
    joint_kind = kind_of(1, ref.joint_sum, ref.joint_core, ref.joint_chain, 2, mid, 3 * part, False)
    expand_kind = [
        kind_of(3 + 2 * u, ref.expand_sum.at[u], ref.expand_core.at[u], ref.expand_chain.at[u], 2, mid, units)
        for u in range(split)
    ]
    shrink_kind = [
        kind_of(7 + 2 * u, ref.shrink_sum.at[u], ref.shrink_core.at[u], ref.shrink_chain.at[u], 2, low, width)
        for u in range(split)
    ]
    adds, add_sem, sent = ref.adds, ref.add_sem, ref.sent
    rounds = types.SimpleNamespace(ring=0, pending=[None, None])

    def reduce_start(kind):
        for half in range(kind.halves):
            at = pl.ds(half * kind.count, kind.count)
            push_all(
                lambda at=at, half=half: (
                    [(kind.total.at[:, 1 - c, at], kind.core.at[:, at])],
                    kind.core.at[:, at],
                    ref.core_send.at[kind.first + half],
                    ref.core_recv.at[kind.first + half],
                    twin,
                )
            )

    def summed(slots, count, columns, into):
        step = min(count, STEP)

        @pl.loop(0, count // step)
        def _(i):
            at = span(i, step)
            total = adds[slots[0], at, 0:columns].astype(F32)
            for slot in slots[1:]:
                total = total + adds[slot, at, 0:columns].astype(F32)
            into(at, total)

    def added(sources, count, columns, into):
        copies = []
        for slot, source in enumerate(sources):
            copies.append(local(source, adds.at[slot, pl.ds(0, count), pl.ds(0, columns)], add_sem.at[slot]))
        for copy in copies:
            copy.wait()
        summed(range(len(sources)), count, columns, into)

    def add_slot(kind, slot):
        return adds.at[slot, pl.ds(0, kind.count), pl.ds(0, kind.columns)]

    def add_load(kind, source, slot):
        return pltpu.make_async_copy(source, add_slot(kind, slot), add_sem.at[slot])

    def blank(kind, slot):
        adds[slot, 0 : kind.count, 0 : kind.columns] = jnp.zeros((kind.count, kind.columns), BF)

    def reduce_round(kind, hop, side, valid):
        count, columns = kind.count, kind.columns
        ring = rounds.ring
        rounds.ring = 1 - ring
        if rounds.pending[ring] is not None:
            rounds.pending[ring]()
        target = lambda: (z + (line - hop) * (1 - 2 * side()) + line) % line
        joined = lambda: z + side() * (line - 1 - 2 * z) > 0
        device = lambda: {DP: d + CORES * (1 - 2 * side())}

        def at(half):
            return span(half, count)

        @pl.when(valid())
        def _():
            @pl.loop(0, kind.halves)
            def _(half):
                add_load(kind, kind.total.at[target(), c, at(half)], half * 3).start()
                add_load(kind, kind.core.at[target(), at(half)], half * 3 + 1).start()

            def behind_of(half):
                return kind.chain.at[side(), target(), at(half)]

            def await_behind(half):
                if hop > 1:

                    @pl.when(joined())
                    def _():
                        arrived(behind_of(half), ref.rs_recv.at[kind.first + half, side(), hop - 2])
                        add_load(kind, behind_of(half), half * 3 + 2).start()

                    @pl.when(jnp.logical_not(joined()))
                    def _():
                        blank(kind, half * 3 + 2)

            def send(half):
                add_load(kind, kind.total.at[target(), c, at(half)], half * 3).wait()
                add_load(kind, kind.core.at[target(), at(half)], half * 3 + 1).wait()
                slots = [half * 3, half * 3 + 1]
                if hop > 1:
                    pl.when(joined())(lambda: add_load(kind, behind_of(half), half * 3 + 2).wait())
                    slots.append(half * 3 + 2)

                def keep(where, total):
                    sent[ring * 2 + half, where, 0:columns] = total.astype(BF)

                summed(slots, count, columns, keep)
                remote(
                    sent.at[ring * 2 + half, pl.ds(0, count), pl.ds(0, columns)],
                    behind_of(half),
                    ref.rs_send.at[kind.first + half, side(), hop - 1],
                    ref.rs_recv.at[kind.first + half, side(), hop - 1],
                    device(),
                ).start()

            if kind.together:
                pl.loop(0, kind.halves)(await_behind)
                pl.loop(0, kind.halves)(send)
            else:

                @pl.loop(0, kind.halves)
                def _(half):
                    await_behind(half)
                    send(half)

        def settle():
            @pl.when(valid())
            def _():
                view = sent.at[0, pl.ds(0, count), pl.ds(0, columns)]
                for half in range(kind.halves):
                    remote(
                        view,
                        view,
                        ref.rs_send.at[kind.first + half, side(), hop - 1],
                        ref.rs_recv.at[kind.first + half, side(), hop - 1],
                        device(),
                    ).wait_send()

        rounds.pending[ring] = settle

    def reduce_hop(hop, *kinds):
        if hop > hops:
            return
        for kind in kinds:
            if hop == 1:
                for half in range(kind.halves):
                    arrived(
                        kind.core.at[:, pl.ds(half * kind.count, kind.count)], ref.core_recv.at[kind.first + half]
                    )
            if 2 * hop <= line:
                reduce_round(kind, hop, lambda: z * 2 // line, lambda: (z < hop) | (z >= line - hop))
            else:
                reduce_round(kind, hop, lambda: 0, lambda: z < hop)
                reduce_round(kind, hop, lambda: 1, lambda: z >= line - hop)

    def reduce_last(kind):
        def sources(half):
            at = span(half, kind.count)
            return kind.total.at[z, c, at], kind.core.at[z, at], kind.chain.at[0, z, at], kind.chain.at[1, z, at]

        ends = ((0, lambda: z > 0), (1, lambda: z < line - 1))

        @pl.loop(0, kind.halves)
        def _(half):
            for slot in range(2):
                add_load(kind, sources(half)[slot], half * 4 + slot).start()
            for side, there in ends:

                @pl.when(there())
                def _():
                    arrived(sources(half)[2 + side], ref.rs_recv.at[kind.first + half, side, hops - 1])
                    add_load(kind, sources(half)[2 + side], half * 4 + 2 + side).start()

                @pl.when(jnp.logical_not(there()))
                def _():
                    blank(kind, half * 4 + 2 + side)

        @pl.loop(0, kind.halves)
        def _(half):
            for slot in range(2):
                add_load(kind, sources(half)[slot], half * 4 + slot).wait()
            for side, there in ends:
                pl.when(there())(lambda: add_load(kind, sources(half)[2 + side], half * 4 + 2 + side).wait())

            def keep(where, total):
                at = pl.ds(pl.multiple_of(half * kind.count + where.start, 16), where.size)
                ref.wide_one[at, 0 : kind.columns] = total

            summed([half * 4 + slot for slot in range(4)], kind.count, kind.columns, keep)

    def finish_rows(kind, out, first=0):
        reduce_last(kind)
        tall = kind.halves * kind.count
        local(ref.wide_one.at[pl.ds(0, tall), pl.ds(0, kind.columns)], out.at[pl.ds(first, tall)], add_sem.at[0]).wait()

    def finish_columns(kind, item, done, out, columns):
        whole = done.at[pl.ds(0, piece)]

        def pairs(j):
            return [
                (done.at[span(j, piece), pl.ds(first, count)], out.at[:, pl.ds(pl.multiple_of(to, LANES), count)])
                for first, to, count in columns
            ]

        def sems(j):
            k = (j - s + n) % n
            return ref.seq_send.at[item, k], ref.seq_recv.at[item, k], {SEQ: j}

        reduce_last(kind)
        tall = kind.halves * kind.count
        local(ref.wide_one.at[pl.ds(0, tall), pl.ds(0, kind.columns)], done.at[pl.ds(0, tall)], add_sem.at[0]).wait()

        @pl.loop(0, n)
        def _(j):
            @pl.when(j != s)
            def _():
                for src, dst in pairs(j):
                    remote(src, dst, *sems(j)).start()

            @pl.when(j == s)
            def _():
                for (first, _, count), (_, dst) in zip(columns, pairs(j)):
                    local(ref.wide_one.at[span(j, piece), pl.ds(first, count)], dst, add_sem.at[0])
                pltpu.make_async_copy(whole, whole, add_sem.at[0]).wait()

        for k in range(1, n):
            drains.append(lambda k=k: remote(whole, whole, *sems((s + k) % n)).wait_send())

    upstream, normed, qkv = ref.upstream, ref.normed, ref.qkv
    gate, mixed, grad_qkv = ref.gate, ref.gate, ref.qkv
    act, slope = ref.act, ref.slope
    left, right = ref.left, ref.right
    wide_one, wide_two = ref.wide_one, ref.wide_two
    stage, gains, tables = ref.stage, ref.gains, ref.tables
    few = 128

    def joined_row(rows_of):
        lane = lax.broadcasted_iota(jnp.int32, (1, LANES), 1)
        value = ref.vectors[pl.ds(rows_of(0), 1), :]
        for q in range(1, LANES // piece):
            value = jnp.where(lane >= q * piece, ref.vectors[pl.ds(rows_of(q), 1), :], value)
        return value

    def vector_row(owner, row):
        return (owner % m * n + owner // m) * VECTOR_ROWS + row

    def unpack_vectors():
        group = LANES // piece
        for j in range(width // LANES):
            at = slice(j * LANES, (j + 1) * LANES)
            natural = lambda row: joined_row(lambda q: vector_row(j * group + q, row))
            for k in range(4):
                gains[k : k + 1, at] = natural(k)
            ref.offsets[0:1, at] = natural(7) + natural(8 + size.feed_pieces)
        for target, per, row, kinds, wide in (
            (ref.joint_bias, 3, 4, 3, part),
            (ref.expand_bias, size.feed_pieces, 8, 1, hidden),
        ):
            for j in range(kinds * wide // LANES):
                kind, inner = j // (wide // LANES), j % (wide // LANES)
                if kinds == 1 and split > 1:
                    owner, within = inner // (share // LANES) % m, inner % (share // LANES)
                    inner = (owner * split + inner // (units // LANES)) * (share // LANES) + within
                first = (kind * wide * n + inner * LANES) // piece + s * (wide // piece)
                target[0:1, j * LANES : (j + 1) * LANES] = joined_row(
                    lambda q: vector_row((first + q) // per, row + (first + q) % per)
                )

    def each_tile(body):
        def load(i, slot):
            return pltpu.make_async_copy(
                ref.tokens_all.at[span(i, rows)],
                stage.at[slot, pl.ds(0, rows), pl.ds(0, width)],
                ref.x_sem.at[slot],
            )

        load(0, 0).start()

        @pl.loop(0, n)
        def _(i):
            slot = i % 2
            load(i, slot).wait()

            @pl.when(i + 1 < n)
            def _():
                load(i + 1, 1 - slot).start()

            body(i, slot)

    def normal_of(slot, at):
        value = stage[slot, at, 0:width].astype(F32)
        center = value - jnp.mean(value, axis=-1, keepdims=True)
        spread = lax.rsqrt(jnp.mean(center * center, axis=-1, keepdims=True) + 1e-05)
        return center * spread, spread

    def norm_stage(which):
        def body(i, slot):
            @pl.loop(0, rows // few)
            def _(j):
                value, _ = normal_of(slot, span(j, few))
                value = value * gains[2 * which : 2 * which + 1, :] + gains[2 * which + 1 : 2 * which + 2, :]
                normed[pl.ds(pl.multiple_of(i * rows + j * few, few), few), :] = value.astype(BF)

        each_tile(body)

    def turn(value, at, sign):
        head = value[:, :LANES]
        lane = lax.broadcasted_iota(jnp.int32, head.shape, 1)
        lower = -sign * pltpu.roll(head, LANES - ROT // 2, 1)
        upper = sign * pltpu.roll(head, ROT // 2, 1)
        head = head * tables[0, at, :] + jnp.where(lane < ROT // 2, lower, upper) * tables[1, at, :]
        if value.shape[1] == LANES:
            return head
        return jnp.concatenate([head, value[:, LANES:]], axis=1)

    def joint_stage():
        @pl.loop(0, n)
        def _(i):
            at = span(i, rows)
            joint = nn(normed[at, :], left[:, 0 : 3 * part]) + ref.joint_bias[...]
            for kind in range(3):
                for head in range(heads):
                    first = kind * part + head * head_size
                    value = joint[:, first : first + head_size]
                    if kind < 2:
                        value = turn(value, at, 1.0)
                    qkv[at, first : first + head_size] = value.astype(BF)

    gate_tall = min(part, size.high)

    def load_dense():
        return [
            local(
                ref.dense_all.at[span(s, part, gate_tall, first)],
                stage.at[k, pl.ds(0, gate_tall), pl.ds(0, width)],
                ref.load_sem.at[1 + k],
            )
            for k, first in enumerate(range(0, part, gate_tall))
        ]

    def gate_stage(copies):
        for copy in copies:
            copy.wait()

        @pl.loop(0, n)
        def _(i):
            for k in range(part // gate_tall):
                weight = stage[k, 0:gate_tall, 0:width]
                gate[span(i, rows), k * gate_tall : (k + 1) * gate_tall] = nt(upstream[span(i, rows), :], weight).astype(BF)

    queries = max(rows * min(1024, length) // length, 16)

    def attend_tile(head, i, sub):
        keys = (i + 1) * rows
        first = i * rows + sub * queries
        at = pl.ds(first, queries)
        seen = pl.ds(0, keys)
        q_at = pl.ds(head * head_size, head_size)
        k_at = pl.ds(part + head * head_size, head_size)
        v_at = pl.ds(2 * part + head * head_size, head_size)
        query, back = qkv[at, q_at], gate[at, q_at]
        scores = nt(query, qkv[seen, k_at]) * scale
        row = lax.broadcasted_iota(jnp.int32, (queries, keys), 0) + first
        column = lax.broadcasted_iota(jnp.int32, (queries, keys), 1)
        scores = jnp.where(column <= row, scores, -1e30)
        expo = jnp.exp(scores - jnp.max(scores, axis=-1, keepdims=True))
        probs = expo / jnp.sum(expo, axis=-1, keepdims=True)
        low_probs = probs.astype(BF)
        mixed[at, q_at] = nn(low_probs, qkv[seen, v_at]).astype(BF)
        grad_probs = nt(back, qkv[seen, v_at])
        inner = jnp.sum(probs * grad_probs, axis=-1, keepdims=True)
        grad_scores = (probs * (grad_probs - inner)).astype(BF)
        grad_query = nn(grad_scores, qkv[seen, k_at]) * scale
        grad_qkv[at, q_at] = turn(grad_query, at, -1.0).astype(BF)
        for total, extra in ((wide_one, tn(grad_scores, query)), (wide_two, tn(low_probs, back))):
            for b in range(i + 1):
                here = (slice(0, rows), slice(b * head_size, (b + 1) * head_size))
                block = extra[b * rows : (b + 1) * rows]
                total[here] = block if i == n - 1 and sub == 0 else total[here] + block

    def attend_stage(head):
        for i in range(n - 1, -1, -1):
            for sub in range(rows // queries):
                attend_tile(head, i, sub)
        for b in range(n):
            at = pl.ds(b * rows, rows)
            here = (slice(0, rows), slice(b * head_size, (b + 1) * head_size))
            k_at = pl.ds(part + head * head_size, head_size)
            v_at = pl.ds(2 * part + head * head_size, head_size)
            grad_qkv[at, k_at] = turn(wide_one[here] * scale, at, -1.0).astype(BF)
            grad_qkv[at, v_at] = wide_two[here].astype(BF)

    def weight_grad(left_of, right_of, tiles, tall, columns, places):
        def stored(b, slot):
            return [
                pltpu.make_async_copy(
                    stage.at[slot, pl.ds(first, count), pl.ds(0, columns)], target, ref.stage_sem.at[slot]
                )
                for first, count, target in places(b)
            ]

        def settled(slot):
            view = stage.at[slot, pl.ds(0, tall), pl.ds(0, columns)]
            pltpu.make_async_copy(view, view, ref.stage_sem.at[slot]).wait()

        @pl.loop(0, tiles)
        def _(b):
            slot = b % 2

            @pl.when(b >= 2)
            def _():
                settled(slot)

            stage[slot, 0:tall, 0:columns] = tn(left_of(b), right_of()).astype(BF)
            for copy in stored(b, slot):
                copy.start()

        for b in range(max(tiles - 2, 0), tiles):
            settled(b % 2)

    def columns_of(buffer, count):
        return lambda b: buffer[:, lanes(b, count)]

    def owner_places(out, tall, each):
        def places(b):
            found = []
            for q in range(tall // each):
                owner = b * (tall // each) + q
                found.append((q * each, each, out.at[owner // CORES, owner % CORES]))
            return found

        return places

    def piece_places(out, tall):
        def places(b):
            found = []
            for q in range(tall // piece):
                g = b * (tall // piece) + q
                owner = g % m
                found.append((q * piece, piece, out.at[owner // CORES, owner % CORES, span(g // m, piece)]))
            return found

        return places

    def group(u):
        return slice(u * units, (u + 1) * units)

    def expand_stage(u):
        @pl.loop(0, n)
        def _(i):
            wide_one[:, 0:units] = nn(normed[span(i, rows), :], left[:, group(u)]) + ref.expand_bias[:, group(u)]

            @pl.loop(0, rows // few)
            def _(j):
                value = wide_one[span(j, few), 0:units]
                area = 0.5 * (1.0 + lax.erf(value * 0.7071067811865476))
                density = jnp.exp(-0.5 * value * value) * 0.3989422804014327
                at = pl.ds(pl.multiple_of(i * rows + j * few, few), few)
                act[at, group(u)] = (value * area).astype(BF)
                slope[at, group(u)] = (area + value * density).astype(BF)

    def shrink_stage(u):
        @pl.loop(0, n)
        def _(i):
            wide_one[:, 0:units] = nt(upstream[span(i, rows), :], right[group(u), :])

            @pl.loop(0, rows // few)
            def _(j):
                at = pl.ds(pl.multiple_of(i * rows + j * few, few), few)
                grad = (wide_one[span(j, few), 0:units] * slope[at, group(u)].astype(F32)).astype(BF)
                slope[at, group(u)] = grad
                ref.expand_total[:, group(u)] += eights(grad.astype(F32))

    def eights(value):
        return jnp.sum(value.reshape(value.shape[0] // 8, 8, value.shape[1]), axis=0)

    outs, out_sem = ref.outs, ref.out_sem

    def tiles_to_owners(item, made, received):
        mine = received.at[span(s, rows)]

        def moved(i, slot):
            return pltpu.make_async_copy(outs.at[slot], made.at[span(i, rows)], out_sem.at[slot])

        def direct(i, k):
            return remote(
                made.at[span(i, rows)], mine, ref.seq_send.at[item, k], ref.seq_recv.at[item, k], {SEQ: i}
            )

        def give(i, slot):
            k = (i - s + n) % n

            @pl.when(k == 0)
            def _():
                local(outs.at[slot], mine, add_sem.at[0]).wait()

            @pl.when(k != 0)
            def _():
                direct(i, k).start()

        def ready(i, slot):
            @pl.when(i >= 2)
            def _():
                moved(i - 2, slot).wait()
                give(i - 2, slot)

        def filled(i, slot):
            moved(i, slot).start()

        def flush():
            for i in range(max(n - 2, 0), n):
                moved(i, i % 2).wait()
                give(i, i % 2)
            for k in range(1, n):
                drains.append(lambda k=k: direct((s + k) % n, k).wait_send())

        def wait():
            seq_wait(item, received.at[pl.ds(0, rows)])

        return types.SimpleNamespace(ready=ready, filled=filled, flush=flush, wait=wait)

    output_tiles = tiles_to_owners(4, ref.output_part, ref.output_all)
    input_tiles = tiles_to_owners(5, ref.input_part, ref.input_all)

    def kept(array):
        load = lambda i, slot: pltpu.make_async_copy(array.at[span(i, rows)], outs.at[slot], ref.keep_sem.at[slot])
        store = lambda i, slot: pltpu.make_async_copy(outs.at[slot], array.at[span(i, rows)], ref.keep_sem.at[slot])
        return load, store

    input_load, input_store = kept(ref.input_kept)

    def output_stage():
        @pl.loop(0, n)
        def _(i):
            slot = i % 2
            output_tiles.ready(i, slot)
            outs[slot] = nn(act[span(i, rows), :], right[0:hidden, :]).astype(BF)
            output_tiles.filled(i, slot)

        output_tiles.flush()

    def gain_sums(which, grad, normal):
        ref.gain_total[2 * which] += eights(grad * normal)
        ref.gain_total[2 * which + 1] += eights(grad)

    def input_feed_stage(i, slot):
        wide_two[...] = nt(slope[span(i, rows), :], left[:, 0:hidden])
        pl.when(i >= 2)(lambda: input_store(i - 2, slot).wait())

        @pl.loop(0, rows // few)
        def _(j):
            at = span(j, few)
            normal, _ = normal_of(slot, at)
            grad = wide_two[at, :]
            outs[slot, at, :] = (grad * gains[2:3, :]).astype(BF)
            gain_sums(1, grad, normal)

        input_store(i, slot).start()

    def input_feed_flush():
        for i in range(max(n - 2, 0), n):
            input_store(i, i % 2).wait()

    def input_stage(i, slot):
        input_tiles.ready(i, slot)
        input_load(i, slot).start()
        wide_one[:, 0:width] = nt(grad_qkv[span(i, rows), :], left[:, 0 : 3 * part])
        input_load(i, slot).wait()

        @pl.loop(0, rows // few)
        def _(j):
            at = span(j, few)
            normal, _ = normal_of(slot, at)
            grad = wide_one[at, 0:width]
            outs[slot, at, :] = (outs[slot, at, :].astype(F32) + grad * gains[0:1, :]).astype(BF)
            gain_sums(0, grad, normal)

        input_tiles.filled(i, slot)

    def joint_total_stage():
        ref.joint_total[...] = jnp.zeros_like(ref.joint_total)

        @pl.loop(0, length // few)
        def _(j):
            ref.joint_total[...] += eights(grad_qkv[span(j, few), :].astype(F32))

    small = ref.small
    wide_rows = size.gain_rows

    def small_pack():
        ref.own_total[...] = jnp.zeros_like(ref.own_total)

        @pl.loop(0, rows // few)
        def _(j):
            at = pl.ds(pl.multiple_of(s * rows + j * few, few), few)
            ref.own_total[...] += eights(upstream[at, :].astype(F32))

        small[0] = jnp.zeros_like(small[0])
        for first, source, count in (
            (0, ref.gain_total.at[0], wide_rows),
            (wide_rows, ref.gain_total.at[1], wide_rows),
            (2 * wide_rows, ref.gain_total.at[2], wide_rows),
            (3 * wide_rows, ref.gain_total.at[3], wide_rows),
            (4 * wide_rows, ref.own_total, wide_rows),
            (size.joint_small, ref.joint_total, 3 * part // LANES),
            (size.expand_small, ref.expand_total, hidden // LANES),
        ):
            for j in range(count):
                value = source[:, j * LANES : (j + 1) * LANES]
                small[0, first + j : first + j + 1, :] = jnp.sum(value, axis=0, keepdims=True)

    def small_core():
        push_all(
            lambda: (
                [(small.at[0], ref.small_in.at[0])], small.at[0], ref.small_send.at[0], ref.small_recv.at[0], twin
            )
        )

    def small_line():
        arrived(small.at[0], ref.small_recv.at[0])
        small[1] = small[0] + ref.small_in[0]
        for k in range(1, line):
            push_all(
                lambda k=k: (
                    [(small.at[1], ref.small_in.at[k])],
                    small.at[1],
                    ref.small_send.at[k],
                    ref.small_recv.at[k],
                    {DP: (z + k) % line * CORES + c},
                )
            )

    def small_seq():
        total = small[1]
        for k in range(1, line):
            arrived(small.at[0], ref.small_recv.at[k])
            total = total + ref.small_in[k]
        ref.small_all[s] = total
        mine = ref.small_all.at[s]
        seq_push(9, lambda j: [(mine, mine)], mine)

    def small_last():
        seq_wait(9, small.at[0])
        total = ref.small_all[0, 0 : 5 * wide_rows, :]
        for j in range(1, n):
            total = total + ref.small_all[j, 0 : 5 * wide_rows, :]
        ref.gain_grads[...] = total
        for j in range(n):
            ref.joint_grads[j] = ref.small_all[j, size.joint_small : size.expand_small, :]
            ref.expand_grads[j] = ref.small_all[j, size.expand_small : size.expand_small + hidden // LANES, :]

    def owner_sum(buffer):
        chunk = min(size.chunk, rows)
        for q in range(rows // chunk):
            for first in range(0, n, 4):
                sources = [buffer.at[pl.ds(j * rows + q * chunk, chunk)] for j in range(first, min(first + 4, n))]

                def into(where, total):
                    at = pl.ds(pl.multiple_of(where.start + q * chunk, 16), where.size)
                    wide_one[at, 0:width] = total if first == 0 else wide_one[at, 0:width] + total

                added(sources, chunk, width, into)

    def own_tokens():
        return local(
            ref.tokens_all.at[span(s, rows)], stage.at[0, pl.ds(0, rows), pl.ds(0, width)], ref.x_sem.at[0]
        )

    def mixed_pairs(j):
        return [(mixed.at[span(j, rows)], ref.mixed_own.at[:, lanes(s, part)])]

    def finish_output():
        copy = own_tokens()
        output_tiles.wait()
        owner_sum(ref.output_all)
        copy.wait()
        seq_wait(12, mixed.at[pl.ds(0, rows)])
        wide_two[...] = nn(ref.mixed_own[...], right[0:width, :])

        @pl.loop(0, rows // few)
        def _(j):
            at = span(j, few)
            total = stage[0, at, 0:width].astype(F32) + (wide_one[at, 0:width] + wide_two[at, :] + ref.offsets[...])
            stage[1, at, 0:width] = total.astype(BF)

        local(stage.at[1, pl.ds(0, rows), pl.ds(0, width)], ref.output, ref.stage_sem.at[0]).wait()

    def finish_input():
        copy = own_tokens()
        input_tiles.wait()
        owner_sum(ref.input_all)
        copy.wait()

        @pl.loop(0, rows // few)
        def _(j):
            at = span(j, few)
            normal, spread = normal_of(0, at)
            grad = wide_one[at, 0:width]
            through = grad - jnp.mean(grad, axis=-1, keepdims=True)
            through = through - normal * jnp.mean(grad * normal, axis=-1, keepdims=True)
            own = upstream[pl.ds(pl.multiple_of(s * rows + j * few, few), few), :].astype(F32)
            wide_two[at, :] = own + spread * through

        local(wide_two, ref.grad_tokens, ref.stage_sem.at[0]).wait()

    def load_joint():
        return local(ref.joint_all, left.at[:, pl.ds(0, 3 * part)], ref.load_sem.at[0])

    def joint_pairs(j):
        return [
            (
                ref.joint_own.at[:, lanes(j, part, kind * width)],
                ref.joint_all.at[span(s * m + d, piece), pl.ds(kind * part, part)],
            )
            for kind in range(3)
        ]

    def expand_columns(j, u):
        if split == 1:
            return [(pl.multiple_of(j * hidden, LANES), 0, hidden)]
        return [
            (pl.multiple_of(j * hidden + owner * shrink_rows + u * share, LANES), owner * share, share)
            for owner in range(m)
        ]

    def expand_pairs(u):
        return lambda j: [
            (
                ref.expand_own.at[:, pl.ds(first, count)],
                ref.expand_all.at[u, span(s * m + d, piece), pl.ds(to, count)],
            )
            for first, to, count in expand_columns(j, u)
        ]

    def vector_pairs(j):
        return [(ref.vector_own, ref.vectors.at[span(d * n + s, VECTOR_ROWS)])]

    expand_whole = ref.expand_all.at[0, pl.ds(0, piece)]
    joint_whole = ref.joint_all.at[pl.ds(0, piece)]
    expand_items = (1, 7)
    seq_push(expand_items[0], expand_pairs(0), expand_whole)
    seq_push(8, vector_pairs, ref.vector_own)

    def room(buffer, slot, source):
        return buffer.at[slot, pl.ds(0, source.shape[0]), pl.ds(0, source.shape[1])]

    moves = [
        ([(ref.shrink_own.at[pl.ds(u * share, share)], stage.at[1, pl.ds(u * share, share), pl.ds(0, width)])],
         ref.shrink_all.at[u, span(d, share)])
        for u in range(split)
    ]
    moves += [([(ref.tokens, room(stage, 0, ref.tokens))], ref.tokens_all.at[span(s, rows)])]
    moves += [
        (
            [
                (src, adds.at[u, pl.ds(0, piece), pl.ds(to, count)])
                for (src, _), (_, to, count) in zip(expand_pairs(u)(s), expand_columns(s, u))
            ],
            ref.expand_all.at[u, span(s * m + d, piece)],
        )
        for u in range(split)
    ]
    moves += [
        ([(ref.dense_own, room(sent, 0, ref.dense_own))], ref.dense_all.at[span(s * m + d, dense_rows)]),
        (
            [
                (src, adds.at[2, pl.ds(0, piece), pl.ds(kind * part, part)])
                for kind, (src, _) in enumerate(joint_pairs(s))
            ],
            ref.joint_all.at[span(s * m + d, piece)],
        ),
    ]
    held = [pairs[0][1] for pairs, _ in moves[: split + 1]]
    held += [adds.at[u, pl.ds(0, piece), pl.ds(0, units)] for u in range(split)]
    held += [room(sent, 0, ref.dense_own), adds.at[2, pl.ds(0, piece), pl.ds(0, 3 * part)]]
    for k, (pairs, _) in enumerate(moves):
        for src, dst in pairs:
            local(src, dst, ref.own_sem.at[k])
    own_vectors = [local(src, dst, ref.vector_sem.at[0]) for src, dst in vector_pairs(s)]
    own_upstream = local(ref.cotangent, upstream.at[span(s, rows)], ref.vector_sem.at[1])
    stored = []
    for k, (_, target) in enumerate(moves):
        pltpu.make_async_copy(held[k], held[k], ref.own_sem.at[k]).wait()
        stored.append(local(held[k], target, ref.own_sem.at[k]))
    own_tokens_at, own_expand_at, own_dense_at = split, split + 1, 2 * split + 1
    stored[0].wait()
    gather_step(shrink_in[0], 0)
    stored[own_tokens_at].wait()
    spread_first(2, ref.tokens_all)
    own_vectors[0].wait()
    seq_wait(8, ref.vector_own)
    vector_send()
    stored[own_expand_at].wait()
    seq_wait(expand_items[0], expand_whole)
    gather_step(expand_in[0], 0)
    for k, copy in enumerate(stored):
        if k not in (0, own_tokens_at, own_expand_at):
            copy.wait()
    own_upstream.wait()
    ref.gain_total[...] = jnp.zeros_like(ref.gain_total)
    ref.expand_total[...] = jnp.zeros_like(ref.expand_total)
    for u in range(1, split):
        seq_push(expand_items[u], expand_pairs(u), expand_whole)
    gather_step(shrink_in[0], 1)
    gather_step(expand_in[0], 1)
    spread_second(2, ref.tokens_all)
    spread_first(3, upstream)
    gather_step(shrink_in[0], 2)
    vector_swap()
    gather_step(dense_in, 0)
    spread_wait(2, ref.tokens_all)
    gather_step(expand_in[0], 2)
    for u in range(1, split):
        gather_step(shrink_in[u], 0)
    gather_wait(vector_in)
    unpack_vectors()
    norm_stage(1)
    gather_step(shrink_in[0], 3)
    for u in range(1, split):
        seq_wait(expand_items[u], expand_whole)
        gather_step(expand_in[u], 0)
    spread_second(3, upstream)
    seq_push(0, joint_pairs, joint_whole)
    gather_step(expand_in[0], 3)
    gather_rest(shrink_in[0], expand_in[0])

    def load_expand(u):
        return local(ref.expand_all.at[u], left.at[:, pl.ds(u * units, units)], ref.load_sem.at[0])

    def load_shrink(u):
        return local(ref.shrink_all.at[u], right.at[pl.ds(u * units, units)], ref.load_sem.at[1])

    def shrink_grad_stage(u):
        weight_grad(
            lambda b: act[:, lanes(b, size.units_tall, u * units)],
            lambda: upstream[...],
            units // size.units_tall,
            size.units_tall,
            width,
            owner_places(ref.shrink_sum.at[u], size.units_tall, share),
        )
        reduce_start(shrink_kind[u])

    def expand_grad_stage(u):
        weight_grad(
            columns_of(normed, mid_rows),
            lambda: slope[:, group(u)],
            m,
            mid_rows,
            units,
            piece_places(ref.expand_sum.at[u], mid_rows),
        )
        reduce_start(expand_kind[u])

    def finish_expand(u):
        columns = [(to, s * hidden + first, count) for first, to, count in expand_columns(0, u)]
        finish_columns(expand_kind[u], 10 + u, ref.expand_done.at[u], ref.expand_grad, columns)

    gather_wait(shrink_in[0], expand_in[0])
    copy_one, copy_two = load_expand(0), load_shrink(0)
    copy_one.wait()
    expand_stage(0)
    gather_step(dense_in, 1)
    if split > 1:
        gather_step(shrink_in[1], 1)
    spread_wait(3, upstream)
    shrink_grad_stage(0)
    copy_two.wait()
    shrink_stage(0)
    if split > 1:
        gather_step(expand_in[1], 1)
    expand_grad_stage(0)
    reduce_hop(1, shrink_kind[0])
    gather_step(dense_in, 2)
    if split > 1:
        gather_step(shrink_in[1], 2)
    reduce_hop(1, expand_kind[0])
    if split > 1:
        gather_step(expand_in[1], 2)
    gather_step(dense_in, 3)
    gather_rest(dense_in)
    gather_wait(dense_in)
    spread_first(13, ref.dense_all, part)
    gate_stage(load_dense())
    seq_wait(0, joint_whole)
    if split > 1:
        gather_step(shrink_in[1], 3)
    gather_step(joint_a, 0)
    reduce_hop(2, shrink_kind[0])
    if split > 1:
        gather_step(expand_in[1], 3)
        gather_rest(shrink_in[1], expand_in[1])
    gather_step(joint_b, 0)
    last = split - 1
    if split > 1:
        gather_wait(shrink_in[1], expand_in[1])
        copy_one, copy_two = load_expand(1), load_shrink(1)
        copy_one.wait()
        expand_stage(1)
    reduce_hop(2, expand_kind[0])
    gather_step(joint_a, 1)
    if split > 1:
        shrink_grad_stage(1)
    reduce_hop(3, shrink_kind[0])
    gather_step(joint_b, 1)
    if split > 1:
        copy_two.wait()
        shrink_stage(1)
    spread_second(13, ref.dense_all, part)
    if split > 1:
        expand_grad_stage(1)
    gather_step(joint_a, 2)
    reduce_hop(3, expand_kind[0])
    for hop in range(4, hops + 1):
        reduce_hop(hop, shrink_kind[0], expand_kind[0])
    if split > 1:
        reduce_hop(1, shrink_kind[1])
    gather_step(joint_b, 2)
    if split > 1:
        reduce_hop(1, expand_kind[1])
    output_stage()
    gather_step(joint_a, 3)
    if split > 1:
        finish_rows(shrink_kind[0], ref.shrink_grad, 0)
        reduce_hop(2, shrink_kind[1])
    gather_step(joint_b, 3)
    gather_rest(joint_a, joint_b)
    if split > 1:
        finish_expand(0)
        reduce_hop(2, expand_kind[1])
    each_tile(input_feed_stage)
    input_feed_flush()
    if split > 1:
        reduce_hop(3, shrink_kind[1])
    gather_wait(joint_a, joint_b)
    copy_one = load_joint()
    norm_stage(0)
    if split > 1:
        reduce_hop(3, expand_kind[1])
        for hop in range(4, hops + 1):
            reduce_hop(hop, shrink_kind[1], expand_kind[1])
    copy_one.wait()
    joint_stage()
    for head in range(heads):
        attend_stage(head)
    seq_push(12, mixed_pairs, mixed.at[pl.ds(0, rows)])
    tall = min(part, size.high)
    weight_grad(
        columns_of(mixed, tall),
        lambda: upstream[...],
        part // tall,
        tall,
        width,
        owner_places(ref.dense_sum, tall, dense_rows),
    )
    reduce_start(dense_kind)
    weight_grad(
        columns_of(normed, mid_rows),
        lambda: grad_qkv[...],
        m,
        mid_rows,
        3 * part,
        piece_places(ref.joint_sum, mid_rows),
    )
    reduce_start(joint_kind)
    spread_wait(13, ref.dense_all, part)
    load_wide = local(ref.dense_all, right.at[pl.ds(0, width)], ref.load_sem.at[1])
    ref.mixed_own[:, lanes(s, part)] = mixed[span(s, rows), :]
    reduce_hop(1, dense_kind, joint_kind)
    each_tile(input_stage)
    input_tiles.flush()
    reduce_hop(2, dense_kind, joint_kind)
    joint_total_stage()
    small_pack()
    small_core()
    finish_rows(shrink_kind[last], ref.shrink_grad, last * share)
    small_line()
    reduce_hop(3, dense_kind, joint_kind)
    small_seq()
    finish_expand(last)
    load_wide.wait()
    finish_output()
    for hop in range(4, hops + 1):
        reduce_hop(hop, dense_kind, joint_kind)
    finish_rows(dense_kind, ref.dense_grad)
    finish_columns(
        joint_kind,
        6,
        ref.joint_done,
        ref.joint_grad,
        [(kind * part, kind * width + s * part, part) for kind in range(3)],
    )
    small_last()
    finish_input()
    seq_wait(6, ref.joint_done.at[pl.ds(0, piece)])
    for u in range(split):
        seq_wait(10 + u, ref.expand_done.at[u, pl.ds(0, piece)])
    for pending in rounds.pending:
        if pending is not None:
            pending()
    for drain in drains:
        drain()


def run_kernel(size, inputs):
    n, m, line, hops = size.n, size.m, size.line, size.hops
    rows, width, piece, part, hidden = size.rows, size.width, size.piece, size.part, size.hidden
    dense_rows, mid_rows, shrink_rows, length = size.dense_rows, size.mid_rows, size.shrink_rows, size.length
    anywhere, vmem = pl.BlockSpec(memory_space=pl.ANY), pl.BlockSpec(memory_space=pltpu.VMEM)

    def reduced(count, columns):
        shape = (count, columns)
        return ((line, CORES) + shape, BF), ((line,) + shape, BF), ((2, line) + shape, BF)

    dense, joint = reduced(dense_rows, width), reduced(mid_rows, 3 * part)
    expand, shrink = reduced(mid_rows, size.units), reduced(size.share, width)
    expand, shrink = [[((size.split,) + shape, kind) for shape, kind in arrays] for arrays in (expand, shrink)]
    small_outputs = dict(
        gain_grads=((5 * size.gain_rows, LANES), F32),
        joint_grads=((n, 3 * part // LANES, LANES), F32),
        expand_grads=((n, hidden // LANES, LANES), F32),
    )
    outputs = dict(
        output=((rows, width), BF),
        grad_tokens=((rows, width), F32),
        dense_grad=((dense_rows, width), F32),
        shrink_grad=((shrink_rows, width), F32),
        joint_grad=((piece, 3 * width), F32),
        expand_grad=((piece, n * hidden), F32),
        dense_all=((width, width), BF),
        joint_all=((width, 3 * part), BF),
        expand_all=((size.split, width, size.units), BF),
        shrink_all=((size.split, size.units, width), BF),
        tokens_all=((length, width), BF),
        output_all=((length, width), BF),
        input_all=((length, width), BF),
        output_part=((length, width), BF),
        input_part=((length, width), BF),
        input_kept=((length, width), BF),
        joint_done=((mid_rows, 3 * part), F32),
        expand_done=((size.split, mid_rows, size.units), F32),
        dense_sum=dense[0],
        dense_core=dense[1],
        dense_chain=dense[2],
        joint_sum=joint[0],
        joint_core=joint[1],
        joint_chain=joint[2],
        expand_sum=expand[0],
        expand_core=expand[1],
        expand_chain=expand[2],
        shrink_sum=shrink[0],
        shrink_core=shrink[1],
        shrink_chain=shrink[2],
    )
    dma = pltpu.SemaphoreType.DMA
    small = (size.small, LANES)
    scratch = dict(
        upstream=pltpu.VMEM((length, width), BF),
        normed=pltpu.VMEM((length, width), BF),
        qkv=pltpu.VMEM((length, 3 * part), BF),
        gate=pltpu.VMEM((length, part), BF),
        act=pltpu.VMEM((length, hidden), BF),
        slope=pltpu.VMEM((length, hidden), BF),
        left=pltpu.VMEM((width, max(hidden, 3 * part)), BF),
        right=pltpu.VMEM((max(hidden, width), width), BF),
        mixed_own=pltpu.VMEM((rows, width), BF),
        outs=pltpu.VMEM((2, rows, width), BF),
        wide_one=pltpu.VMEM((max(rows, size.chunk), max(width, hidden)), F32),
        wide_two=pltpu.VMEM((rows, width), F32),
        stage=pltpu.VMEM((2, size.high, size.broad), BF),
        adds=pltpu.VMEM((8, size.chunk, size.broad), BF),
        sent=pltpu.VMEM((4, size.chunk, size.broad), BF),
        vectors=pltpu.VMEM((n * m * VECTOR_ROWS, LANES), F32),
        gains=pltpu.VMEM((4, width), F32),
        offsets=pltpu.VMEM((1, width), F32),
        joint_bias=pltpu.VMEM((1, 3 * part), F32),
        expand_bias=pltpu.VMEM((1, hidden), F32),
        gain_total=pltpu.VMEM((4, 8, width), F32),
        own_total=pltpu.VMEM((8, width), F32),
        joint_total=pltpu.VMEM((8, 3 * part), F32),
        expand_total=pltpu.VMEM((8, hidden), F32),
        small=pltpu.VMEM((2,) + small, F32),
        small_in=pltpu.VMEM((line,) + small, F32),
        small_all=pltpu.VMEM((n,) + small, F32),
        seq_send=dma((14, max(n, 4))),
        seq_recv=dma((14, max(n, 4))),

        ag_send=dma((8, 2, hops)),
        ag_recv=dma((8, 2, hops)),
        swap_send=dma((8, line)),
        swap_recv=dma((8, line)),
        core_send=dma((11,)),
        core_recv=dma((11,)),
        rs_send=dma((11, 2, hops)),
        rs_recv=dma((11, 2, hops)),
        small_send=dma((line,)),
        small_recv=dma((line,)),
        add_sem=dma((8,)),
        stage_sem=dma((2,)),
        load_sem=dma((3,)),
        own_sem=dma((7,)),
        vector_sem=dma((2,)),
        vector_out=dma((line,)),
        vector_back=dma((line,)),
        out_sem=dma((2,)),
        keep_sem=dma((2,)),
        x_sem=dma((2,)),
    )
    names = list(inputs) + list(outputs) + list(small_outputs) + list(scratch)
    results = pl.pallas_call(
        functools.partial(kernel, size, names),
        out_shape=[
            jax.ShapeDtypeStruct(shape, kind)
            for shape, kind in list(outputs.values()) + list(small_outputs.values())
        ],
        in_specs=[vmem if name == next(reversed(inputs)) else anywhere for name in inputs],
        out_specs=[anywhere] * len(outputs) + [vmem] * len(small_outputs),
        scratch_shapes=list(scratch.values()),
        compiler_params=pltpu.CompilerParams(
            collective_id=0, has_side_effects=True, vmem_limit_bytes=64 * 2**20 - 2**17
        ),
        name="block",
    )(*inputs.values())
    return types.SimpleNamespace(**dict(zip(list(outputs) + list(small_outputs), results)))


def block_plan(n, m, tokens, cotangent, shards):
    (
        first_gain,
        first_shift,
        second_gain,
        second_shift,
        joint_weight,
        joint_bias,
        dense_weight,
        dense_bias,
        expand_weight,
        expand_bias,
        shrink_weight,
        shrink_bias,
    ) = shards
    rows, width = tokens.shape[1:]
    size = sizes_of(n, m, rows, width, expand_weight.shape[1])
    piece, devices = size.piece, n * m
    vectors = jnp.concatenate(
        [
            vector.astype(F32).reshape(-1, piece)
            for vector in (
                first_gain,
                first_shift,
                second_gain,
                second_shift,
                joint_bias,
                dense_bias,
                expand_bias,
                shrink_bias,
            )
        ]
    )
    vectors = jnp.pad(vectors, ((0, VECTOR_ROWS - vectors.shape[0]), (0, 0)))
    vectors = jnp.concatenate([vectors] * (LANES // piece), axis=1)
    got = run_kernel(
        size,
        dict(
            tokens=tokens[0],
            cotangent=cotangent[0],
            joint_own=joint_weight,
            expand_own=expand_weight,
            dense_own=dense_weight,
            shrink_own=shrink_weight,
            vector_own=vectors,
            tables=turn_tables(size.length),
        ),
    )
    index = lax.axis_index(SEQ) * m + lax.axis_index(DP)

    def own(values):
        return lax.dynamic_index_in_dim(values.reshape(devices, -1), index, 0, keepdims=False)

    gains = lax.dynamic_slice_in_dim(got.gain_grads.reshape(5, width), index * piece, piece, 1)
    joint_grads = jnp.swapaxes(got.joint_grads.reshape(n, 3, size.part), 0, 1)
    expand_grads = jnp.swapaxes(got.expand_grads.reshape(n, size.split, m, size.share), 1, 2)
    return (
        got.output[None],
        got.grad_tokens[None],
        gains[0],
        gains[1],
        gains[2],
        gains[3],
        got.joint_grad,
        own(joint_grads),
        got.dense_grad,
        gains[4],
        got.expand_grad,
        own(expand_grads),
        got.shrink_grad,
        gains[4],
    )


def solution(mesh):
    n, m = mesh.shape[SEQ], mesh.shape[DP]

    def body(tokens, cotangent, *shards):
        return block_plan(n, m, tokens, cotangent, shards)

    both = (SEQ, DP)
    tokens = P(DP, SEQ, None)
    vector, matrix = P(both), P(both, None)
    return jax.shard_map(
        body,
        mesh=mesh,
        in_specs=(tokens, tokens) + (vector,) * 4 + (matrix, vector) * 4,
        out_specs=(tokens, tokens) + (vector,) * 4 + (matrix, vector) * 4,
        check_vma=False,
    )
```
